128 devices in a mesh: dp: 4 (over y_lo, core), ctx: 32 (over y_hi, x, z).
Axes of the slice: x: 4, y: 4 (y_hi: 2, y_lo: 2; y = y_hi * 2 + y_lo), z: 4, core: 2. Of those that a mesh axis runs over, the one named last changes fastest.
Arguments:
- tokens: bfloat16 [4, 4096, 1152], P('dp', 'ctx'), may hold values from -6 to 6
- grad_out: bfloat16 [4, 4096, 1152], P('dp', 'ctx'), may hold values from -6 to 6
- pair_order: int32 [32], replicated, may hold values from 0 to 31, each once
- attn_gain: bfloat16 [1152], P(('dp', 'ctx')), may hold values from 0.5 to 1.5
- query_weight: bfloat16 [1152, 1152], P(('dp', 'ctx')), may hold values from -0.1875 to 0.1875
- key_weight: bfloat16 [1152, 384], P(('dp', 'ctx')), may hold values from -0.1875 to 0.1875
- value_weight: bfloat16 [1152, 384], P(('dp', 'ctx')), may hold values from -0.1875 to 0.1875
- output_weight: bfloat16 [1152, 1152], P(('dp', 'ctx')), may hold values from -4 to 4
- ffn_gain: bfloat16 [1152], P(('dp', 'ctx')), may hold values from 0.5 to 1.5
- gate_weight: bfloat16 [1152, 3072], P(('dp', 'ctx')), may hold values from -0.1875 to 0.1875
- up_weight: bfloat16 [1152, 3072], P(('dp', 'ctx')), may hold values from -0.1875 to 0.1875
- down_weight: bfloat16 [1152, 3072], P(('dp', 'ctx')), may hold values from -0.109375 to 0.109375
Outputs:
- block_out: bfloat16 [4, 4096, 1152], P('dp', 'ctx')
- grad_tokens: bfloat16 [4, 4096, 1152], P('dp', 'ctx')
- grad_attn_gain: float32 [1152], P(('dp', 'ctx'))
- grad_query_weight: float32 [1152, 1152], P(('dp', 'ctx'))
- grad_key_weight: float32 [1152, 384], P(('dp', 'ctx'))
- grad_value_weight: float32 [1152, 384], P(('dp', 'ctx'))
- grad_output_weight: float32 [1152, 1152], P(('dp', 'ctx'))
- grad_ffn_gain: float32 [1152], P(('dp', 'ctx'))
- grad_gate_weight: float32 [1152, 3072], P(('dp', 'ctx'))
- grad_up_weight: float32 [1152, 3072], P(('dp', 'ctx'))
- grad_down_weight: float32 [1152, 3072], P(('dp', 'ctx'))
The draws below stay inside these ranges and needn't reach their ends.
Inputs may be any that keep to these rules, and one draw needn't show every extreme that they name: A permutation of 0 to 31; index i of ctx holds the position blocks pair_order[i] and 63 - pair_order[i] of 64 positions each, in this order.
All inputs are finite; a program needn't handle non-finite values.
Results may differ from the reference program's by a relative error of at most 0.02.
Values may be sent and summed in bfloat16 or wider, within the bound.
No kernel may reach another device: no remote copies, remote signals or barrier semaphores. Data moves between devices by JAX's collectives and lax.ppermute only.
A program may use at most 256 MiB of HBM per device.

```python
import math
import jax
import jax.numpy as jnp
from jax import lax

D = 1152
HEADS = 18
KV_HEADS = 6
HEAD = 64
FF = 3072
TOK_DEV = 128
KVW = 384
PAIRS = 32
SEQ_LEN = 4096
SEQS = 4


def block_levels(stream_key, shape, split, least, high):
    def one(dim, parts):
        draws = jax.random.uniform(jax.random.fold_in(jax.random.fold_in(stream_key, 6), dim), (parts,), jnp.float32, least / len(split), high / len(split))
        return jnp.repeat(jnp.exp(draws), shape[dim] // parts).reshape((-1,) + (1,) * (len(shape) - dim - 1))

    factor_of = one(*split[0])
    for cut in split[1:]:
        factor_of = factor_of * one(*cut)
    return factor_of


def noise(key, dims, scale, bound, pieces=(), kind=jnp.bfloat16):
    values = scale * jax.random.normal(key, dims, jnp.float32)
    if pieces:
        values = values * block_levels(key, dims, pieces, -0.22, 0.18)
    return jnp.clip(values, -bound, bound).astype(kind)


def setup_inputs(seed: int = 0) -> dict:
    keys = jax.random.split(jax.random.key(seed), 13)
    tokens = noise(keys[0], (SEQS, SEQ_LEN, D), 1.0, 6.0, ((0, 4), (1, 32)))
    grad_out = noise(keys[1], (SEQS, SEQ_LEN, D), 1.0, 6.0, ((0, 4), (1, 32)))
    pair_order = jax.random.permutation(keys[2], PAIRS).astype(jnp.int32)
    attn_gain = jnp.clip(1.0 + 0.1 * jax.random.normal(keys[3], (D,), jnp.float32), 0.5, 1.5).astype(jnp.bfloat16)
    query_weight = noise(keys[4], (D, D), D ** -0.5, 0.1875, ((0, 128),))
    key_weight = noise(keys[5], (D, KVW), D ** -0.5, 0.1875, ((0, 128),))
    value_weight = noise(keys[6], (D, KVW), D ** -0.5, 0.1875, ((0, 128),))
    output_weight = noise(keys[7], (D, D), (max(D // 512, 1)) ** -0.5, 4.0, ((0, 128),))
    ffn_gain = jnp.clip(1.0 + 0.1 * jax.random.normal(keys[8], (D,), jnp.float32), 0.5, 1.5).astype(jnp.bfloat16)
    gate_weight = noise(keys[9], (D, FF), D ** -0.5, 0.1875, ((0, 128),))
    up_weight = noise(keys[10], (D, FF), D ** -0.5, 0.1875, ((0, 128),))
    down_weight = noise(keys[11], (D, FF), FF ** -0.5, 0.109375, ((0, 128),))
    return dict(tokens=tokens, grad_out=grad_out, pair_order=pair_order, attn_gain=attn_gain, query_weight=query_weight, key_weight=key_weight, value_weight=value_weight, output_weight=output_weight, ffn_gain=ffn_gain, gate_weight=gate_weight, up_weight=up_weight, down_weight=down_weight)


@jax.custom_vjp
def low(v):
    return lax.optimization_barrier(v.astype(jnp.bfloat16)).astype(jnp.float32)

@jax.custom_vjp
def low_back(v):
    return v

def low_keep(v):
    return (low(v), None)

def low_pass(kept, grad):
    return (grad,)

def back_keep(v):
    return (v, None)

def back_low(kept, grad):
    return (low(grad),)
low.defvjp(low_keep, low_pass)
low_back.defvjp(back_keep, back_low)

def product(left, right):
    return jnp.dot(left, right, precision=lax.Precision.HIGHEST, preferred_element_type=jnp.float32)

def rms_scaled(inputs, gain):
    inverse = lax.rsqrt(lax.optimization_barrier(jnp.mean(inputs * inputs, axis=-1, keepdims=True)) + 1e-05)
    return inputs * inverse * gain

def rope_tables(positions, width):
    half_width = width // 2
    inverse = 1.0 / 10000.0 ** (jnp.arange(half_width, dtype=jnp.float32) * (2.0 / width))
    angles = positions.astype(jnp.float32)[:, None] * inverse[None, :]
    return (jnp.cos(angles)[:, None, :], jnp.sin(angles)[:, None, :])

def rotate(vectors, cos_table, sin_table):
    half_width = vectors.shape[-1] // 2
    front_half = vectors[..., :half_width]
    back_half = vectors[..., half_width:]
    return jnp.concatenate([front_half * cos_table - back_half * sin_table, back_half * cos_table + front_half * sin_table], axis=-1)

def attend_block(query_block, pos_block, key_rot, value_rows, positions):
    count = query_block.shape[0]
    grouped = query_block.reshape(count, KV_HEADS, -1, HEAD)
    raw_scores = jnp.einsum('qkgd,tkd->kgqt', grouped, key_rot, precision=lax.Precision.HIGHEST) * HEAD ** (-0.5)
    raw_scores = low_back(raw_scores)
    allowed = positions[None, :] <= pos_block[:, None]
    masked = jnp.where(allowed, raw_scores, -1e+30)
    shifted = masked - lax.optimization_barrier(jnp.max(masked, axis=-1, keepdims=True))
    exponent = jnp.exp(shifted)
    attn_prob = exponent / lax.optimization_barrier(jnp.sum(exponent, axis=-1, keepdims=True))
    attended = jnp.einsum('kgqt,tkd->qkgd', low(attn_prob), value_rows, precision=lax.Precision.HIGHEST)
    return attended.reshape(count, -1)

def layer(inputs, weights_all, positions):
    attn_gain, query_weight, key_weight, value_weight, output_weight, ffn_gain, gate_weight, up_weight, down_weight = weights_all
    seq_rows = inputs.shape[0]
    normed_a = low(rms_scaled(inputs, attn_gain))
    queries = low_back(product(normed_a, query_weight))
    key_proj = low_back(product(normed_a, key_weight))
    value_proj = low(low_back(product(normed_a, value_weight)))
    cos_table, sin_table = rope_tables(positions, HEAD)
    query_rot = low(rotate(queries.reshape(seq_rows, -1, HEAD), cos_table, sin_table))
    key_rot = low(rotate(key_proj.reshape(seq_rows, -1, HEAD), cos_table, sin_table))
    value_rows = value_proj.reshape(seq_rows, -1, HEAD)
    block = math.gcd(512, seq_rows)
    checked = jax.checkpoint(attend_block)

    def per_block(block_data):
        return checked(block_data[0], block_data[1], key_rot, value_rows, positions)
    attended = lax.map(per_block, (query_rot.reshape(seq_rows // block, block, HEADS, HEAD), positions.reshape(seq_rows // block, block)))
    attended = low(low_back(attended.reshape(seq_rows, -1)))
    hidden_one = inputs + low_back(product(attended, output_weight.T))
    normed_f = low(rms_scaled(hidden_one, ffn_gain))
    gate = low_back(product(normed_f, gate_weight))
    up_proj = low_back(product(normed_f, up_weight))
    hidden = low(jax.nn.silu(gate) * up_proj)
    return hidden_one + product(hidden, down_weight.T)

def reference(tokens, grad_out, pair_order, attn_gain, query_weight, key_weight, value_weight, output_weight, ffn_gain, gate_weight, up_weight, down_weight):
    half_rows = TOK_DEV // 2
    offsets = jnp.arange(half_rows, dtype=jnp.int32)
    early_pos = pair_order[:, None] * half_rows + offsets[None, :]
    late_pos = (2 * PAIRS - 1 - pair_order)[:, None] * half_rows + offsets[None, :]
    positions = jnp.concatenate([early_pos, late_pos], axis=1).reshape(SEQ_LEN).astype(jnp.int32)
    params = tuple((weight.astype(jnp.float32) for weight in (attn_gain, query_weight, key_weight, value_weight, output_weight, ffn_gain, gate_weight, up_weight, down_weight)))

    def run_layer(inputs, *weights_all):
        return layer(inputs, weights_all, positions)

    def one_sequence(totals, seq_data):
        outputs, pullback = jax.vjp(run_layer, seq_data[0].astype(jnp.float32), *params)
        gradients = pullback(seq_data[1].astype(jnp.float32))
        totals = tuple((total + grad for total, grad in zip(totals, gradients[1:])))
        return (totals, (outputs.astype(jnp.bfloat16), gradients[0].astype(jnp.bfloat16)))
    zeros = tuple((jnp.zeros_like(weight) for weight in params))
    totals, (outputs, grad_inputs) = lax.scan(one_sequence, zeros, (tokens, grad_out))
    return (outputs, grad_inputs, totals[0], totals[1], totals[2], totals[3], totals[4], totals[5], totals[6], totals[7], totals[8])
```

```python
import functools
import itertools

import jax
import jax.numpy as jnp
from jax import lax
from jax.experimental import pallas as pl
from jax.experimental.pallas import tpu as pltpu
from jax.sharding import PartitionSpec as P

ALL = ("dp", "ctx")
EPS = 1e-05
DIM = 1152
HEAD = 64
HALF_Q = 576
KV = 384
QKV = 1024
FF_PART = 768
TILE = 256
BF = jnp.bfloat16
F32 = jnp.float32


def flat(l, c, h, x, z):
    return (2 * l + c) * 32 + (4 * h + x) * 4 + z


def moves(target):
    places = itertools.product(range(2), range(2), range(2), range(4), range(4))
    return [(flat(*place), flat(*target(*place))) for place in places]


def send(value, target):
    return lax.ppermute(value, ALL, moves(target))


def to_z(step):
    return lambda l, c, h, x, z: (l, c, h, x, (z + step) % 4)


def to_x(step):
    return lambda l, c, h, x, z: (l, c, h, (x + step) % 4, z)


def to_y(step):
    def target(l, c, h, x, z):
        y = (2 * h + l + step) % 4
        return (y % 2, c, y // 2, x, z)

    return target


def other_core(l, c, h, x, z):
    return (l, 1 - c, h, x, z)


def other_h(l, c, h, x, z):
    return (l, c, 1 - h, x, z)


def z_pair(l, c, h, x, z):
    return (l, c, h, x, z ^ 1)


def home(l, c, h, x, z):
    return (l, z // 2, h, x, 2 * c + z % 2)


def home_pair(l, c, h, x, z):
    return (l, z // 2, h, x, 2 * c + 1 - z % 2)


def swap_halves(block):
    lane = lax.broadcasted_iota(jnp.int32, block.shape, 1) % HEAD
    return jnp.where(
        lane < HEAD // 2, pltpu.roll(block, 128 - HEAD // 2, 1), pltpu.roll(block, HEAD // 2, 1)
    )


def qkv_kernel(rows_ref, order_ref, weight_ref, gain_ref, cos_ref, sin_ref, x_ref, normed_ref, q_ref, kv_ref):
    inputs = jnp.dot(rows_ref[...], order_ref[...], preferred_element_type=F32)
    x_ref[...] = inputs
    inverse = lax.rsqrt(jnp.mean(inputs * inputs, axis=-1, keepdims=True) + EPS)
    normed = (inputs * inverse * gain_ref[...]).astype(BF)
    normed_ref[...] = normed
    proj = jnp.dot(normed, weight_ref[...], preferred_element_type=F32)
    cos_table, sin_table = cos_ref[...], sin_ref[...]
    for start in range(0, QKV, 128):
        block = proj[:, start : start + 128]
        turned = block * cos_table + swap_halves(block) * sin_table
        if start < 512:
            q_ref[:, start : start + 128] = (turned * 0.125).astype(BF)
        elif start == 512:
            q_ref[:, 512:576] = (turned[:, :64] * 0.125).astype(BF)
        elif start == 640:
            kv_ref[:, 0:128] = turned.astype(BF)
        elif start == 768:
            lane = lax.broadcasted_iota(jnp.int32, block.shape, 1)
            kv_ref[:, 128:256] = jnp.where(lane < HEAD, turned, block).astype(BF)
        else:
            kv_ref[:, 256:384] = block.astype(BF)


def stack_heads(block, kv_head, upper):
    parts = []
    for group in range(3):
        start = (kv_head * 3 + group) * HEAD
        parts.append(block[:, start : start + HEAD])
    rows = jnp.concatenate(parts, axis=0)
    zeros = jnp.zeros_like(rows)
    return jnp.concatenate([zeros, rows] if upper else [rows, zeros], axis=1)


K_GROUP = (0, 0, 128)
K_UPPER = (False, True, False)
V_GROUP = (128, 256, 256)
V_UPPER = (True, False, True)
NT = (((1,), (1,)), ((), ()))
TN = (((0,), (0,)), ((), ()))


def mask_tile(scores, place, tile):
    row = lax.broadcasted_iota(jnp.int32, scores.shape, 0) % 64 + place * 64
    key = lax.broadcasted_iota(jnp.int32, scores.shape, 1) + tile * TILE
    return jnp.where(key <= row, scores, -1e30)


def attend_kernel(source_ref, place_ref, q_ref, kv_ref, out_ref, log_ref, sorted_ref, score_ref):
    def put(index, carry):
        origin = pl.multiple_of(source_ref[index] * 64, 64)
        here = pl.multiple_of(index * 64, 64)
        sorted_ref[pl.ds(here, 64), :] = kv_ref[pl.ds(origin, 64), :]
        return carry

    lax.fori_loop(0, 64, put, 0)
    for block in range(4):
        place = place_ref[block]
        last = (place * 64) // TILE
        rows = q_ref[block * 64 : block * 64 + 64, :]
        queries = [stack_heads(rows, head, K_UPPER[head]) for head in range(3)]

        def score(tile, carry, masked):
            start = pl.multiple_of(tile * TILE, TILE)
            result = []
            for head in range(3):
                keys = sorted_ref[pl.ds(start, TILE), K_GROUP[head] : K_GROUP[head] + 128]
                scores = lax.dot_general(queries[head], keys, NT, preferred_element_type=F32)
                if masked:
                    scores = mask_tile(scores, place, tile)
                score_ref[head, tile] = scores
                result.append(
                    jnp.maximum(carry[head], jnp.maximum(scores[:, :128], scores[:, 128:]))
                )
            return tuple(result)

        least = tuple(jnp.full((192, 128), -1e30, F32) for _ in range(3))
        top = lax.fori_loop(0, last, functools.partial(score, masked=False), least)
        top = score(last, top, True)
        row_max = [jnp.max(part, axis=1, keepdims=True) for part in top]

        def weigh(tile, carry):
            totals, sums = carry
            start = pl.multiple_of(tile * TILE, TILE)
            next_totals, next_sums = [], []
            for head in range(3):
                values = sorted_ref[pl.ds(start, TILE), V_GROUP[head] : V_GROUP[head] + 128]
                weights = jnp.exp(score_ref[head, tile] - row_max[head])
                next_totals.append(totals[head] + weights[:, :128] + weights[:, 128:])
                next_sums.append(
                    sums[head] + jnp.dot(weights.astype(BF), values, preferred_element_type=F32)
                )
            return (tuple(next_totals), tuple(next_sums))

        zeros = tuple(jnp.zeros((192, 128), F32) for _ in range(3))
        totals, sums = lax.fori_loop(0, last + 1, weigh, (zeros, zeros))
        for head in range(3):
            row_total = jnp.sum(totals[head], axis=1, keepdims=True)
            result = sums[head] / row_total
            side = result[:, 64:] if V_UPPER[head] else result[:, :64]
            for group in range(3):
                start = (head * 3 + group) * HEAD
                out_ref[block * 64 : block * 64 + 64, start : start + HEAD] = side[
                    group * 64 : group * 64 + 64
                ]
            log_ref[block, head] = jnp.broadcast_to(row_max[head] + jnp.log(row_total), (192, 128))


def attend_back_kernel(
    spot_ref, place_ref, q_ref, sorted_ref, out_ref, log_ref, grad_ref, dq_ref, dkv_ref, total_ref
):
    total_ref[...] = jnp.zeros_like(total_ref)
    for block in range(4):
        place = place_ref[block]
        last = (place * 64) // TILE
        here = slice(block * 64, block * 64 + 64)
        rows, grads, outs = q_ref[here, :], grad_ref[here, :], out_ref[here, :]
        products = grads.astype(F32) * outs
        queries, grad_rows, deltas, logs = [], [], [], []
        for head in range(3):
            queries.append(stack_heads(rows, head, K_UPPER[head]))
            grad_rows.append(stack_heads(grads, head, V_UPPER[head]))
            deltas.append(
                jnp.sum(stack_heads(products, head, False), axis=1, keepdims=True)
            )
            logs.append(log_ref[block, head][:, :1])

        def step(tile, carry, masked):
            start = pl.multiple_of(tile * TILE, TILE)
            span = pl.ds(start, TILE)
            result = []
            for head in range(3):
                k_lanes = slice(K_GROUP[head], K_GROUP[head] + 128)
                v_lanes = slice(V_GROUP[head], V_GROUP[head] + 128)
                keys = sorted_ref[span, k_lanes]
                values = sorted_ref[span, v_lanes]
                scores = lax.dot_general(queries[head], keys, NT, preferred_element_type=F32)
                if masked:
                    scores = mask_tile(scores, place, tile)
                prob = jnp.exp(scores - logs[head])
                grad_prob = lax.dot_general(grad_rows[head], values, NT, preferred_element_type=F32)
                grad_scores = (prob * (grad_prob - deltas[head])).astype(BF)
                total_ref[span, v_lanes] += lax.dot_general(
                    prob.astype(BF), grad_rows[head], TN, preferred_element_type=F32
                )
                total_ref[span, k_lanes] += lax.dot_general(
                    grad_scores, queries[head], TN, preferred_element_type=F32
                )
                result.append(
                    carry[head] + jnp.dot(grad_scores, keys, preferred_element_type=F32)
                )
            return tuple(result)

        zeros = tuple(jnp.zeros((192, 128), F32) for _ in range(3))
        dq = lax.fori_loop(0, last, functools.partial(step, masked=False), zeros)
        dq = step(last, dq, True)
        for head in range(3):
            side = dq[head][:, 64:] if K_UPPER[head] else dq[head][:, :64]
            for group in range(3):
                start = (head * 3 + group) * HEAD
                dq_ref[here, start : start + HEAD] = side[group * 64 : group * 64 + 64] * 0.125

    def put(index, carry):
        origin = pl.multiple_of(spot_ref[index] * 64, 64)
        there = pl.multiple_of(index * 64, 64)
        dkv_ref[pl.ds(there, 64), :] = total_ref[pl.ds(origin, 64), :].astype(BF)
        return carry

    lax.fori_loop(0, 64, put, 0)


def unrotate_kernel(dq_ref, dkv_ref, cos_ref, sin_ref, out_ref):
    cos_table, sin_table = cos_ref[...], sin_ref[...]

    def turn(block):
        return block * cos_table - swap_halves(block) * sin_table

    for start in range(0, 512, 128):
        out_ref[:, start : start + 128] = turn(dq_ref[:, start : start + 128]).astype(BF)
    tail = dq_ref[:, 512:576]
    wide = jnp.concatenate([tail, jnp.zeros_like(tail)], axis=1)
    out_ref[:, 512:640] = turn(wide).astype(BF)
    out_ref[:, 640:768] = turn(dkv_ref[:, 0:128]).astype(BF)
    block = dkv_ref[:, 128:256]
    lane = lax.broadcasted_iota(jnp.int32, block.shape, 1)
    out_ref[:, 768:896] = jnp.where(lane < HEAD, turn(block), block).astype(BF)
    out_ref[:, 896:1024] = dkv_ref[:, 256:384].astype(BF)


VMEM = pl.BlockSpec(memory_space=pltpu.VMEM)
SMEM = pl.BlockSpec(memory_space=pltpu.SMEM)
ROOM = pltpu.CompilerParams(vmem_limit_bytes=48 * 1024 * 1024)


def project(rows, order, weight, gain, cos_table, sin_table):
    return pl.pallas_call(
        qkv_kernel,
        out_shape=(
            jax.ShapeDtypeStruct((256, DIM), F32),
            jax.ShapeDtypeStruct((256, DIM), BF),
            jax.ShapeDtypeStruct((256, HALF_Q), BF),
            jax.ShapeDtypeStruct((256, KV), BF),
        ),
        in_specs=[VMEM] * 6,
        out_specs=(VMEM,) * 4,
        compiler_params=ROOM,
    )(rows, order, weight, gain, cos_table, sin_table)


def attend(source, place, queries, kv):
    return pl.pallas_call(
        attend_kernel,
        out_shape=(
            jax.ShapeDtypeStruct((256, HALF_Q), F32),
            jax.ShapeDtypeStruct((4, 3, 192, 128), F32),
            jax.ShapeDtypeStruct((4096, KV), BF),
        ),
        in_specs=[SMEM, SMEM, VMEM, VMEM],
        out_specs=(VMEM,) * 3,
        scratch_shapes=[pltpu.VMEM((3, 16, 192, TILE), F32)],
        compiler_params=ROOM,
    )(source, place, queries, kv)


def attend_back(spot, place, queries, kv, out, logs, grad):
    return pl.pallas_call(
        attend_back_kernel,
        out_shape=(
            jax.ShapeDtypeStruct((256, HALF_Q), F32),
            jax.ShapeDtypeStruct((4096, KV), BF),
        ),
        in_specs=[SMEM, SMEM] + [VMEM] * 5,
        out_specs=(VMEM,) * 2,
        scratch_shapes=[pltpu.VMEM((4096, KV), F32)],
        compiler_params=ROOM,
    )(spot, place, queries, kv, out, logs, grad)


def unrotate(dq, dkv, cos_table, sin_table):
    return pl.pallas_call(
        unrotate_kernel,
        out_shape=jax.ShapeDtypeStruct((256, QKV), BF),
        in_specs=[VMEM] * 4,
        out_specs=VMEM,
        compiler_params=ROOM,
    )(dq, dkv, cos_table, sin_table)


def pick(matrix, value):
    return jnp.dot(matrix, value, preferred_element_type=F32).astype(BF)


def gather_y(pieces, z_order, y_order):
    part = pick(z_order, jnp.concatenate(pieces, axis=0))
    parts = [part] + [send(part, to_y(step)) for step in (1, 2, 3)]
    return pick(y_order, jnp.concatenate(parts, axis=0))


def gather_x(block):
    half = jnp.concatenate([block] + [send(block, to_x(step)) for step in (1, 2, 3)], axis=0)
    return jnp.concatenate([half, send(half, other_core)], axis=0)


def add_up(parts):
    total = parts[0].astype(F32)
    for part in parts[1:]:
        total = total + part.astype(F32)
    return total


def scatter(value, z_order, y_order):
    count = value.shape[0] // 2
    half = add_up([value[:count], send(value[count:].astype(BF), other_core)])
    quarter = half.reshape(4, 144, half.shape[1])
    low = quarter[1:].astype(BF)
    block = add_up([quarter[0]] + [send(low[step - 1], to_x(-step)) for step in (1, 2, 3)])
    spread = jnp.dot(y_order.T, block.astype(BF), preferred_element_type=F32).astype(BF)
    spread = spread.reshape(4, 48, -1)
    part = add_up([spread[0]] + [send(spread[step], to_y(-step)) for step in (1, 2, 3)])
    pieces = jnp.dot(z_order.T, part.astype(BF), preferred_element_type=F32).astype(BF)
    pieces = pieces.reshape(4, 16, -1)
    return [pieces[0]] + [send(pieces[step], to_z(-step)) for step in (1, 2, 3)]


def rms_parts(inputs, gain):
    inverse = lax.rsqrt(jnp.mean(inputs * inputs, axis=-1, keepdims=True) + EPS)
    scaled = inputs * inverse
    return (scaled * gain, scaled, inverse)


def rms_back(grad_normed, scaled, inverse, gain):
    gain_terms = grad_normed * scaled
    grad_scaled = grad_normed * gain
    grad_inputs = inverse * (
        grad_scaled - scaled * jnp.mean(grad_scaled * scaled, axis=-1, keepdims=True)
    )
    return (grad_inputs, gain_terms)


def rope_tables(positions):
    lane = jnp.arange(128, dtype=jnp.int32)
    inverse = 1.0 / 10000.0 ** ((lane % 32).astype(F32) * (2.0 / HEAD))
    angles = positions.astype(F32)[:, None] * inverse[None, :]
    sign = jnp.where(lane % HEAD < HEAD // 2, -1.0, 1.0)
    return (jnp.cos(angles), jnp.sin(angles) * sign[None, :])


def one_hot(rows, columns):
    return (rows == columns).astype(BF)


def body(
    tokens,
    grad_out,
    pair_order,
    attn_gain,
    query_weight,
    key_weight,
    value_weight,
    output_weight,
    ffn_gain,
    gate_weight,
    up_weight,
    down_weight,
):
    dp, ctx = lax.axis_index("dp"), lax.axis_index("ctx")
    l, c = dp // 2, dp % 2
    h, x, z = ctx // 16, (ctx // 4) % 4, ctx % 4
    y, b = 2 * h + l, z % 2
    even = b == 0

    local = jnp.arange(DIM, dtype=jnp.int32)
    from_c = (local // 576) ^ c
    from_x = (x - (local // 144) % 4) % 4
    from_y = (y - (local // 36) % 4) % 4
    from_z = (local // 9) % 4
    owner = (2 * (from_y % 2) + from_c) * 32 + (4 * (from_y // 2) + from_x) * 4 + from_z
    natural = owner * 9 + local % 9
    order = one_hot(jnp.arange(DIM, dtype=jnp.int32)[:, None], natural[None, :])
    rows48 = jnp.arange(48, dtype=jnp.int32)
    z_column = jnp.where(rows48 < 36, ((z - rows48 // 9) % 4) * 16 + rows48 % 9, -1)
    z_order = one_hot(z_column[:, None], jnp.arange(64, dtype=jnp.int32)[None, :])
    rows144 = jnp.arange(144, dtype=jnp.int32)
    y_order = one_hot(
        ((rows144 // 36) * 48 + rows144 % 36)[:, None], jnp.arange(192, dtype=jnp.int32)[None, :]
    )
    chunk = jnp.arange(64, dtype=jnp.int32)
    chunk_ctx = (
        ((chunk // 4) % 2 ^ h) * 16
        + ((x - (chunk // 8) % 4) % 4) * 4
        + 2 * ((chunk // 32) ^ c)
        + ((chunk // 2) % 2 ^ b)
    )
    ctx_match = chunk_ctx[:, None] == jnp.arange(32, dtype=jnp.int32)[None, :]
    chunk_pair = jnp.sum(jnp.where(ctx_match, pair_order[None, :], 0), axis=1)
    spot = jnp.where(chunk % 2 == 0, chunk_pair, 63 - chunk_pair)
    source = jnp.sum(jnp.where(spot[None, :] == chunk[:, None], chunk[None, :], 0), axis=1)
    place = spot[:4]
    positions = (place[:, None] * 64 + jnp.arange(64, dtype=jnp.int32)[None, :]).reshape(256)
    cos_table, sin_table = rope_tables(positions)

    rows_own = send(tokens[0], home)
    rows_pair = send(tokens[0], home_pair)

    def half_weights(side):
        return jnp.concatenate(
            [
                query_weight[:, side * 576 : side * 576 + 576],
                attn_gain[:, None],
                ffn_gain[:, None],
                jnp.zeros((9, 62), BF),
                key_weight[:, side * 192 : side * 192 + 192],
                value_weight[:, side * 192 : side * 192 + 192],
            ],
            axis=1,
        )

    rows_pad = ((0, 7), (0, 0))
    side_zero, side_one = half_weights(0), half_weights(1)
    mine = jnp.pad(jnp.where(even, side_zero, side_one), rows_pad)
    other = jnp.pad(jnp.where(even, side_one, side_zero), rows_pad)
    qkv_pieces = [
        mine,
        send(other, to_z(1)),
        send(mine, to_z(2)),
        send(other, to_z(3)),
    ]
    qkv_weight = gather_x(gather_y(qkv_pieces, z_order, y_order))
    gain_rows = jnp.einsum(
        "kc,dc->kd",
        one_hot(576 + jnp.arange(2, dtype=jnp.int32)[:, None], jnp.arange(QKV, dtype=jnp.int32)[None, :]),
        qkv_weight,
        preferred_element_type=F32,
    )
    gain_attn, gain_ffn = gain_rows[0:1], gain_rows[1:2]

    def slice_weights(step):
        start = ((z + step) % 4) * FF_PART
        parts = [
            lax.dynamic_slice_in_dim(weight, start, FF_PART, 1)
            for weight in (gate_weight, up_weight, down_weight)
        ]
        return jnp.pad(jnp.concatenate(parts + [output_weight], axis=1), rows_pad)

    ffn_pieces = [slice_weights(0)] + [send(slice_weights(step), to_z(step)) for step in (1, 2, 3)]
    ffn_weights = gather_x(gather_y(ffn_pieces, z_order, y_order))
    gate_part = ffn_weights[:, 0:768]
    up_part = ffn_weights[:, 768:1536]
    down_part = ffn_weights[:, 1536:2304]
    full_output = ffn_weights[:, 2304:3456]

    inputs, normed_a, queries, kv_own = project(
        jnp.concatenate([rows_own, rows_pair], axis=0),
        order,
        qkv_weight,
        gain_attn,
        cos_table,
        sin_table,
    )
    kv = jnp.concatenate([kv_own, send(kv_own, other_h)], axis=0)
    kv = jnp.concatenate([kv] + [send(kv, to_x(step)) for step in (1, 2, 3)], axis=0)
    kv = jnp.concatenate([kv, send(kv, other_core)], axis=0)
    heads_out, logs, kv_sorted = attend(source, place, queries, kv)
    heads_low = heads_out.astype(BF)

    grad_own = send(grad_out[0], home)
    ffn_rows = jnp.concatenate([rows_own, grad_own], axis=1)
    ffn_rows = [ffn_rows] + [send(ffn_rows, to_z(step)) for step in (1, 2, 3)]
    ffn_rows = jnp.concatenate(ffn_rows, axis=0)
    ffn_inputs = jnp.dot(ffn_rows[:, :DIM], order, preferred_element_type=F32)
    grad_rows = pick_columns(ffn_rows[:, DIM:], order)
    heads_all = [heads_low] + [send(heads_low, to_z(step)) for step in (1, 2, 3)]

    def whole_rows(low_from, upper_from, low_own):
        low = heads_all[low_from][:128] if low_own else heads_all[low_from][128:]
        upper = heads_all[upper_from][128:] if low_own else heads_all[upper_from][:128]
        return jnp.concatenate([low, upper], axis=1)

    attended = jnp.where(
        even,
        jnp.concatenate(
            [
                whole_rows(0, 3, True),
                whole_rows(2, 1, False),
                whole_rows(2, 1, True),
                whole_rows(0, 3, False),
            ],
            axis=0,
        ),
        jnp.concatenate(
            [
                whole_rows(1, 0, False),
                whole_rows(1, 0, True),
                whole_rows(3, 2, False),
                whole_rows(3, 2, True),
            ],
            axis=0,
        ),
    )
    hidden_one = ffn_inputs + jnp.einsum(
        "tq,dq->td", attended, full_output, preferred_element_type=F32
    )
    normed_f, scaled_f, inverse_f = rms_parts(hidden_one, gain_ffn)
    normed_f = normed_f.astype(BF)
    gate = jnp.dot(normed_f, gate_part, preferred_element_type=F32)
    up_proj = jnp.dot(normed_f, up_part, preferred_element_type=F32)
    sigmoid_gate = jax.nn.sigmoid(gate)
    activated = gate * sigmoid_gate
    hidden = (activated * up_proj).astype(BF)
    out_terms = jnp.einsum("tf,df->td", hidden, down_part, preferred_element_type=F32)
    grad_hidden = jnp.dot(grad_rows, down_part, preferred_element_type=F32)
    grad_gate = (grad_hidden * up_proj * sigmoid_gate * (1.0 + gate * (1.0 - sigmoid_gate))).astype(BF)
    grad_up = (grad_hidden * activated).astype(BF)
    grad_normed_f = jnp.einsum(
        "tf,df->td", grad_gate, gate_part, preferred_element_type=F32
    ) + jnp.einsum("tf,df->td", grad_up, up_part, preferred_element_type=F32)

    def sum_rows(terms):
        low = terms[128:].astype(BF).reshape(3, 128, DIM)
        return add_up([terms[:128]] + [send(low[step - 1], to_z(-step)) for step in (1, 2, 3)])

    grad_from_ffn, ffn_gain_terms = rms_back(
        sum_rows(grad_normed_f), scaled_f[:128], inverse_f[:128], gain_ffn
    )
    grad_hidden_one = grad_rows[:128].astype(F32) + grad_from_ffn
    grad_branch = grad_hidden_one.astype(BF)
    grad_branch = jnp.concatenate([grad_branch, send(grad_branch, z_pair)], axis=0)
    block_out = (hidden_one[:128] + sum_rows(out_terms)).astype(BF)
    block_out = send(unpick_columns(block_out, order), home)

    output_part = jnp.where(even, full_output[:, :576], full_output[:, 576:])
    grad_heads = jnp.dot(grad_branch, output_part, preferred_element_type=F32).astype(BF)
    output_grad = jnp.einsum("td,tq->dq", grad_branch, heads_low, preferred_element_type=F32)
    dq, dkv = attend_back(spot, place, queries, kv_sorted, heads_out, logs, grad_heads)

    down_grad = jnp.einsum("td,tf->df", grad_rows, hidden, preferred_element_type=F32)
    gate_grad = jnp.einsum("td,tf->df", normed_f, grad_gate, preferred_element_type=F32)
    up_grad = jnp.einsum("td,tf->df", normed_f, grad_up, preferred_element_type=F32)
    ffn_grads = jnp.concatenate([gate_grad, up_grad, down_grad], axis=1)
    ffn_pieces = scatter(ffn_grads, z_order, y_order)

    dkv = add_up([dkv[:2048], send(dkv[2048:], other_core)])
    dkv = dkv.reshape(4, 512, KV)
    low = dkv[1:].astype(BF)
    dkv = add_up([dkv[0]] + [send(low[step - 1], to_x(-step)) for step in (1, 2, 3)])
    dkv = add_up([dkv[:256], send(dkv[256:].astype(BF), other_h)])
    grad_qkv = unrotate(dq, dkv, cos_table, sin_table)
    qkv_grad = jnp.einsum("td,tq->dq", normed_a, grad_qkv, preferred_element_type=F32)
    grad_normed_a = jnp.einsum("tq,dq->td", grad_qkv, qkv_weight, preferred_element_type=F32)
    grad_normed_a = grad_normed_a[:128] + send(grad_normed_a[128:].astype(BF), z_pair).astype(F32)
    _, scaled_a, inverse_a = rms_parts(inputs[:128], gain_attn)
    grad_from_attn, attn_gain_terms = rms_back(grad_normed_a, scaled_a, inverse_a, gain_attn)
    grad_inputs = (grad_hidden_one + grad_from_attn).astype(BF)
    grad_inputs = send(unpick_columns(grad_inputs, order), home)

    lanes = jnp.arange(QKV, dtype=jnp.int32)[None, :]
    gain_grads = jnp.einsum(
        "td,tk->dk",
        jnp.concatenate([attn_gain_terms, ffn_gain_terms], axis=0).astype(BF),
        one_hot(576 + jnp.arange(256, dtype=jnp.int32)[:, None] // 128, lanes),
        preferred_element_type=F32,
    )
    attn_pieces = scatter(
        jnp.concatenate([qkv_grad + gain_grads, output_grad], axis=1), z_order, y_order
    )

    from_mine = add_up([attn_pieces[0], attn_pieces[2]])[:9]
    from_other = add_up([attn_pieces[1], attn_pieces[3]])[:9]
    side_zero = jnp.where(even, from_mine, from_other)
    side_one = jnp.where(even, from_other, from_mine)

    def both(start, count):
        return jnp.concatenate(
            [side_zero[:, start : start + count], side_one[:, start : start + count]], axis=1
        )

    attn_gain_grad = side_zero[:, 576] + side_one[:, 576]
    ffn_gain_grad = side_zero[:, 577] + side_one[:, 577]
    stacked = jnp.stack(ffn_pieces)[:, :9].astype(F32)

    def whole(start):
        slices = [
            lax.dynamic_index_in_dim(stacked, (part - z) % 4, 0, keepdims=False)[:, start : start + 768]
            for part in range(4)
        ]
        return jnp.concatenate(slices, axis=1)

    return (
        block_out[None],
        grad_inputs[None],
        attn_gain_grad,
        both(0, 576),
        both(640, 192),
        both(832, 192),
        both(1024, 576),
        ffn_gain_grad,
        whole(0),
        whole(768),
        whole(1536),
    )


def pick_columns(rows, order):
    return jnp.dot(rows, order, preferred_element_type=F32).astype(BF)


def unpick_columns(rows, order):
    return jnp.einsum("tk,dk->td", rows, order, preferred_element_type=F32).astype(BF)


def solution(mesh):
    weights = P(ALL, None)
    rows = P("dp", "ctx", None)
    return jax.shard_map(
        body,
        mesh=mesh,
        in_specs=(rows, rows, P(), P(ALL), weights, weights, weights, weights, P(ALL), weights, weights, weights),
        out_specs=(rows, rows, P(ALL), weights, weights, weights, weights, P(ALL), weights, weights, weights),
        check_vma=False,
    )
```

```python
import functools
import itertools

import jax
import jax.numpy as jnp
from jax import lax
from jax.experimental import pallas as pl
from jax.experimental.pallas import tpu as pltpu
from jax.sharding import PartitionSpec as P

ALL = ("dp", "ctx")
EPS = 1e-05
DIM = 1152
HEAD = 64
HALF_Q = 576
KV = 384
QKV = 1024
FF_PART = 768
FFN = 3456
PIECES = 3968
TILE = 256
BF = jnp.bfloat16
F32 = jnp.float32


def flat(l, c, h, x, z):
    return (2 * l + c) * 32 + (4 * h + x) * 4 + z


def moves(target):
    places = itertools.product(range(2), range(2), range(2), range(4), range(4))
    return [(flat(*place), flat(*target(*place))) for place in places]


def send(value, target):
    return lax.ppermute(value, ALL, moves(target))


def to_z(step):
    return lambda l, c, h, x, z: (l, c, h, x, (z + step) % 4)


def turn_by(step, first):
    def target(l, c, h, x, z):
        y = 2 * h + l
        if (c == 0) == first:
            y = (y + step) % 4
        else:
            x = (x + step) % 4
        return (y % 2, c, y // 2, x, z)

    return target


def other_core(l, c, h, x, z):
    return (l, 1 - c, h, x, z)


def z_pair(l, c, h, x, z):
    return (l, c, h, x, z ^ 1)


def home(flip):
    return lambda l, c, h, x, z: (l, z // 2, h, x, (2 * c + z % 2) ^ flip)


Z_GROUPS = [[ring * 4 + z for z in range(4)] for ring in range(8)]
CHIP_GROUPS = [
    [flat(y % 2, c, y // 2, x, z) for x in range(4) for y in range(4) for z in range(4)] for c in range(2)
]
HX_GROUPS = [[place * 4 + z for place in range(8)] for z in range(4)]


def exchange(parts, groups):
    return lax.all_to_all(parts, "ctx", 0, 0, tiled=True, axis_index_groups=groups)


def swap_halves(block):
    lane = lax.broadcasted_iota(jnp.int32, block.shape, 1) % HEAD
    return jnp.where(
        lane < HEAD // 2, pltpu.roll(block, 128 - HEAD // 2, 1), pltpu.roll(block, HEAD // 2, 1)
    )


def fill(ref, row, lane, value):
    ref[row : row + value.shape[0], lane : lane + value.shape[1]] = value


def pack_kernel(z_ref, *refs):
    arrived, sems = refs[13:21], refs[21]
    copies = [
        pltpu.make_async_copy(here, there, sems.at[index])
        for index, (here, there) in enumerate(zip(refs[:8], arrived))
    ]
    for copy in copies:
        copy.start()
    for copy in copies:
        copy.wait()
    gain_ref, q_ref, k_ref, v_ref, o_ref, gate_ref, up_ref, down_ref = arrived
    attn_ref = refs[8]
    attn_ref[0:32, :] = jnp.zeros((32, QKV), BF)
    for side in range(2):
        row = side * 16
        fill(attn_ref, row, 0, q_ref[:, side * 576 : side * 576 + 576])
        fill(attn_ref, row, 576, gain_ref[...])
        fill(attn_ref, row, 640, k_ref[:, side * 192 : side * 192 + 192])
        fill(attn_ref, row, 832, v_ref[:, side * 192 : side * 192 + 192])
    both = attn_ref[0:32, :]

    def copy_both(index, carry):
        attn_ref[pl.ds(pl.multiple_of(index * 32, 32), 32), :] = both
        return carry

    lax.fori_loop(1, 32, copy_both, 0)
    for step in range(4):
        ffn_ref = refs[9 + step]
        ffn_ref[...] = jnp.zeros((16, FFN), BF)
        start = pl.multiple_of(((z_ref[0] + step) % 4) * FF_PART, FF_PART)
        fill(ffn_ref, 0, 0, gate_ref[:, pl.ds(start, FF_PART)])
        fill(ffn_ref, 0, 768, up_ref[:, pl.ds(start, FF_PART)])
        fill(ffn_ref, 0, 1536, down_ref[:, pl.ds(start, FF_PART)])
        fill(ffn_ref, 0, 2304, o_ref[...])


def qkv_kernel(
    own_ref, pair_ref, order_ref, half_ref, other_ref, cos_ref, sin_ref,
    x_ref, normed_ref, q_ref, kv_ref, weight_ref, gain_ref, rows_ref,
):
    rows_ref[0:128, :] = own_ref[...]
    rows_ref[128:256, :] = pair_ref[...]
    weight_ref[0:576, :] = half_ref[...]
    weight_ref[576:1152, :] = other_ref[...]
    inputs = jnp.dot(rows_ref[...], order_ref[...], preferred_element_type=F32)
    x_ref[...] = inputs
    lane = lax.broadcasted_iota(jnp.int32, (8, 128), 1)
    row = lax.broadcasted_iota(jnp.int32, (8, 128), 0)
    gains = lax.dot_general(
        (lane == row + 64).astype(BF), weight_ref[:, 512:640], NT, preferred_element_type=F32
    )
    gain_ref[...] = gains
    inverse = lax.rsqrt(jnp.mean(inputs * inputs, axis=-1, keepdims=True) + EPS)
    normed = (inputs * inverse * gains[0:1]).astype(BF)
    normed_ref[...] = normed
    proj = jnp.dot(normed, weight_ref[...], preferred_element_type=F32)
    cos_table, sin_table = cos_ref[...], sin_ref[...]
    kv_parts = []
    for start in range(0, QKV, 128):
        block = proj[:, start : start + 128]
        turned = block * cos_table + swap_halves(block) * sin_table
        if start < 512:
            q_ref[:, start : start + 128] = (turned * 0.125).astype(BF)
        elif start == 512:
            q_ref[:, 512:576] = (turned[:, :64] * 0.125).astype(BF)
        elif start == 640:
            kv_parts.append(turned.astype(BF))
        elif start == 768:
            side = lax.broadcasted_iota(jnp.int32, block.shape, 1)
            kv_parts.append(jnp.where(side < HEAD, turned, block).astype(BF))
        else:
            kv_parts.append(block.astype(BF))
    for copy in range(8):
        for part in range(3):
            fill(kv_ref, copy * 256, part * 128, kv_parts[part])


def stack_heads(block, kv_head, upper):
    parts = []
    for group in range(3):
        start = (kv_head * 3 + group) * HEAD
        parts.append(block[:, start : start + HEAD])
    rows = jnp.concatenate(parts, axis=0)
    zeros = jnp.zeros_like(rows)
    return jnp.concatenate([zeros, rows] if upper else [rows, zeros], axis=1)


K_GROUP = (0, 0, 128)
K_UPPER = (False, True, False)
V_GROUP = (128, 256, 256)
V_UPPER = (True, False, True)
NT = (((1,), (1,)), ((), ()))
TN = (((0,), (0,)), ((), ()))


def mask_tile(scores, place, tile):
    row = lax.broadcasted_iota(jnp.int32, scores.shape, 0) % 64 + place * 64
    key = lax.broadcasted_iota(jnp.int32, scores.shape, 1) + tile * TILE
    return jnp.where(key <= row, scores, -1e30)


def attend_kernel(
    spot_ref, place_ref, side_ref, q_ref, near_ref, far_ref, out_ref, log_ref, sorted_ref, low_ref, score_ref
):
    def put(index, carry):
        here = pl.ds(pl.multiple_of(index * 64, 64), 64)
        sorted_ref[pl.ds(pl.multiple_of(spot_ref[index] * 64, 64), 64), :] = near_ref[here, :]
        sorted_ref[pl.ds(pl.multiple_of(spot_ref[index + 32] * 64, 64), 64), :] = far_ref[here, :]
        return carry

    lax.fori_loop(0, 32, put, 0)
    for block in range(4):
        place = place_ref[block]
        last = (place * 64) // TILE
        rows = q_ref[block * 64 : block * 64 + 64, :]
        queries = [stack_heads(rows, head, K_UPPER[head]) for head in range(3)]

        def score(tile, carry, masked):
            start = pl.multiple_of(tile * TILE, TILE)
            result = []
            for head in range(3):
                keys = sorted_ref[pl.ds(start, TILE), K_GROUP[head] : K_GROUP[head] + 128]
                scores = lax.dot_general(queries[head], keys, NT, preferred_element_type=F32)
                if masked:
                    scores = mask_tile(scores, place, tile)
                score_ref[head, tile] = scores
                result.append(
                    jnp.maximum(carry[head], jnp.maximum(scores[:, :128], scores[:, 128:]))
                )
            return tuple(result)

        least = tuple(jnp.full((192, 128), -1e30, F32) for _ in range(3))
        top = lax.fori_loop(0, last, functools.partial(score, masked=False), least)
        top = score(last, top, True)
        row_max = [jnp.max(part, axis=1, keepdims=True) for part in top]

        def weigh(tile, carry):
            totals, sums = carry
            start = pl.multiple_of(tile * TILE, TILE)
            next_totals, next_sums = [], []
            for head in range(3):
                values = sorted_ref[pl.ds(start, TILE), V_GROUP[head] : V_GROUP[head] + 128]
                weights = jnp.exp(score_ref[head, tile] - row_max[head])
                next_totals.append(totals[head] + weights[:, :128] + weights[:, 128:])
                next_sums.append(
                    sums[head] + jnp.dot(weights.astype(BF), values, preferred_element_type=F32)
                )
            return (tuple(next_totals), tuple(next_sums))

        zeros = tuple(jnp.zeros((192, 128), F32) for _ in range(3))
        totals, sums = lax.fori_loop(0, last + 1, weigh, (zeros, zeros))
        for head in range(3):
            row_total = jnp.sum(totals[head], axis=1, keepdims=True)
            result = sums[head] / row_total
            side = result[:, 64:] if V_UPPER[head] else result[:, :64]
            for group in range(3):
                start = (head * 3 + group) * HEAD
                out_ref[block * 64 : block * 64 + 64, start : start + HEAD] = side[
                    group * 64 : group * 64 + 64
                ]
            log_ref[block, head] = jnp.broadcast_to(row_max[head] + jnp.log(row_total), (192, 128))
    side = side_ref[0]
    for copy in range(4):
        for block in range(2):
            start = pl.multiple_of(copy * 256 + (block ^ side) * 128, 128)
            low_ref[pl.ds(start, 128), :] = out_ref[block * 128 : block * 128 + 128, :].astype(BF)


def attend_back_kernel(
    spot_ref, place_ref, q_ref, sorted_ref, out_ref, log_ref, own_ref, pair_ref, part_ref,
    dq_ref, near_ref, far_ref, total_ref, rows_ref, grad_ref,
):
    rows_ref[0:128, :] = own_ref[...]
    rows_ref[128:256, :] = pair_ref[...]
    grad_ref[...] = jnp.dot(rows_ref[...], part_ref[...], preferred_element_type=F32).astype(BF)
    total_ref[...] = jnp.zeros_like(total_ref)
    for block in range(4):
        place = place_ref[block]
        last = (place * 64) // TILE
        here = slice(block * 64, block * 64 + 64)
        rows, grads, outs = q_ref[here, :], grad_ref[here, :], out_ref[here, :]
        products = grads.astype(F32) * outs
        queries, grad_rows, deltas, logs = [], [], [], []
        for head in range(3):
            queries.append(stack_heads(rows, head, K_UPPER[head]))
            grad_rows.append(stack_heads(grads, head, V_UPPER[head]))
            deltas.append(
                jnp.sum(stack_heads(products, head, False), axis=1, keepdims=True)
            )
            logs.append(log_ref[block, head][:, :1])

        def step(tile, carry, masked):
            start = pl.multiple_of(tile * TILE, TILE)
            span = pl.ds(start, TILE)
            result = []
            for head in range(3):
                k_lanes = slice(K_GROUP[head], K_GROUP[head] + 128)
                v_lanes = slice(V_GROUP[head], V_GROUP[head] + 128)
                keys = sorted_ref[span, k_lanes]
                values = sorted_ref[span, v_lanes]
                scores = lax.dot_general(queries[head], keys, NT, preferred_element_type=F32)
                if masked:
                    scores = mask_tile(scores, place, tile)
                prob = jnp.exp(scores - logs[head])
                grad_prob = lax.dot_general(grad_rows[head], values, NT, preferred_element_type=F32)
                grad_scores = (prob * (grad_prob - deltas[head])).astype(BF)
                total_ref[span, v_lanes] += lax.dot_general(
                    prob.astype(BF), grad_rows[head], TN, preferred_element_type=F32
                )
                total_ref[span, k_lanes] += lax.dot_general(
                    grad_scores, queries[head], TN, preferred_element_type=F32
                )
                result.append(
                    carry[head] + jnp.dot(grad_scores, keys, preferred_element_type=F32)
                )
            return tuple(result)

        zeros = tuple(jnp.zeros((192, 128), F32) for _ in range(3))
        dq = lax.fori_loop(0, last, functools.partial(step, masked=False), zeros)
        dq = step(last, dq, True)
        for head in range(3):
            side = dq[head][:, 64:] if K_UPPER[head] else dq[head][:, :64]
            for group in range(3):
                start = (head * 3 + group) * HEAD
                dq_ref[here, start : start + HEAD] = side[group * 64 : group * 64 + 64] * 0.125

    def put(index, carry):
        there = pl.ds(pl.multiple_of(index * 64, 64), 64)
        origin = pl.ds(pl.multiple_of(spot_ref[index] * 64, 64), 64)
        near_ref[there, :] = total_ref[origin, :].astype(BF)
        origin = pl.ds(pl.multiple_of(spot_ref[index + 32] * 64, 64), 64)
        far_ref[there, :] = total_ref[origin, :].astype(BF)
        return carry

    lax.fori_loop(0, 32, put, 0)


def join_kernel(*refs):
    count = len(refs) - 2
    target, sems = refs[count], refs[count + 1]
    rows = refs[0].shape[0]
    copies = [
        pltpu.make_async_copy(refs[index], target.at[pl.ds(index * rows, rows)], sems.at[index])
        for index in range(count)
    ]
    for copy in copies:
        copy.start()
    for copy in copies:
        copy.wait()


def rows_kernel(z_ref, x0_ref, x1_ref, both2_ref, both3_ref, g0_ref, g1_ref, order_ref, out_ref, grad_ref):
    slots = [
        (x0_ref, g0_ref, 0),
        (x1_ref, g1_ref, 0),
        (both2_ref, both2_ref, DIM),
        (both3_ref, both3_ref, DIM),
    ]
    for slot, (rows_ref, grads_ref, lane) in enumerate(slots):
        here = pl.ds(pl.multiple_of((z_ref[0] ^ slot) * 128, 128), 128)
        grad_ref[here, 0:DIM] = rows_ref[:, 0:DIM]
        grad_ref[here, DIM:] = grads_ref[:, lane : lane + DIM]
    rows = grad_ref[:, 0:DIM]
    for start in range(0, DIM, 384):
        columns = order_ref[:, start : start + 384]
        out_ref[:, start : start + 384] = jnp.dot(rows, columns, preferred_element_type=F32).astype(BF)
    rows = grad_ref[:, DIM:]
    for start in range(0, DIM, 384):
        columns = order_ref[:, start : start + 384]
        grad_ref[:, start : start + 384] = jnp.dot(rows, columns, preferred_element_type=F32).astype(BF)


def ffn_kernel(
    z_ref, x_ref, grad_ref, heads_ref, gain_ref,
    w0_ref, w1_ref, w2_ref, w3_ref, far0_ref, far_ref,
    dn_ref, out0_ref, out1_ref, out2_ref, out3_ref, own_ref, grad_own_ref, hidden_ref, dgate_ref, dup_ref, normed_ref, part_ref, gain_grad_ref,
    w_ref, scaled_ref, heads_all_ref, h1_ref, dn_sum_ref, out_sum_ref, gate_ref, up_ref, dh_ref, sems,
):
    pieces = [(w0_ref, 0), (w1_ref, 144), (w2_ref, 288), (w3_ref, 432), (far0_ref, 576), (far_ref, 720)]
    copies = [
        pltpu.make_async_copy(piece, w_ref.at[pl.ds(row, piece.shape[0])], sems.at[index])
        for index, (piece, row) in enumerate(pieces)
    ]
    for copy in copies:
        copy.start()
    z = z_ref[0]
    for side in range(2):
        for half in range(2):
            start = (2 * side + half) * 256
            heads_all_ref[side * 256 : side * 256 + 256, half * 576 : half * 576 + 576] = heads_ref[
                start : start + 256, :
            ]
    for copy in copies:
        copy.wait()
    heads = heads_all_ref[...]
    for start in range(0, DIM, 384):
        h1_ref[:, start : start + 384] = x_ref[:, start : start + 384].astype(F32) + lax.dot_general(
            heads, w_ref[start : start + 384, 2304:3456], NT, preferred_element_type=F32
        )

    def norm(index, carry):
        here = pl.ds(pl.multiple_of(index * 64, 64), 64)
        rows = h1_ref[here, :]
        inverse = lax.rsqrt(jnp.mean(rows * rows, axis=-1, keepdims=True) + EPS)
        scaled = rows * inverse
        scaled_ref[here, :] = scaled.astype(BF)
        normed_ref[here, :] = (scaled * gain_ref[1:2, :]).astype(BF)
        return carry

    lax.fori_loop(0, 8, norm, 0)
    here = pl.ds(pl.multiple_of(z * 128, 128), 128)
    own_ref[...] = h1_ref[here, :]
    grad_own_ref[...] = grad_ref[here, 0:DIM]
    normed, grads = normed_ref[...], grad_ref[:, 0:DIM]

    def units(index, carry):
        start = pl.multiple_of(index * 256, 256)
        w_gate = w_ref[:, pl.ds(start, 256)]
        w_up = w_ref[:, pl.ds(start + 768, 256)]
        w_down = w_ref[:, pl.ds(start + 1536, 256)]
        gate_ref[...] = jnp.dot(normed, w_gate, preferred_element_type=F32)
        up_ref[...] = jnp.dot(normed, w_up, preferred_element_type=F32)
        dh_ref[...] = jnp.dot(grads, w_down, preferred_element_type=F32)

        def act(block, carry):
            here = pl.ds(pl.multiple_of(block * 64, 64), 64)
            there = pl.ds(start, 256)
            gate, up, grad = gate_ref[here, :], up_ref[here, :], dh_ref[here, :]
            sigmoid = jax.nn.sigmoid(gate)
            active = gate * sigmoid
            hidden_ref[here, there] = (active * up).astype(BF)
            dgate_ref[here, there] = (grad * up * sigmoid * (1.0 + gate * (1.0 - sigmoid))).astype(BF)
            dup_ref[here, there] = (grad * active).astype(BF)
            return carry

        lax.fori_loop(0, 8, act, 0)
        return carry

    lax.fori_loop(0, 3, units, 0)
    hidden, dgate, dup = hidden_ref[...], dgate_ref[...], dup_ref[...]
    for first in range(0, DIM, 384):
        rows = slice(first, first + 384)
        dn_sum_ref[:, rows] = lax.dot_general(
            dgate, w_ref[rows, 0:768], NT, preferred_element_type=F32
        ) + lax.dot_general(dup, w_ref[rows, 768:1536], NT, preferred_element_type=F32)
        out_sum_ref[:, rows] = lax.dot_general(
            hidden, w_ref[rows, 1536:2304], NT, preferred_element_type=F32
        )

    def finish(index, total):
        here = pl.ds(pl.multiple_of(index * 64, 64), 64)
        grad = dn_sum_ref[here, :]
        dn_ref[here, :] = grad.astype(BF)
        terms = grad * scaled_ref[here, :].astype(F32)
        return total + jnp.sum(terms.reshape(8, 8, DIM), axis=0)

    gain_grad_ref[...] = lax.fori_loop(0, 8, finish, jnp.zeros((8, DIM), F32))

    out0_ref[...] = own_ref[...] + out_sum_ref[here, :]
    for step, out_ref in enumerate((out1_ref, out2_ref, out3_ref)):
        there = pl.ds(pl.multiple_of(((z + step + 1) % 4) * 128, 128), 128)
        out_ref[...] = out_sum_ref[there, :].astype(BF)

    @pl.when(z % 2 == 0)
    def _():
        part_ref[...] = w_ref[:, 2304:2880]

    @pl.when(z % 2 == 1)
    def _():
        part_ref[...] = w_ref[:, 2880:3456]


def outer_products(lefts, rights, near_ref, far_ref, extra=None):
    for start in range(0, DIM, 128):
        lane = 0
        for left, right in zip(lefts, rights):
            block = lax.dot_general(
                left[:, start : start + 128], right[...], TN, preferred_element_type=F32
            )
            if extra is not None:
                block = extra(start, block)
            block = block.astype(near_ref.dtype)
            width = block.shape[1]
            lanes = slice(lane, lane + width)
            if start < 512:
                near_ref[start : start + 128, lanes] = block
            elif start == 512:
                near_ref[512:576, lanes] = block[:64]
                far_ref[0:64, lanes] = block[64:].astype(BF)
            else:
                far_ref[start - 576 : start - 448, lanes] = block.astype(BF)
            lane += width


def ffn_grad_kernel(normed_ref, grad_ref, hidden_ref, dgate_ref, dup_ref, near_ref, far_ref):
    outer_products(
        (normed_ref, normed_ref, grad_ref), (dgate_ref, dup_ref, hidden_ref), near_ref, far_ref
    )


def output_grad_kernel(own_ref, pair_ref, heads_ref, near_ref, far_ref, rows_ref):
    rows_ref[0:128, :] = own_ref[...]
    rows_ref[128:256, :] = pair_ref[...]
    outer_products((rows_ref,), (heads_ref,), near_ref, far_ref)


def merge_kernel(*refs):
    count = len(refs) // 2 - 2
    targets = refs[2 * count :]
    for index in range(4):
        lane = 0
        for near_ref, far_ref in zip(refs[:count], refs[count : 2 * count]):
            width = near_ref.shape[1]
            rows = slice(index * 144, index * 144 + 144)
            total = near_ref[rows, :].astype(F32) + far_ref[rows, :].astype(F32)
            targets[index][:, lane : lane + width] = total.astype(targets[index].dtype)
            lane += width


def spread_kernel(order_ref, *refs):
    targets = refs[-4:]
    first = 0
    for group in range(2):
        near_ref, *others = refs[4 * group : 4 * group + 4]
        count = near_ref.shape[1]
        for start in range(0, count, 512):
            lanes = slice(start, min(start + 512, count))
            total = near_ref[:, lanes]
            for other_ref in others:
                total = total + other_ref[:, lanes].astype(F32)
            parts = lax.dot_general(order_ref[...], total.astype(BF), TN, preferred_element_type=F32)
            there = slice(first + lanes.start, first + lanes.stop)
            for index in range(4):
                targets[index][:, there] = parts[index * 48 : index * 48 + 48].astype(BF)
        first += count
        if first % 128:
            for target in targets:
                target[:, first : first + 64] = jnp.zeros((48, 64), BF)
            first += 64


def split_kernel(order_ref, near_ref, a_ref, b_ref, c_ref, target):
    for start in range(0, target.shape[1], 512):
        lanes = slice(start, min(start + 512, target.shape[1]))
        total = near_ref[:, lanes].astype(F32) + a_ref[:, lanes].astype(F32)
        total = total + b_ref[:, lanes].astype(F32) + c_ref[:, lanes].astype(F32)
        target[:, lanes] = lax.dot_general(
            order_ref[...], total.astype(BF), TN, preferred_element_type=F32
        ).astype(BF)


def core_sum_kernel(near_ref, far_ref, out_ref):
    out_ref[...] = (near_ref[...].astype(F32) + far_ref[...].astype(F32)).astype(BF)


def branch_kernel(terms_ref, own_ref, grad_ref, gain_ref, full_ref, low_ref):
    grad = terms_ref[0:128, :].astype(F32)
    for part in range(1, 4):
        grad = grad + terms_ref[part * 128 : part * 128 + 128, :].astype(F32)
    rows = own_ref[...]
    inverse = lax.rsqrt(jnp.mean(rows * rows, axis=-1, keepdims=True) + EPS)
    scaled = rows * inverse
    grad = grad * gain_ref[1:2, :]
    grad = inverse * (grad - scaled * jnp.mean(grad * scaled, axis=-1, keepdims=True))
    grad = grad + grad_ref[...].astype(F32)
    full_ref[...] = grad
    low_ref[...] = grad.astype(BF)


def out_kernel(own_ref, a_ref, b_ref, c_ref, order_ref, out_ref):
    total = own_ref[...] + a_ref[...].astype(F32)
    total = total + b_ref[...].astype(F32) + c_ref[...].astype(F32)
    out_ref[...] = lax.dot_general(
        total.astype(BF), order_ref[...], NT, preferred_element_type=F32
    ).astype(BF)


def attn_grad_kernel(
    dq_ref, dkv_ref, cos_ref, sin_ref, normed_ref, weight_ref, x_ref, gain_ref, ffn_gain_ref,
    near_ref, far_ref, own_ref, pair_ref, grad_ref,
):
    cos_table, sin_table = cos_ref[...], sin_ref[...]

    def turn(block):
        return block * cos_table - swap_halves(block) * sin_table

    def summed(start):
        total = dkv_ref[0:256, start : start + 128].astype(F32)
        for part in range(1, 8):
            total = total + dkv_ref[part * 256 : part * 256 + 256, start : start + 128].astype(F32)
        return total

    for start in range(0, 512, 128):
        grad_ref[:, start : start + 128] = turn(dq_ref[:, start : start + 128]).astype(BF)
    tail = dq_ref[:, 512:576]
    wide = jnp.concatenate([tail, jnp.zeros_like(tail)], axis=1)
    grad_ref[:, 512:640] = turn(wide).astype(BF)
    grad_ref[:, 640:768] = turn(summed(0)).astype(BF)
    block = summed(128)
    lane = lax.broadcasted_iota(jnp.int32, block.shape, 1)
    grad_ref[:, 768:896] = jnp.where(lane < HEAD, turn(block), block).astype(BF)
    grad_ref[:, 896:1024] = summed(256).astype(BF)
    grads = lax.dot_general(grad_ref[...], weight_ref[...], NT, preferred_element_type=F32)
    own_ref[...] = grads[:128]
    pair_ref[...] = grads[128:].astype(BF)
    rows = x_ref[...]
    inverse = lax.rsqrt(jnp.mean(rows * rows, axis=-1, keepdims=True) + EPS)
    attn_terms = jnp.sum(grads * (rows * inverse), axis=0, keepdims=True)
    ffn_terms = jnp.sum(ffn_gain_ref[...], axis=0, keepdims=True)
    parts = []
    for terms in (attn_terms, ffn_terms):
        high = terms.astype(BF)
        parts.append(high.astype(F32))
        parts.append(terms - high.astype(F32))
    row = lax.broadcasted_iota(jnp.int32, (16, DIM), 0)
    gains = jnp.zeros((16, DIM), F32)
    for index, part in enumerate(parts):
        gains = jnp.where(row == index, part, gains)
    gains = gains.astype(BF)
    place_row = lax.broadcasted_iota(jnp.int32, (16, 128), 0)
    place_lane = lax.broadcasted_iota(jnp.int32, (16, 128), 1)
    places = ((place_lane == 64 + place_row // 2) & (place_row < 4)).astype(BF)

    def extra(start, block):
        columns = lax.dot_general(
            gains[:, start : start + 128], places, TN, preferred_element_type=F32
        )
        return jnp.concatenate([block[:, :512], block[:, 512:640] + columns, block[:, 640:]], axis=1)

    outer_products((normed_ref,), (grad_ref,), near_ref, far_ref, extra)


def token_kernel(own_ref, pair_ref, x_ref, gain_ref, full_ref, order_ref, out_ref):
    grad = own_ref[...] + pair_ref[...].astype(F32)
    rows = x_ref[0:128, :]
    inverse = lax.rsqrt(jnp.mean(rows * rows, axis=-1, keepdims=True) + EPS)
    scaled = rows * inverse
    grad = grad * gain_ref[0:1, :]
    grad = inverse * (grad - scaled * jnp.mean(grad * scaled, axis=-1, keepdims=True))
    total = (full_ref[...] + grad).astype(BF)
    out_ref[...] = lax.dot_general(
        total, order_ref[...], NT, preferred_element_type=F32
    ).astype(BF)


def finish_kernel(pieces_ref, gain_ref, q_ref, k_ref, v_ref, o_ref, gate_ref, up_ref, down_ref):
    for side in range(2):
        first = pieces_ref[side * 16 : side * 16 + 16, 0:1600].astype(F32)[:9]
        second = pieces_ref[side * 16 + 32 : side * 16 + 48, 0:1600].astype(F32)[:9]
        total = first + second
        q_ref[:, side * 576 : side * 576 + 576] = total[:, 0:576]
        k_ref[:, side * 192 : side * 192 + 192] = total[:, 640:832]
        v_ref[:, side * 192 : side * 192 + 192] = total[:, 832:1024]
        o_ref[:, side * 576 : side * 576 + 576] = total[:, 1024:1600]
        if side == 0:
            gain_ref[...] = total[:, 512:640]
        else:
            gain_ref[...] += total[:, 512:640]
    for part in range(4):
        rows = slice(part * 16, part * 16 + 16)
        lanes = slice(part * FF_PART, part * FF_PART + FF_PART)
        gate_ref[:, lanes] = pieces_ref[rows, 1664:2432].astype(F32)[:9]
        up_ref[:, lanes] = pieces_ref[rows, 2432:3200].astype(F32)[:9]
        down_ref[:, lanes] = pieces_ref[rows, 3200:3968].astype(F32)[:9]


VMEM = pl.BlockSpec(memory_space=pltpu.VMEM)
SMEM = pl.BlockSpec(memory_space=pltpu.SMEM)
HBM = pl.BlockSpec(memory_space=pltpu.HBM)


def takes(microseconds):
    return pl.CostEstimate(flops=int(microseconds * 6e8), bytes_accessed=1 << 20, transcendentals=0)


def shapes(*sizes):
    return tuple(jax.ShapeDtypeStruct(size[:-1], size[-1]) for size in sizes)


def kernel_call(kernel, ins, outs, scalars=0, scratch=(), micros=3, far=(), sems=0, far_out=False, room=6):
    specs = [SMEM if index < scalars else HBM if index in far else VMEM for index in range(len(ins))]
    scratch_shapes = [pltpu.VMEM(size[:-1], size[-1]) for size in scratch]
    if sems:
        scratch_shapes.append(pltpu.SemaphoreType.DMA((sems,)))
    return pl.pallas_call(
        kernel,
        out_shape=shapes(*outs),
        in_specs=specs,
        out_specs=(HBM if far_out else VMEM,) * len(outs),
        scratch_shapes=scratch_shapes,
        compiler_params=pltpu.CompilerParams(vmem_limit_bytes=room * 1024 * 1024),
        cost_estimate=takes(micros),
    )(*ins)


def pack(z, *weights):
    return kernel_call(
        pack_kernel,
        (z,) + weights,
        ((1024, QKV, BF),) + ((16, FFN, BF),) * 4,
        scalars=1,
        scratch=[weight.shape + (BF,) for weight in weights],
        far=range(1, 9),
        sems=8,
        room=60,
    )


def join(pieces):
    rows, width = pieces[0].shape
    return kernel_call(
        join_kernel,
        pieces,
        ((rows * len(pieces), width, BF),),
        far=range(len(pieces)),
        sems=len(pieces),
        far_out=True,
    )[0]


def feed_forward(*ins):
    return kernel_call(
        ffn_kernel,
        ins,
        (
            (512, DIM, BF),
            (128, DIM, F32),
            (128, DIM, BF),
            (128, DIM, BF),
            (128, DIM, BF),
            (128, DIM, F32),
            (128, DIM, BF),
            (512, FF_PART, BF),
            (512, FF_PART, BF),
            (512, FF_PART, BF),
            (512, DIM, BF),
            (DIM, HALF_Q, BF),
            (8, DIM, F32),
        ),
        scalars=1,
        scratch=(
            (DIM, FFN, BF),
            (512, DIM, BF),
            (512, DIM, BF),
            (512, DIM, F32),
            (512, DIM, F32),
            (512, DIM, F32),
            (512, 256, F32),
            (512, 256, F32),
            (512, 256, F32),
        ),
        far=range(5, 11),
        sems=6,
        micros=15,
        room=60,
    )


def project(*ins):
    return kernel_call(
        qkv_kernel,
        ins,
        (
            (256, DIM, F32),
            (256, DIM, BF),
            (256, HALF_Q, BF),
            (2048, KV, BF),
            (DIM, QKV, BF),
            (8, DIM, F32),
        ),
        scratch=((256, DIM, BF),),
        room=60,
    )


def attend(*ins):
    return kernel_call(
        attend_kernel,
        ins,
        ((256, HALF_Q, F32), (4, 3, 192, 128, F32), (4096, KV, BF), (1024, HALF_Q, BF)),
        scalars=3,
        scratch=((3, 16, 192, TILE, F32),),
        micros=20,
        room=16,
    )


def attend_back(*ins):
    return kernel_call(
        attend_back_kernel,
        ins,
        ((256, HALF_Q, F32), (2048, KV, BF), (2048, KV, BF)),
        scalars=2,
        scratch=((4096, KV, F32), (256, DIM, BF), (256, HALF_Q, BF)),
        micros=40,
        room=14,
    )


def pick(matrix, value):
    return jnp.dot(matrix, value, preferred_element_type=F32).astype(BF)


def send_turn(block, first):
    return [send(block, turn_by(step, first)) for step in (1, 3, 2)]


def scatter_turns(nears, fars):
    width = sum(near.shape[1] for near in nears)
    near, *rest = kernel_call(
        merge_kernel, tuple(nears) + tuple(fars), ((144, width, F32),) + ((144, width, BF),) * 3
    )
    rest = [send(part, turn_by(-step, False)) for part, step in zip(rest, (1, 3, 2))]
    return near, rest


def scatter_rows(groups, inner_order):
    near, *rest = kernel_call(
        spread_kernel, (inner_order, *groups), ((48, PIECES, BF),) * 4
    )
    return [near] + [send(part, turn_by(-step, True)) for part, step in zip(rest, (1, 3, 2))]


def rope_tables(positions):
    lane = jnp.arange(128, dtype=jnp.int32)
    inverse = 1.0 / 10000.0 ** ((lane % 32).astype(F32) * (2.0 / HEAD))
    angles = positions.astype(F32)[:, None] * inverse[None, :]
    sign = jnp.where(lane % HEAD < HEAD // 2, -1.0, 1.0)
    return (jnp.cos(angles), jnp.sin(angles) * sign[None, :])


def after(value, *others):
    return lax.optimization_barrier((value,) + others)[0]


def one_hot(rows, columns):
    return (rows == columns).astype(BF)


def body(
    tokens,
    grad_out,
    pair_order,
    attn_gain,
    query_weight,
    key_weight,
    value_weight,
    output_weight,
    ffn_gain,
    gate_weight,
    up_weight,
    down_weight,
):
    dp, ctx = lax.axis_index("dp"), lax.axis_index("ctx")
    l, c = dp // 2, dp % 2
    h, x, z = ctx // 16, (ctx // 4) % 4, ctx % 4
    y, b = 2 * h + l, z % 2
    even = b == 0

    local = jnp.arange(DIM, dtype=jnp.int32)
    from_c = (local // 576) ^ c
    turns = jnp.array([0, 1, 3, 2], jnp.int32)
    outer, inner = turns[(local // 144) % 4], turns[(local // 36) % 4]
    from_x = (x - jnp.where(from_c == 0, outer, inner)) % 4
    from_y = (y - jnp.where(from_c == 0, inner, outer)) % 4
    from_z = (local // 9) % 4
    owner = (2 * (from_y % 2) + from_c) * 32 + (4 * (from_y // 2) + from_x) * 4 + from_z
    natural = owner * 9 + local % 9
    order = one_hot(jnp.arange(DIM, dtype=jnp.int32)[:, None], natural[None, :])
    rows48 = jnp.arange(48, dtype=jnp.int32)
    z_order = one_hot(
        jnp.where(rows48 < 36, (rows48 // 9) * 16 + rows48 % 9, -1)[:, None],
        jnp.arange(64, dtype=jnp.int32)[None, :],
    )
    z_arrival = one_hot(
        jnp.where(rows48 < 36, ((z - rows48 // 9) % 4) * 16 + rows48 % 9, -1)[:, None],
        jnp.arange(64, dtype=jnp.int32)[None, :],
    )
    rows144 = jnp.arange(144, dtype=jnp.int32)
    inner_order = one_hot(
        ((rows144 // 36) * 48 + rows144 % 36)[:, None], jnp.arange(192, dtype=jnp.int32)[None, :]
    )
    chunk = jnp.arange(64, dtype=jnp.int32)
    chunk_ctx = (
        ((chunk // 4) % 8) * 4
        + 2 * ((chunk // 32) ^ c)
        + ((chunk // 2) % 2 ^ b)
    )
    ctx_match = chunk_ctx[:, None] == jnp.arange(32, dtype=jnp.int32)[None, :]
    chunk_pair = jnp.sum(jnp.where(ctx_match, pair_order[None, :], 0), axis=1)
    spot = jnp.where(chunk % 2 == 0, chunk_pair, 63 - chunk_pair)
    place = lax.dynamic_slice_in_dim(spot, (4 * h + x) * 4, 4)
    positions = (place[:, None] * 64 + jnp.arange(64, dtype=jnp.int32)[None, :]).reshape(256)
    cos_table, sin_table = rope_tables(positions)

    rows_own = send(tokens[0], home(0))
    rows_pair = send(tokens[0], home(1))

    z_own = jnp.reshape(z, (1,))
    attn_send, *ffn_send = pack(
        z_own,
        jnp.stack([attn_gain, ffn_gain], axis=1),
        query_weight,
        key_weight,
        value_weight,
        output_weight,
        gate_weight,
        up_weight,
        down_weight,
    )
    ffn_all = [ffn_send[0]] + [send(ffn_send[step], to_z(step)) for step in (1, 2, 3)]
    attn_all = lax.all_to_all(attn_send, ALL, 0, 0, tiled=True, axis_index_groups=CHIP_GROUPS)
    rows64 = jnp.arange(1024, dtype=jnp.int32)
    chip = rows64 // 16
    far_x, far_y = (x - chip // 16) % 4, (y - (chip // 4) % 4) % 4
    turn_x, turn_y = turns[far_x], turns[far_y]
    target = jnp.where(c == 0, turn_x * 4 + turn_y, turn_y * 4 + turn_x) * 36 + (chip % 4) * 9
    target = jnp.where(rows64 % 16 < 9, target + rows64 % 16, -1)
    chip_order = one_hot(jnp.arange(576, dtype=jnp.int32)[:, None], target[None, :])
    attn_half = pick(chip_order, after(attn_all, order, cos_table, sin_table, rows_own, rows_pair, *ffn_all))
    ffn_half = after(pick(z_arrival, jnp.concatenate(ffn_all, axis=0)), attn_all)
    ffn_half = [ffn_half] + send_turn(ffn_half, True)
    rows_both = after(jnp.concatenate([tokens[0], grad_out[0]], axis=1), attn_all)
    rows_both = [send(rows_both, home(flip)) for flip in (2, 3)]

    inputs, normed_a, queries, kv_send, qkv_weight, gains = project(
        rows_own,
        rows_pair,
        order,
        attn_half,
        send(attn_half, other_core),
        cos_table,
        sin_table,
    )
    kv = exchange(kv_send, HX_GROUPS)
    kv = after(kv, *ffn_half, *rows_both)
    ffn_half = pick(inner_order, jnp.concatenate(ffn_half, axis=0))
    ffn_near = [ffn_half] + send_turn(ffn_half, False)
    grad_rows = after(grad_out[0], kv)
    grad_rows = [send(grad_rows, home(flip)) for flip in (0, 1)]
    heads_out, logs, kv_sorted, heads_send = attend(
        spot, place, jnp.reshape(b, (1,)), queries, kv, send(kv, other_core)
    )
    heads_low = heads_out.astype(BF)
    heads_all = exchange(after(heads_send, *grad_rows), Z_GROUPS)
    ffn_near = [after(piece, heads_send) for piece in ffn_near]
    ffn_far = [send(ffn_near[0], other_core), send(join(ffn_near[1:]), other_core)]

    ffn_rows, grad_local = kernel_call(
        rows_kernel,
        (z_own, rows_own, rows_pair, *rows_both, *grad_rows, after(order, heads_send)),
        ((512, DIM, BF), (512, 2 * DIM, BF)),
        scalars=1,
        micros=8,
    )

    (
        normed_grad,
        out_own,
        *out_terms,
        hidden_own,
        grad_own,
        hidden,
        dgate,
        dup,
        normed_f,
        output_part,
        ffn_gain_terms,
    ) = feed_forward(
        z_own, ffn_rows, grad_local, heads_all, gains, *ffn_near, *ffn_far
    )
    normed_grad = exchange(normed_grad, Z_GROUPS)
    ffn_near, ffn_far = kernel_call(
        ffn_grad_kernel,
        (normed_f, grad_local, hidden, dgate, dup),
        ((576, 2304, BF), (576, 2304, BF)),
        micros=6,
    )
    grad_hidden_one, grad_branch = kernel_call(
        branch_kernel, (normed_grad, hidden_own, grad_own, gains), ((128, DIM, F32), (128, DIM, BF))
    )
    grad_pair = send(grad_branch, z_pair)
    ffn_far = send(after(ffn_far, grad_branch), other_core)
    ffn_near, ffn_rest = scatter_turns([ffn_near], [ffn_far])

    output_near, output_far = kernel_call(
        output_grad_kernel,
        (grad_branch, grad_pair, heads_low),
        ((576, HALF_Q, BF), (576, HALF_Q, BF)),
        scratch=((256, DIM, BF),),
    )
    output_far = send(output_far, other_core)
    dq, dkv, dkv_far = attend_back(
        spot, place, queries, kv_sorted, heads_out, logs, after(grad_branch, ffn_near), grad_pair, output_part
    )
    out_terms = [after(terms, dq) for terms in out_terms]
    out_terms = [send(terms, to_z(step)) for step, terms in enumerate(out_terms, 1)]
    dkv = kernel_call(core_sum_kernel, (dkv, send(after(dkv_far, *ffn_rest), other_core)), ((2048, KV, BF),))[0]
    dkv = exchange(dkv, HX_GROUPS)
    block_out = kernel_call(out_kernel, (out_own, *out_terms, order), ((128, DIM, BF),))[0]
    block_out = send(block_out, home(0))
    attn_near, attn_far, grad_own, grad_pair = kernel_call(
        attn_grad_kernel,
        (after(dq, *out_terms), dkv, cos_table, sin_table, normed_a, qkv_weight, inputs, gains, ffn_gain_terms),
        ((576, QKV, BF), (576, QKV, BF), (128, DIM, F32), (128, DIM, BF)),
        scratch=((256, QKV, BF),),
    )
    attn_far = send(attn_far, other_core)
    grad_pair = send(grad_pair, z_pair)
    attn_near, attn_rest = scatter_turns([attn_near, output_near], [attn_far, output_far])
    grad_inputs = kernel_call(
        token_kernel,
        (grad_own, grad_pair, inputs, gains, grad_hidden_one, order),
        ((128, DIM, BF),),
    )[0]
    grad_inputs = send(grad_inputs, home(0))
    parts = scatter_rows((attn_near, *attn_rest, ffn_near, *ffn_rest), inner_order)

    pieces = kernel_call(split_kernel, (z_order, *parts), ((64, PIECES, BF),))[0]
    pieces = exchange(pieces, Z_GROUPS)
    gain_grads, *weight_grads = kernel_call(
        finish_kernel,
        (pieces,),
        ((9, 128, F32), (9, DIM, F32), (9, KV, F32), (9, KV, F32), (9, DIM, F32)) + ((9, 3072, F32),) * 3,
    )

    return (
        block_out[None],
        grad_inputs[None],
        gain_grads[:, 64],
        *weight_grads[:4],
        gain_grads[:, 65],
        *weight_grads[4:],
    )


def solution(mesh):
    weights = P(ALL, None)
    rows = P("dp", "ctx", None)
    return jax.shard_map(
        body,
        mesh=mesh,
        in_specs=(rows, rows, P(), P(ALL), weights, weights, weights, weights, P(ALL), weights, weights, weights),
        out_specs=(rows, rows, P(ALL), weights, weights, weights, weights, P(ALL), weights, weights, weights),
        check_vma=False,
    )
```

```python
import functools
import itertools

import jax
import jax.numpy as jnp
from jax import lax
from jax.experimental import pallas as pl
from jax.experimental.pallas import tpu as pltpu
from jax.sharding import PartitionSpec as P

ALL = ("dp", "ctx")
EPS = 1e-05
DIM = 1152
HEAD = 64
HALF_Q = 576
KV = 384
QKV = 1024
FF_PART = 768
FFN = 3456
PIECES = 3968
TILE = 256
BF = jnp.bfloat16
F32 = jnp.float32


def flat(l, c, h, x, z):
    return (2 * l + c) * 32 + (4 * h + x) * 4 + z


def moves(target):
    places = itertools.product(range(2), range(2), range(2), range(4), range(4))
    return [(flat(*place), flat(*target(*place))) for place in places]


def send(value, target):
    return lax.ppermute(value, ALL, moves(target))


def to_z(step):
    return lambda l, c, h, x, z: (l, c, h, x, (z + step) % 4)


def turn_by(step, first):
    def target(l, c, h, x, z):
        y = 2 * h + l
        if (c == 0) == first:
            y = (y + step) % 4
        else:
            x = (x + step) % 4
        return (y % 2, c, y // 2, x, z)

    return target


def other_core(l, c, h, x, z):
    return (l, 1 - c, h, x, z)


def z_pair(l, c, h, x, z):
    return (l, c, h, x, z ^ 1)


def home(flip):
    return lambda l, c, h, x, z: (l, z // 2, h, x, (2 * c + z % 2) ^ flip)


Z_GROUPS = [[ring * 4 + z for z in range(4)] for ring in range(8)]
CHIP_GROUPS = [
    [flat(y % 2, c, y // 2, x, z) for x in range(4) for y in range(4) for z in range(4)] for c in range(2)
]
HX_GROUPS = [[place * 4 + z for place in range(8)] for z in range(4)]


def exchange(parts, groups):
    return lax.all_to_all(parts, "ctx", 0, 0, tiled=True, axis_index_groups=groups)


def swap_halves(block):
    lane = lax.broadcasted_iota(jnp.int32, block.shape, 1) % HEAD
    return jnp.where(
        lane < HEAD // 2, pltpu.roll(block, 128 - HEAD // 2, 1), pltpu.roll(block, HEAD // 2, 1)
    )


def fill(ref, row, lane, value):
    ref[row : row + value.shape[0], lane : lane + value.shape[1]] = value


def pack_kernel(z_ref, *refs):
    arrived, sems = refs[13:21], refs[21]
    copies = [
        pltpu.make_async_copy(here, there, sems.at[index])
        for index, (here, there) in enumerate(zip(refs[:8], arrived))
    ]
    for copy in copies:
        copy.start()
    for copy in copies:
        copy.wait()
    gain_ref, q_ref, k_ref, v_ref, o_ref, gate_ref, up_ref, down_ref = arrived
    attn_ref, wide_ref = refs[8], refs[22]
    wide_ref[...] = jnp.zeros(wide_ref.shape, BF)
    for side in range(2):
        row = side * 16
        fill(wide_ref, row, 0, q_ref[:, side * 576 : side * 576 + 576])
        fill(wide_ref, row, 576, gain_ref[...])
        fill(wide_ref, row, 640, k_ref[:, side * 192 : side * 192 + 192])
        fill(wide_ref, row, 832, v_ref[:, side * 192 : side * 192 + 192])
    chunks = []
    for side in range(2):
        rows = wide_ref[side * 16 : side * 16 + 16, :].astype(F32)
        last = jnp.concatenate([rows[8:9, part * 128 : part * 128 + 128] for part in range(8)], axis=0)
        chunks.append(jnp.concatenate([rows[:8], last], axis=1))
    both = jnp.concatenate(chunks, axis=0).astype(BF)

    def copy_both(index, carry):
        attn_ref[pl.ds(pl.multiple_of(index * 16, 16), 16), :] = both
        return carry

    lax.fori_loop(0, 32, copy_both, 0)
    for step in range(4):
        ffn_ref = refs[9 + step]
        ffn_ref[...] = jnp.zeros((16, FFN), BF)
        start = pl.multiple_of(((z_ref[0] + step) % 4) * FF_PART, FF_PART)
        fill(ffn_ref, 0, 0, gate_ref[:, pl.ds(start, FF_PART)])
        fill(ffn_ref, 0, 768, up_ref[:, pl.ds(start, FF_PART)])
        fill(ffn_ref, 0, 1536, down_ref[:, pl.ds(start, FF_PART)])
        fill(ffn_ref, 0, 2304, o_ref[...])


def unpack_kernel(all_ref, order_ref, last_order_ref, out_ref, tail_ref):
    tail_ref[...] = all_ref[:, QKV:].astype(F32)
    last = jnp.concatenate([tail_ref[pl.ds(part, 64, stride=8), :] for part in range(8)], axis=1)
    out_ref[...] = (
        jnp.dot(order_ref[...], all_ref[:, :QKV], preferred_element_type=F32)
        + jnp.dot(last_order_ref[...], last.astype(BF), preferred_element_type=F32)
    ).astype(BF)


def qkv_kernel(
    own_ref, pair_ref, half_ref, other_ref, cos_ref, sin_ref,
    x_ref, normed_ref, q_ref, kv_ref, gain_ref, weight_ref,
):
    x_ref[0:128, :] = own_ref[:, 0:DIM]
    x_ref[128:256, :] = pair_ref[:, 0:DIM]
    weight_ref[0:576, :] = half_ref[...]
    weight_ref[576:1152, :] = other_ref[...]
    inputs = x_ref[...].astype(F32)
    lane = lax.broadcasted_iota(jnp.int32, (8, 128), 1)
    row = lax.broadcasted_iota(jnp.int32, (8, 128), 0)
    gains = lax.dot_general(
        (lane == row + 64).astype(BF), weight_ref[:, 512:640], NT, preferred_element_type=F32
    )
    gain_ref[...] = gains
    inverse = lax.rsqrt(jnp.mean(inputs * inputs, axis=-1, keepdims=True) + EPS)
    normed = (inputs * inverse * gains[0:1]).astype(BF)
    normed_ref[...] = normed
    proj = jnp.dot(normed, weight_ref[...], preferred_element_type=F32)
    cos_table, sin_table = cos_ref[...], sin_ref[...]
    kv_parts = []
    for start in range(0, QKV, 128):
        block = proj[:, start : start + 128]
        turned = block * cos_table + swap_halves(block) * sin_table
        if start < 512:
            q_ref[:, start : start + 128] = (turned * 0.125).astype(BF)
        elif start == 512:
            q_ref[:, 512:576] = (turned[:, :64] * 0.125).astype(BF)
        elif start == 640:
            kv_parts.append(turned.astype(BF))
        elif start == 768:
            side = lax.broadcasted_iota(jnp.int32, block.shape, 1)
            kv_parts.append(jnp.where(side < HEAD, turned, block).astype(BF))
        else:
            kv_parts.append(block.astype(BF))
    for copy in range(8):
        for part in range(3):
            fill(kv_ref, copy * 256, part * 128, kv_parts[part])


def stack_heads(block, kv_head, upper):
    parts = []
    for group in range(3):
        start = (kv_head * 3 + group) * HEAD
        parts.append(block[:, start : start + HEAD])
    rows = jnp.concatenate(parts, axis=0)
    zeros = jnp.zeros_like(rows)
    return jnp.concatenate([zeros, rows] if upper else [rows, zeros], axis=1)


K_GROUP = (0, 0, 128)
K_UPPER = (False, True, False)
V_GROUP = (128, 256, 256)
V_UPPER = (True, False, True)
NT = (((1,), (1,)), ((), ()))
TN = (((0,), (0,)), ((), ()))


def mask_rows(scores, place, tile):
    row = lax.broadcasted_iota(jnp.int32, scores.shape, 0) % 64 + place * 64
    key = lax.broadcasted_iota(jnp.int32, scores.shape, 1) + tile * TILE
    return jnp.where(key <= row, scores, -1e30)


def over_tiles(rank_ref, step, carry):
    first = jnp.int32(0)
    for count in (4, 3, 2, 1):
        last = rank_ref[count - 1] // 4
        carry = lax.fori_loop(first, last, functools.partial(step, count=count, masked=False), carry)
        carry = lax.cond(
            first <= last,
            functools.partial(step, last, count=count, masked=True),
            lambda value: value,
            carry,
        )
        first = last + 1
    return carry


def stack_blocks(rank_ref, ref, target_ref, uppers):
    for rank in range(4):
        rows = ref[pl.ds(pl.multiple_of(rank_ref[4 + rank] * 64, 64), 64), :]
        for head in range(3):
            target_ref[head, rank * 192 : rank * 192 + 192, :] = stack_heads(rows, head, uppers[head])


def attend_kernel(
    spot_ref, rank_ref, side_ref, q_ref, near_ref, far_ref,
    out_ref, log_ref, sorted_ref, low_ref, score_ref, stack_ref, top_ref, sum_ref, total_ref,
):
    def put(index, carry):
        here = pl.ds(pl.multiple_of(index * 64, 64), 64)
        sorted_ref[pl.ds(pl.multiple_of(spot_ref[index] * 64, 64), 64), :] = near_ref[here, :]
        sorted_ref[pl.ds(pl.multiple_of(spot_ref[index + 32] * 64, 64), 64), :] = far_ref[here, :]
        return carry

    lax.fori_loop(0, 32, put, 0)
    stack_blocks(rank_ref, q_ref, stack_ref, K_UPPER)
    top_ref[...] = jnp.full(top_ref.shape, -1e30, F32)

    def score(tile, base, count, masked):
        span = pl.ds(pl.multiple_of(tile * TILE, TILE), TILE)
        for head in range(3):
            keys = sorted_ref[span, K_GROUP[head] : K_GROUP[head] + 128]
            for rank in range(count):
                rows = slice(rank * 192, rank * 192 + 192)
                scores = lax.dot_general(
                    stack_ref[head, rows, :], keys, NT, preferred_element_type=F32
                )
                if masked:
                    scores = mask_rows(scores, rank_ref[rank], tile)
                score_ref[head, base + rank] = scores
                top_ref[head, rows, :] = jnp.maximum(
                    top_ref[head, rows, :], jnp.maximum(scores[:, :128], scores[:, 128:])
                )
        return base + count

    over_tiles(rank_ref, score, jnp.int32(0))
    for head in range(3):
        top_ref[head] = jnp.broadcast_to(jnp.max(top_ref[head], axis=1, keepdims=True), (768, 128))
    sum_ref[...] = jnp.zeros(sum_ref.shape, F32)
    total_ref[...] = jnp.zeros(total_ref.shape, F32)

    def weigh(tile, base, count, masked):
        span = pl.ds(pl.multiple_of(tile * TILE, TILE), TILE)
        for head in range(3):
            values = sorted_ref[span, V_GROUP[head] : V_GROUP[head] + 128]
            for rank in range(count):
                rows = slice(rank * 192, rank * 192 + 192)
                scores = score_ref[head, base + rank]
                top = top_ref[head, rows, :]
                left = jnp.exp(scores[:, :128] - top)
                right = jnp.exp(scores[:, 128:] - top)
                total_ref[head, rows, :] += left + right
                weights = jnp.concatenate([left.astype(BF), right.astype(BF)], axis=1)
                sum_ref[head, rows, :] += jnp.dot(weights, values, preferred_element_type=F32)
        return base + count

    over_tiles(rank_ref, weigh, jnp.int32(0))
    for head in range(3):
        row_total = jnp.sum(total_ref[head], axis=1, keepdims=True)
        log_ref[head] = top_ref[head] + jnp.log(row_total)
        result = sum_ref[head] / row_total
        side = result[:, 64:] if V_UPPER[head] else result[:, :64]
        for rank in range(4):
            rows = pl.ds(pl.multiple_of(rank_ref[4 + rank] * 64, 64), 64)
            for group in range(3):
                start = (head * 3 + group) * HEAD
                row = rank * 192 + group * 64
                out_ref[rows, start : start + HEAD] = side[row : row + 64]
    side = side_ref[0]
    for copy in range(4):
        for block in range(2):
            start = pl.multiple_of(copy * 256 + (block ^ side) * 128, 128)
            low_ref[pl.ds(start, 128), 0:576] = out_ref[block * 128 : block * 128 + 128, :].astype(BF)
            low_ref[pl.ds(start, 128), 576:640] = jnp.zeros((128, 64), BF)


def attend_back_kernel(
    spot_ref, rank_ref, q_ref, sorted_ref, out_ref, log_ref, own_ref, pair_ref, part_ref,
    dq_ref, near_ref, far_ref,
    total_ref, rows_ref, grad_ref, stack_ref, grads_ref, delta_ref, prob_ref, dscore_ref, dq_sum_ref,
):
    rows_ref[0:128, :] = own_ref[...]
    rows_ref[128:256, :] = pair_ref[...]
    grad_ref[...] = jnp.dot(rows_ref[...], part_ref[...], preferred_element_type=F32).astype(BF)
    total_ref[...] = jnp.zeros_like(total_ref)
    dq_sum_ref[...] = jnp.zeros_like(dq_sum_ref)
    stack_blocks(rank_ref, q_ref, stack_ref, K_UPPER)
    stack_blocks(rank_ref, grad_ref, grads_ref, V_UPPER)
    for rank in range(4):
        rows = pl.ds(pl.multiple_of(rank_ref[4 + rank] * 64, 64), 64)
        products = grad_ref[rows, :].astype(F32) * out_ref[rows, :]
        for head in range(3):
            delta_ref[head, rank * 192 : rank * 192 + 192, :] = jnp.broadcast_to(
                jnp.sum(stack_heads(products, head, False), axis=1, keepdims=True), (192, 128)
            )

    def step(tile, carry, count, masked):
        span = pl.ds(pl.multiple_of(tile * TILE, TILE), TILE)
        size = count * 192
        for head in range(3):
            k_lanes = slice(K_GROUP[head], K_GROUP[head] + 128)
            v_lanes = slice(V_GROUP[head], V_GROUP[head] + 128)
            keys, values = sorted_ref[span, k_lanes], sorted_ref[span, v_lanes]
            scores_all = lax.dot_general(stack_ref[head, :size, :], keys, NT, preferred_element_type=F32)
            grad_all = lax.dot_general(grads_ref[head, :size, :], values, NT, preferred_element_type=F32)
            for rank in range(count):
                rows = slice(rank * 192, rank * 192 + 192)
                scores = scores_all[rows]
                if masked:
                    scores = mask_rows(scores, rank_ref[rank], tile)
                logs, delta = log_ref[head, rows, :], delta_ref[head, rows, :]
                for lane in (0, 128):
                    lanes = slice(lane, lane + 128)
                    prob = jnp.exp(scores[:, lanes] - logs)
                    prob_ref[head, rows, lanes] = prob.astype(BF)
                    dscore_ref[head, rows, lanes] = (prob * (grad_all[rows, lanes] - delta)).astype(BF)
        for head in range(3):
            k_lanes = slice(K_GROUP[head], K_GROUP[head] + 128)
            v_lanes = slice(V_GROUP[head], V_GROUP[head] + 128)
            keys = sorted_ref[span, k_lanes]
            dq_sum_ref[head, :size, :] += jnp.dot(
                dscore_ref[head, :size, :], keys, preferred_element_type=F32
            )
            total_ref[span, v_lanes] += lax.dot_general(
                prob_ref[head, :size, :], grads_ref[head, :size, :], TN, preferred_element_type=F32
            )
            total_ref[span, k_lanes] += lax.dot_general(
                dscore_ref[head, :size, :], stack_ref[head, :size, :], TN, preferred_element_type=F32
            )
        return carry

    over_tiles(rank_ref, step, jnp.int32(0))
    for head in range(3):
        for rank in range(4):
            rows = pl.ds(pl.multiple_of(rank_ref[4 + rank] * 64, 64), 64)
            for group in range(3):
                start = (head * 3 + group) * HEAD
                row = rank * 192 + group * 64
                block = dq_sum_ref[head, row : row + 64, :] * 0.125
                side = block[:, 64:] if K_UPPER[head] else block[:, :64]
                dq_ref[rows, start : start + HEAD] = side

    def put(index, carry):
        there = pl.ds(pl.multiple_of(index * 64, 64), 64)
        origin = pl.ds(pl.multiple_of(spot_ref[index] * 64, 64), 64)
        near_ref[there, :] = total_ref[origin, :].astype(BF)
        origin = pl.ds(pl.multiple_of(spot_ref[index + 32] * 64, 64), 64)
        far_ref[there, :] = total_ref[origin, :].astype(BF)
        return carry

    lax.fori_loop(0, 32, put, 0)


def rows_kernel(x_ref, grad_ref, order_ref, out_ref):
    for side, rows_ref in enumerate((x_ref, grad_ref)):
        out_ref[:, side * DIM : side * DIM + DIM] = jnp.dot(
            rows_ref[...], order_ref[...], preferred_element_type=F32
        ).astype(BF)


def ffn_kernel(
    z_ref, rows0_ref, rows1_ref, rows2_ref, rows3_ref, heads_ref, gain_ref,
    w0_ref, w1_ref, w2_ref, w3_ref, w4_ref, w5_ref, w6_ref, w7_ref,
    dn_ref, out0_ref, out1_ref, out2_ref, out3_ref, own_ref, grad_own_ref, grad_ref, hidden_ref, dgate_ref, dup_ref, normed_ref, part_ref, gain_grad_ref,
    w_ref, scaled_ref, heads_all_ref, h1_ref, dn_sum_ref, out_sum_ref, gate_ref, up_ref, dh_ref, sems,
):
    pieces = (w0_ref, w1_ref, w2_ref, w3_ref, w4_ref, w5_ref, w6_ref, w7_ref)
    copies = [
        pltpu.make_async_copy(piece, w_ref.at[pl.ds(index * 144, 144)], sems.at[index])
        for index, piece in enumerate(pieces)
    ]
    for copy in copies:
        copy.start()
    z = z_ref[0]
    for slot, rows_ref in enumerate((rows0_ref, rows1_ref, rows2_ref, rows3_ref)):
        here = pl.ds(pl.multiple_of((z ^ slot) * 128, 128), 128)
        h1_ref[here, :] = rows_ref[:, 0:DIM].astype(F32)
        grad_ref[here, :] = rows_ref[:, DIM:]
    for side in range(2):
        for half in range(2):
            start = (2 * side + half) * 256
            heads_all_ref[side * 256 : side * 256 + 256, half * 576 : half * 576 + 576] = heads_ref[
                start : start + 256, 0:576
            ]
    for copy in copies:
        copy.wait()
    heads = heads_all_ref[...]
    for start in range(0, DIM, 384):
        h1_ref[:, start : start + 384] += lax.dot_general(
            heads, w_ref[start : start + 384, 2304:3456], NT, preferred_element_type=F32
        )

    def norm(index, carry):
        here = pl.ds(pl.multiple_of(index * 64, 64), 64)
        rows = h1_ref[here, :]
        inverse = lax.rsqrt(jnp.mean(rows * rows, axis=-1, keepdims=True) + EPS)
        scaled = rows * inverse
        scaled_ref[here, :] = scaled.astype(BF)
        normed_ref[here, :] = (scaled * gain_ref[1:2, :]).astype(BF)
        return carry

    lax.fori_loop(0, 8, norm, 0)
    here = pl.ds(pl.multiple_of(z * 128, 128), 128)
    own_ref[...] = h1_ref[here, :]
    grad_own_ref[...] = grad_ref[here, :]
    normed, grads = normed_ref[...], grad_ref[...]

    def units(index, carry):
        start = pl.multiple_of(index * 256, 256)
        w_gate = w_ref[:, pl.ds(start, 256)]
        w_up = w_ref[:, pl.ds(start + 768, 256)]
        w_down = w_ref[:, pl.ds(start + 1536, 256)]
        gate_ref[...] = jnp.dot(normed, w_gate, preferred_element_type=F32)
        up_ref[...] = jnp.dot(normed, w_up, preferred_element_type=F32)
        dh_ref[...] = jnp.dot(grads, w_down, preferred_element_type=F32)

        def act(block, carry):
            here = pl.ds(pl.multiple_of(block * 64, 64), 64)
            there = pl.ds(start, 256)
            gate, up, grad = gate_ref[here, :], up_ref[here, :], dh_ref[here, :]
            sigmoid = jax.nn.sigmoid(gate)
            active = gate * sigmoid
            hidden_ref[here, there] = (active * up).astype(BF)
            dgate_ref[here, there] = (grad * up * sigmoid * (1.0 + gate * (1.0 - sigmoid))).astype(BF)
            dup_ref[here, there] = (grad * active).astype(BF)
            return carry

        lax.fori_loop(0, 8, act, 0)
        return carry

    lax.fori_loop(0, 3, units, 0)
    hidden, dgate, dup = hidden_ref[...], dgate_ref[...], dup_ref[...]
    for first in range(0, DIM, 384):
        rows = slice(first, first + 384)
        dn_sum_ref[:, rows] = lax.dot_general(
            dgate, w_ref[rows, 0:768], NT, preferred_element_type=F32
        ) + lax.dot_general(dup, w_ref[rows, 768:1536], NT, preferred_element_type=F32)
        out_sum_ref[:, rows] = lax.dot_general(
            hidden, w_ref[rows, 1536:2304], NT, preferred_element_type=F32
        )

    def finish(index, total):
        here = pl.ds(pl.multiple_of(index * 64, 64), 64)
        grad = dn_sum_ref[here, :]
        dn_ref[here, :] = grad.astype(BF)
        terms = grad * scaled_ref[here, :].astype(F32)
        return total + jnp.sum(terms.reshape(8, 8, DIM), axis=0)

    gain_grad_ref[...] = lax.fori_loop(0, 8, finish, jnp.zeros((8, DIM), F32))

    out0_ref[...] = own_ref[...] + out_sum_ref[here, :]
    for step, out_ref in enumerate((out1_ref, out2_ref, out3_ref)):
        there = pl.ds(pl.multiple_of(((z + step + 1) % 4) * 128, 128), 128)
        out_ref[...] = out_sum_ref[there, :].astype(BF)

    @pl.when(z % 2 == 0)
    def _():
        part_ref[...] = w_ref[:, 2304:2880]

    @pl.when(z % 2 == 1)
    def _():
        part_ref[...] = w_ref[:, 2880:3456]


def outer_products(lefts, rights, near_ref, far_ref, extra=None):
    for start in range(0, DIM, 128):
        lane = 0
        for left, right in zip(lefts, rights):
            block = lax.dot_general(
                left[:, start : start + 128], right[...], TN, preferred_element_type=F32
            )
            if extra is not None:
                block = extra(start, block)
            block = block.astype(near_ref.dtype)
            width = block.shape[1]
            lanes = slice(lane, lane + width)
            if start < 512:
                near_ref[start : start + 128, lanes] = block
            elif start == 512:
                near_ref[512:576, lanes] = block[:64]
                far_ref[0:64, lanes] = block[64:].astype(BF)
            else:
                far_ref[start - 576 : start - 448, lanes] = block.astype(BF)
            lane += width


def ffn_grad_kernel(normed_ref, grad_ref, hidden_ref, dgate_ref, dup_ref, near_ref, far_ref):
    outer_products(
        (normed_ref, normed_ref, grad_ref), (dgate_ref, dup_ref, hidden_ref), near_ref, far_ref
    )


def output_grad_kernel(own_ref, pair_ref, heads_ref, near_ref, far_ref, rows_ref):
    rows_ref[0:128, :] = own_ref[...]
    rows_ref[128:256, :] = pair_ref[...]
    outer_products((rows_ref,), (heads_ref,), near_ref, far_ref)


def merge_kernel(*refs):
    count = len(refs) // 2 - 2
    targets = refs[2 * count :]
    for index in range(4):
        lane = 0
        for near_ref, far_ref in zip(refs[:count], refs[count : 2 * count]):
            width = near_ref.shape[1]
            rows = slice(index * 144, index * 144 + 144)
            total = near_ref[rows, :].astype(F32) + far_ref[rows, :].astype(F32)
            targets[index][:, lane : lane + width] = total.astype(targets[index].dtype)
            lane += width


def spread_kernel(order_ref, *refs):
    targets = refs[-4:]
    first = 0
    for group in range(2):
        near_ref, *others = refs[4 * group : 4 * group + 4]
        count = near_ref.shape[1]
        for start in range(0, count, 512):
            lanes = slice(start, min(start + 512, count))
            total = near_ref[:, lanes]
            for other_ref in others:
                total = total + other_ref[:, lanes].astype(F32)
            parts = lax.dot_general(order_ref[...], total.astype(BF), TN, preferred_element_type=F32)
            there = slice(first + lanes.start, first + lanes.stop)
            for index in range(4):
                targets[index][:, there] = parts[index * 40 : index * 40 + 40].astype(BF)
        first += count
        if first % 128:
            for target in targets:
                target[:, first : first + 64] = jnp.zeros((40, 64), BF)
            first += 64


def split_kernel(order_ref, near_ref, a_ref, b_ref, c_ref, target):
    for start in range(0, target.shape[1], 512):
        lanes = slice(start, min(start + 512, target.shape[1]))
        total = near_ref[:, lanes].astype(F32) + a_ref[:, lanes].astype(F32)
        total = total + b_ref[:, lanes].astype(F32) + c_ref[:, lanes].astype(F32)
        target[:, lanes] = lax.dot_general(
            order_ref[...], total.astype(BF), TN, preferred_element_type=F32
        ).astype(BF)


def core_sum_kernel(near_ref, far_ref, out_ref):
    out_ref[...] = (near_ref[...].astype(F32) + far_ref[...].astype(F32)).astype(BF)


def branch_kernel(terms_ref, own_ref, grad_ref, gain_ref, full_ref, low_ref):
    grad = terms_ref[0:128, :].astype(F32)
    for part in range(1, 4):
        grad = grad + terms_ref[part * 128 : part * 128 + 128, :].astype(F32)
    rows = own_ref[...]
    inverse = lax.rsqrt(jnp.mean(rows * rows, axis=-1, keepdims=True) + EPS)
    scaled = rows * inverse
    grad = grad * gain_ref[1:2, :]
    grad = inverse * (grad - scaled * jnp.mean(grad * scaled, axis=-1, keepdims=True))
    grad = grad + grad_ref[...].astype(F32)
    full_ref[...] = grad
    low_ref[...] = grad.astype(BF)


def out_kernel(own_ref, a_ref, b_ref, c_ref, out_ref):
    total = own_ref[...] + a_ref[...].astype(F32)
    out_ref[...] = (total + b_ref[...].astype(F32) + c_ref[...].astype(F32)).astype(BF)


def attn_grad_kernel(
    dq_ref, dkv_ref, cos_ref, sin_ref, normed_ref, half_ref, other_ref, x_ref, gain_ref, ffn_gain_ref,
    near_ref, far_ref, own_ref, pair_ref, grad_ref, weight_ref,
):
    weight_ref[0:576, :] = half_ref[...]
    weight_ref[576:1152, :] = other_ref[...]
    cos_table, sin_table = cos_ref[...], sin_ref[...]

    def turn(block):
        return block * cos_table - swap_halves(block) * sin_table

    def summed(start):
        total = dkv_ref[0:256, start : start + 128].astype(F32)
        for part in range(1, 8):
            total = total + dkv_ref[part * 256 : part * 256 + 256, start : start + 128].astype(F32)
        return total

    for start in range(0, 512, 128):
        grad_ref[:, start : start + 128] = turn(dq_ref[:, start : start + 128]).astype(BF)
    tail = dq_ref[:, 512:576]
    wide = jnp.concatenate([tail, jnp.zeros_like(tail)], axis=1)
    grad_ref[:, 512:640] = turn(wide).astype(BF)
    grad_ref[:, 640:768] = turn(summed(0)).astype(BF)
    block = summed(128)
    lane = lax.broadcasted_iota(jnp.int32, block.shape, 1)
    grad_ref[:, 768:896] = jnp.where(lane < HEAD, turn(block), block).astype(BF)
    grad_ref[:, 896:1024] = summed(256).astype(BF)
    grads = lax.dot_general(grad_ref[...], weight_ref[...], NT, preferred_element_type=F32)
    own_ref[...] = grads[:128]
    pair_ref[...] = grads[128:].astype(BF)
    rows = x_ref[...].astype(F32)
    inverse = lax.rsqrt(jnp.mean(rows * rows, axis=-1, keepdims=True) + EPS)
    attn_terms = jnp.sum(grads * (rows * inverse), axis=0, keepdims=True)
    ffn_terms = jnp.sum(ffn_gain_ref[...], axis=0, keepdims=True)
    parts = []
    for terms in (attn_terms, ffn_terms):
        high = terms.astype(BF)
        parts.append(high.astype(F32))
        parts.append(terms - high.astype(F32))
    row = lax.broadcasted_iota(jnp.int32, (16, DIM), 0)
    gains = jnp.zeros((16, DIM), F32)
    for index, part in enumerate(parts):
        gains = jnp.where(row == index, part, gains)
    gains = gains.astype(BF)
    place_row = lax.broadcasted_iota(jnp.int32, (16, 128), 0)
    place_lane = lax.broadcasted_iota(jnp.int32, (16, 128), 1)
    places = ((place_lane == 64 + place_row // 2) & (place_row < 4)).astype(BF)

    def extra(start, block):
        columns = lax.dot_general(
            gains[:, start : start + 128], places, TN, preferred_element_type=F32
        )
        return jnp.concatenate([block[:, :512], block[:, 512:640] + columns, block[:, 640:]], axis=1)

    outer_products((normed_ref,), (grad_ref,), near_ref, far_ref, extra)


def token_kernel(own_ref, pair_ref, x_ref, gain_ref, full_ref, out_ref):
    grad = own_ref[...] + pair_ref[...].astype(F32)
    rows = x_ref[0:128, :].astype(F32)
    inverse = lax.rsqrt(jnp.mean(rows * rows, axis=-1, keepdims=True) + EPS)
    scaled = rows * inverse
    grad = grad * gain_ref[0:1, :]
    grad = inverse * (grad - scaled * jnp.mean(grad * scaled, axis=-1, keepdims=True))
    out_ref[...] = (full_ref[...] + grad).astype(BF)


def finish_kernel(pieces_ref, gain_ref, q_ref, k_ref, v_ref, o_ref, gate_ref, up_ref, down_ref):
    for side in range(2):
        first = pieces_ref[side * 16 : side * 16 + 16, 0:1600].astype(F32)[:9]
        second = pieces_ref[side * 16 + 32 : side * 16 + 48, 0:1600].astype(F32)[:9]
        total = first + second
        q_ref[:, side * 576 : side * 576 + 576] = total[:, 0:576]
        k_ref[:, side * 192 : side * 192 + 192] = total[:, 640:832]
        v_ref[:, side * 192 : side * 192 + 192] = total[:, 832:1024]
        o_ref[:, side * 576 : side * 576 + 576] = total[:, 1024:1600]
        if side == 0:
            gain_ref[...] = total[:, 512:640]
        else:
            gain_ref[...] += total[:, 512:640]
    for part in range(4):
        rows = slice(part * 16, part * 16 + 16)
        lanes = slice(part * FF_PART, part * FF_PART + FF_PART)
        gate_ref[:, lanes] = pieces_ref[rows, 1664:2432].astype(F32)[:9]
        up_ref[:, lanes] = pieces_ref[rows, 2432:3200].astype(F32)[:9]
        down_ref[:, lanes] = pieces_ref[rows, 3200:3968].astype(F32)[:9]


VMEM = pl.BlockSpec(memory_space=pltpu.VMEM)
SMEM = pl.BlockSpec(memory_space=pltpu.SMEM)
HBM = pl.BlockSpec(memory_space=pltpu.HBM)


def takes(microseconds):
    return pl.CostEstimate(flops=int(microseconds * 6e8), bytes_accessed=1 << 20, transcendentals=0)


def shapes(*sizes):
    return tuple(jax.ShapeDtypeStruct(size[:-1], size[-1]) for size in sizes)


def kernel_call(kernel, ins, outs, scalars=0, scratch=(), micros=3, far=(), sems=0, far_out=False, room=6, late=()):
    specs = [SMEM if index < scalars else HBM if index in far else VMEM for index in range(len(ins))]
    scratch_shapes = [pltpu.VMEM(size[:-1], size[-1]) for size in scratch]
    if sems:
        scratch_shapes.append(pltpu.SemaphoreType.DMA((sems,)))
    scratch_shapes += [pltpu.VMEM(size[:-1], size[-1]) for size in late]
    return pl.pallas_call(
        kernel,
        out_shape=shapes(*outs),
        in_specs=specs,
        out_specs=(HBM if far_out else VMEM,) * len(outs),
        scratch_shapes=scratch_shapes,
        compiler_params=pltpu.CompilerParams(vmem_limit_bytes=room * 1024 * 1024),
        cost_estimate=takes(micros),
    )(*ins)


def pack(z, *weights):
    return kernel_call(
        pack_kernel,
        (z,) + weights,
        ((512, DIM, BF),) + ((16, FFN, BF),) * 4,
        scalars=1,
        scratch=[weight.shape + (BF,) for weight in weights],
        far=range(1, 9),
        sems=8,
        room=60,
        late=((32, QKV, BF),),
    )


def feed_forward(*ins):
    return kernel_call(
        ffn_kernel,
        ins,
        (
            (512, DIM, BF),
            (128, DIM, F32),
            (128, DIM, BF),
            (128, DIM, BF),
            (128, DIM, BF),
            (128, DIM, F32),
            (128, DIM, BF),
            (512, DIM, BF),
            (512, FF_PART, BF),
            (512, FF_PART, BF),
            (512, FF_PART, BF),
            (512, DIM, BF),
            (DIM, HALF_Q, BF),
            (8, DIM, F32),
        ),
        scalars=1,
        scratch=(
            (DIM, FFN, BF),
            (512, DIM, BF),
            (512, DIM, BF),
            (512, DIM, F32),
            (512, DIM, F32),
            (512, DIM, F32),
            (512, 256, F32),
            (512, 256, F32),
            (512, 256, F32),
        ),
        far=range(7, 15),
        sems=8,
        micros=15,
        room=60,
    )


def project(*ins):
    return kernel_call(
        qkv_kernel,
        ins,
        (
            (256, DIM, BF),
            (256, DIM, BF),
            (256, HALF_Q, BF),
            (2048, KV, BF),
            (8, DIM, F32),
        ),
        scratch=((DIM, QKV, BF),),
        room=60,
    )


def attend(*ins):
    return kernel_call(
        attend_kernel,
        ins,
        ((256, HALF_Q, F32), (3, 768, 128, F32), (4096, KV, BF), (1024, 640, BF)),
        scalars=3,
        scratch=((3, 34, 192, TILE, F32), (3, 768, 128, BF)) + ((3, 768, 128, F32),) * 3,
        micros=20,
        room=30,
    )


def attend_back(*ins):
    return kernel_call(
        attend_back_kernel,
        ins,
        ((256, HALF_Q, F32), (2048, KV, BF), (2048, KV, BF)),
        scalars=2,
        scratch=(
            (4096, KV, F32),
            (256, DIM, BF),
            (256, HALF_Q, BF),
            (3, 768, 128, BF),
            (3, 768, 128, BF),
            (3, 768, 128, F32),
            (3, 768, TILE, BF),
            (3, 768, TILE, BF),
            (3, 768, 128, F32),
        ),
        micros=40,
        room=20,
    )


def pick(matrix, value):
    return jnp.dot(matrix, value, preferred_element_type=F32).astype(BF)


def send_turn(block, first):
    return [send(block, turn_by(step, first)) for step in (1, 3, 2)]


def scatter_turns(nears, fars):
    width = sum(near.shape[1] for near in nears)
    near, *rest = kernel_call(
        merge_kernel, tuple(nears) + tuple(fars), ((144, width, F32),) + ((144, width, BF),) * 3
    )
    rest = [send(part, turn_by(-step, False)) for part, step in zip(rest, (1, 3, 2))]
    return near, rest


def scatter_rows(groups, inner_order):
    near, *rest = kernel_call(
        spread_kernel, (inner_order, *groups), ((40, PIECES, BF),) * 4
    )
    return [near] + [send(part, turn_by(-step, True)) for part, step in zip(rest, (1, 3, 2))]


def rope_tables(positions):
    lane = jnp.arange(128, dtype=jnp.int32)
    inverse = 1.0 / 10000.0 ** ((lane % 32).astype(F32) * (2.0 / HEAD))
    angles = positions.astype(F32)[:, None] * inverse[None, :]
    sign = jnp.where(lane % HEAD < HEAD // 2, -1.0, 1.0)
    return (jnp.cos(angles), jnp.sin(angles) * sign[None, :])


def after(value, *others):
    return lax.optimization_barrier((value,) + others)[0]


def one_hot(rows, columns):
    return (rows == columns).astype(BF)


def body(
    tokens,
    grad_out,
    pair_order,
    attn_gain,
    query_weight,
    key_weight,
    value_weight,
    output_weight,
    ffn_gain,
    gate_weight,
    up_weight,
    down_weight,
):
    dp, ctx = lax.axis_index("dp"), lax.axis_index("ctx")
    l, c = dp // 2, dp % 2
    h, x, z = ctx // 16, (ctx // 4) % 4, ctx % 4
    y, b = 2 * h + l, z % 2
    even = b == 0

    local = jnp.arange(DIM, dtype=jnp.int32)
    from_c = (local // 576) ^ (z // 2)
    turns = jnp.array([0, 1, 3, 2], jnp.int32)
    outer, inner = turns[(local // 144) % 4], turns[(local // 36) % 4]
    from_x = (x - jnp.where(from_c == 0, outer, inner)) % 4
    from_y = (y - jnp.where(from_c == 0, inner, outer)) % 4
    from_z = (local // 9) % 4
    owner = (2 * (from_y % 2) + from_c) * 32 + (4 * (from_y // 2) + from_x) * 4 + from_z
    natural = owner * 9 + local % 9
    order = one_hot(jnp.arange(DIM, dtype=jnp.int32)[:, None], natural[None, :])
    rows40 = jnp.arange(40, dtype=jnp.int32)
    z_order = one_hot(
        jnp.where(rows40 < 36, (rows40 // 9) * 16 + rows40 % 9, -1)[:, None],
        jnp.arange(64, dtype=jnp.int32)[None, :],
    )
    z_arrival = one_hot(
        jnp.where(rows40 < 36, ((z - rows40 // 9) % 4) * 16 + rows40 % 9, -1)[:, None],
        jnp.arange(64, dtype=jnp.int32)[None, :],
    )
    rows144 = jnp.arange(144, dtype=jnp.int32)
    inner_order = one_hot(
        ((rows144 // 36) * 40 + rows144 % 36)[:, None], jnp.arange(160, dtype=jnp.int32)[None, :]
    )
    chunk = jnp.arange(64, dtype=jnp.int32)
    chunk_ctx = (
        ((chunk // 4) % 8) * 4
        + 2 * ((chunk // 32) ^ c)
        + ((chunk // 2) % 2 ^ b)
    )
    ctx_match = chunk_ctx[:, None] == jnp.arange(32, dtype=jnp.int32)[None, :]
    chunk_pair = jnp.sum(jnp.where(ctx_match, pair_order[None, :], 0), axis=1)
    spot = jnp.where(chunk % 2 == 0, chunk_pair, 63 - chunk_pair)
    place = lax.dynamic_slice_in_dim(spot, (4 * h + x) * 4, 4)
    ahead = jnp.sum((place[None, :] > place[:, None]).astype(jnp.int32), axis=1)
    at_rank = ahead[None, :] == jnp.arange(4, dtype=jnp.int32)[:, None]
    rank = jnp.concatenate(
        [
            jnp.sum(jnp.where(at_rank, place[None, :], 0), axis=1),
            jnp.sum(jnp.where(at_rank, jnp.arange(4, dtype=jnp.int32)[None, :], 0), axis=1),
        ]
    )
    positions = (place[:, None] * 64 + jnp.arange(64, dtype=jnp.int32)[None, :]).reshape(256)
    cos_table, sin_table = rope_tables(positions)


    z_own = jnp.reshape(z, (1,))
    attn_send, *ffn_send = pack(
        z_own,
        jnp.stack([attn_gain, ffn_gain], axis=1),
        query_weight,
        key_weight,
        value_weight,
        output_weight,
        gate_weight,
        up_weight,
        down_weight,
    )
    rows_both = kernel_call(
        rows_kernel, (after(tokens[0], attn_send), grad_out[0], order), ((128, 2 * DIM, BF),)
    )[0]
    rows_near = [send(rows_both, home(flip)) for flip in (0, 1)]
    ffn_all = [ffn_send[0]] + [send(ffn_send[step], to_z(step)) for step in (1, 2, 3)]
    attn_all = lax.all_to_all(attn_send, ALL, 0, 0, tiled=True, axis_index_groups=CHIP_GROUPS)
    chip = jnp.arange(64, dtype=jnp.int32)
    far_x, far_y = (x - chip // 16) % 4, (y - (chip // 4) % 4) % 4
    turn_x, turn_y = turns[far_x], turns[far_y]
    target = jnp.where(c == 0, turn_x * 4 + turn_y, turn_y * 4 + turn_x) * 36 + (chip % 4) * 9
    first_rows = (target[:, None] + jnp.arange(8, dtype=jnp.int32)[None, :]).reshape(512)
    rows576 = jnp.arange(576, dtype=jnp.int32)[:, None]
    attn_half = kernel_call(
        unpack_kernel,
        (
            after(attn_all, cos_table, sin_table, *rows_near),
            one_hot(rows576, first_rows[None, :]),
            one_hot(rows576, (target + 8)[None, :]),
        ),
        ((576, QKV, BF),),
        scratch=((512, 128, F32),),
    )[0]
    ffn_half = after(pick(z_arrival, jnp.concatenate(ffn_all, axis=0)), attn_all)
    rows_both = after(rows_both, attn_all)
    rows_far = [send(rows_both, home(flip)) for flip in (2, 3)]

    attn_other = send(attn_half, other_core)
    inputs, normed_a, queries, kv_send, gains = project(
        *rows_near,
        attn_half,
        attn_other,
        cos_table,
        sin_table,
    )
    ffn_half = [ffn_half] + send_turn(ffn_half, True)
    kv = after(exchange(kv_send, HX_GROUPS), *ffn_half, *rows_far)
    ffn_half = pick(inner_order, jnp.concatenate(ffn_half, axis=0))
    ffn_near = [ffn_half] + send_turn(ffn_half, False)
    heads_out, logs, kv_sorted, heads_send = attend(
        spot, rank, jnp.reshape(b, (1,)), queries, kv, send(kv, other_core)
    )
    heads_low = heads_out.astype(BF)
    heads_all = exchange(heads_send, Z_GROUPS)
    ffn_far = [send(ffn_near[0], other_core)]
    ffn_far += [send(after(piece, heads_all), other_core) for piece in ffn_near[1:]]
    (
        normed_grad,
        out_own,
        *out_terms,
        hidden_own,
        grad_own,
        grad_local,
        hidden,
        dgate,
        dup,
        normed_f,
        output_part,
        ffn_gain_terms,
    ) = feed_forward(
        z_own, *rows_near, *rows_far, heads_all, gains, *ffn_near, *ffn_far
    )
    normed_grad = exchange(normed_grad, Z_GROUPS)
    ffn_near, ffn_far = kernel_call(
        ffn_grad_kernel,
        (normed_f, grad_local, hidden, dgate, dup),
        ((576, 2304, BF), (576, 2304, BF)),
        micros=6,
        room=60,
    )
    grad_hidden_one, grad_branch = kernel_call(
        branch_kernel, (normed_grad, hidden_own, grad_own, gains), ((128, DIM, F32), (128, DIM, BF))
    )
    grad_pair = send(grad_branch, z_pair)
    ffn_far = send(after(ffn_far, grad_branch), other_core)
    ffn_near, ffn_rest = scatter_turns([ffn_near], [ffn_far])

    output_near, output_far = kernel_call(
        output_grad_kernel,
        (grad_branch, grad_pair, heads_low),
        ((576, HALF_Q, BF), (576, HALF_Q, BF)),
        scratch=((256, DIM, BF),),
    )
    output_far = send(output_far, other_core)
    dq, dkv, dkv_far = attend_back(
        spot, rank, queries, kv_sorted, heads_out, logs, after(grad_branch, ffn_near), grad_pair, output_part
    )
    out_terms = [after(terms, dq) for terms in out_terms]
    out_terms = [send(terms, to_z(step)) for step, terms in enumerate(out_terms, 1)]
    dkv = kernel_call(core_sum_kernel, (dkv, send(after(dkv_far, *ffn_rest), other_core)), ((2048, KV, BF),))[0]
    dkv = exchange(dkv, HX_GROUPS)
    block_out = kernel_call(out_kernel, (out_own, *out_terms), ((128, DIM, BF),))[0]
    block_out = unpick_columns(send(block_out, home(0)), order)
    attn_near, attn_far, grad_own, grad_pair = kernel_call(
        attn_grad_kernel,
        (after(dq, *out_terms), dkv, cos_table, sin_table, normed_a, attn_half, attn_other, inputs, gains, ffn_gain_terms),
        ((576, QKV, BF), (576, QKV, BF), (128, DIM, F32), (128, DIM, BF)),
        scratch=((256, QKV, BF), (DIM, QKV, BF)),
        room=60,
    )
    attn_far = send(attn_far, other_core)
    grad_pair = send(grad_pair, z_pair)
    attn_near, attn_rest = scatter_turns([attn_near, output_near], [attn_far, output_far])
    grad_inputs = kernel_call(
        token_kernel,
        (grad_own, grad_pair, inputs, gains, grad_hidden_one),
        ((128, DIM, BF),),
    )[0]
    grad_inputs = unpick_columns(send(grad_inputs, home(0)), order)
    parts = scatter_rows((attn_near, *attn_rest, ffn_near, *ffn_rest), inner_order)

    pieces = kernel_call(split_kernel, (z_order, *parts), ((64, PIECES, BF),))[0]
    pieces = exchange(pieces, Z_GROUPS)
    gain_grads, *weight_grads = kernel_call(
        finish_kernel,
        (pieces,),
        ((9, 128, F32), (9, DIM, F32), (9, KV, F32), (9, KV, F32), (9, DIM, F32)) + ((9, 3072, F32),) * 3,
    )

    return (
        block_out[None],
        grad_inputs[None],
        gain_grads[:, 64],
        *weight_grads[:4],
        gain_grads[:, 65],
        *weight_grads[4:],
    )


def unpick_columns(rows, order):
    return jnp.einsum("tk,dk->td", rows, order, preferred_element_type=F32).astype(BF)


def solution(mesh):
    weights = P(ALL, None)
    rows = P("dp", "ctx", None)
    return jax.shard_map(
        body,
        mesh=mesh,
        in_specs=(rows, rows, P(), P(ALL), weights, weights, weights, weights, P(ALL), weights, weights, weights),
        out_specs=(rows, rows, P(ALL), weights, weights, weights, weights, P(ALL), weights, weights, weights),
        check_vma=False,
    )
```

```python
import functools
import itertools

import jax
import jax.numpy as jnp
from jax import lax
from jax.experimental import pallas as pl
from jax.experimental.pallas import tpu as pltpu
from jax.sharding import PartitionSpec as P

ALL = ("dp", "ctx")
EPS = 1e-05
DIM = 1152
HEAD = 64
HALF_Q = 576
KV = 384
QKV = 1024
FF_PART = 768
FFN = 3456
PIECES = 3968
TILE = 256
BF = jnp.bfloat16
F32 = jnp.float32


def flat(l, c, h, x, z):
    return (2 * l + c) * 32 + (4 * h + x) * 4 + z


def moves(target):
    places = itertools.product(range(2), range(2), range(2), range(4), range(4))
    return [(flat(*place), flat(*target(*place))) for place in places]


def send(value, target):
    return lax.ppermute(value, ALL, moves(target))


def to_z(step):
    return lambda l, c, h, x, z: (l, c, h, x, (z + step) % 4)


def turn_by(step, first):
    def target(l, c, h, x, z):
        y = 2 * h + l
        if (c == 0) == first:
            y = (y + step) % 4
        else:
            x = (x + step) % 4
        return (y % 2, c, y // 2, x, z)

    return target


def other_core(l, c, h, x, z):
    return (l, 1 - c, h, x, z)


def z_pair(l, c, h, x, z):
    return (l, c, h, x, z ^ 1)


def home(flip):
    return lambda l, c, h, x, z: (l, z // 2, h, x, (2 * c + z % 2) ^ flip)


Z_GROUPS = [[ring * 4 + z for z in range(4)] for ring in range(8)]
CHIP_GROUPS = [
    [flat(y % 2, c, y // 2, x, z) for x in range(4) for y in range(4) for z in range(4)] for c in range(2)
]
HX_GROUPS = [[place * 4 + z for place in range(8)] for z in range(4)]


def exchange(parts, groups):
    return lax.all_to_all(parts, "ctx", 0, 0, tiled=True, axis_index_groups=groups)


def swap_halves(block):
    lane = lax.broadcasted_iota(jnp.int32, block.shape, 1) % HEAD
    return jnp.where(
        lane < HEAD // 2, pltpu.roll(block, 128 - HEAD // 2, 1), pltpu.roll(block, HEAD // 2, 1)
    )


def fill(ref, row, lane, value):
    ref[row : row + value.shape[0], lane : lane + value.shape[1]] = value


def pack_kernel(z_ref, *refs):
    arrived, sems = refs[13:21], refs[21]
    copies = [
        pltpu.make_async_copy(here, there, sems.at[index])
        for index, (here, there) in enumerate(zip(refs[:8], arrived))
    ]
    for copy in copies:
        copy.start()
    for copy in copies:
        copy.wait()
    gain_ref, q_ref, k_ref, v_ref, o_ref, gate_ref, up_ref, down_ref = arrived
    attn_ref, wide_ref = refs[8], refs[22]
    wide_ref[...] = jnp.zeros(wide_ref.shape, BF)
    for side in range(2):
        row = side * 16
        fill(wide_ref, row, 0, q_ref[:, side * 576 : side * 576 + 576])
        fill(wide_ref, row, 576, gain_ref[...])
        fill(wide_ref, row, 640, k_ref[:, side * 192 : side * 192 + 192])
        fill(wide_ref, row, 832, v_ref[:, side * 192 : side * 192 + 192])
    chunks = []
    for side in range(2):
        rows = wide_ref[side * 16 : side * 16 + 16, :].astype(F32)
        last = jnp.concatenate([rows[8:9, part * 128 : part * 128 + 128] for part in range(8)], axis=0)
        chunks.append(jnp.concatenate([rows[:8], last], axis=1))
    both = jnp.concatenate(chunks, axis=0).astype(BF)

    def copy_both(index, carry):
        attn_ref[pl.ds(pl.multiple_of(index * 16, 16), 16), :] = both
        return carry

    lax.fori_loop(0, 32, copy_both, 0)
    for step in range(4):
        ffn_ref = refs[9 + step]
        ffn_ref[...] = jnp.zeros((16, FFN), BF)
        start = pl.multiple_of(((z_ref[0] + step) % 4) * FF_PART, FF_PART)
        fill(ffn_ref, 0, 0, gate_ref[:, pl.ds(start, FF_PART)])
        fill(ffn_ref, 0, 768, up_ref[:, pl.ds(start, FF_PART)])
        fill(ffn_ref, 0, 1536, down_ref[:, pl.ds(start, FF_PART)])
        fill(ffn_ref, 0, 2304, o_ref[...])


def unpack_kernel(all_ref, order_ref, last_order_ref, out_ref, tail_ref):
    tail_ref[...] = all_ref[:, QKV:].astype(F32)
    last = jnp.concatenate([tail_ref[pl.ds(part, 64, stride=8), :] for part in range(8)], axis=1)
    out_ref[...] = (
        jnp.dot(order_ref[...], all_ref[:, :QKV], preferred_element_type=F32)
        + jnp.dot(last_order_ref[...], last.astype(BF), preferred_element_type=F32)
    ).astype(BF)


def qkv_kernel(
    own_ref, pair_ref, half_ref, other_ref, cos_ref, sin_ref,
    x_ref, normed_ref, q_ref, kv_ref, gain_ref, weight_ref,
):
    x_ref[0:128, :] = own_ref[:, 0:DIM]
    x_ref[128:256, :] = pair_ref[:, 0:DIM]
    weight_ref[0:576, :] = half_ref[...]
    weight_ref[576:1152, :] = other_ref[...]
    inputs = x_ref[...].astype(F32)
    lane = lax.broadcasted_iota(jnp.int32, (8, 128), 1)
    row = lax.broadcasted_iota(jnp.int32, (8, 128), 0)
    gains = lax.dot_general(
        (lane == row + 64).astype(BF), weight_ref[:, 512:640], NT, preferred_element_type=F32
    )
    gain_ref[...] = gains
    inverse = lax.rsqrt(jnp.mean(inputs * inputs, axis=-1, keepdims=True) + EPS)
    normed = (inputs * inverse * gains[0:1]).astype(BF)
    normed_ref[...] = normed
    proj = jnp.dot(normed, weight_ref[...], preferred_element_type=F32)
    cos_table, sin_table = cos_ref[...], sin_ref[...]
    kv_parts = []
    for start in range(0, QKV, 128):
        block = proj[:, start : start + 128]
        turned = block * cos_table + swap_halves(block) * sin_table
        if start < 512:
            q_ref[:, start : start + 128] = (turned * 0.125).astype(BF)
        elif start == 512:
            q_ref[:, 512:576] = (turned[:, :64] * 0.125).astype(BF)
        elif start == 640:
            kv_parts.append(turned.astype(BF))
        elif start == 768:
            side = lax.broadcasted_iota(jnp.int32, block.shape, 1)
            kv_parts.append(jnp.where(side < HEAD, turned, block).astype(BF))
        else:
            kv_parts.append(block.astype(BF))
    for copy in range(8):
        for part in range(3):
            fill(kv_ref, copy * 256, part * 128, kv_parts[part])


def stack_heads(block, kv_head, upper):
    parts = []
    for group in range(3):
        start = (kv_head * 3 + group) * HEAD
        parts.append(block[:, start : start + HEAD])
    rows = jnp.concatenate(parts, axis=0)
    zeros = jnp.zeros_like(rows)
    return jnp.concatenate([zeros, rows] if upper else [rows, zeros], axis=1)


K_GROUP = (0, 0, 128)
K_UPPER = (False, True, False)
V_GROUP = (128, 256, 256)
V_UPPER = (True, False, True)
NT = (((1,), (1,)), ((), ()))
TN = (((0,), (0,)), ((), ()))


def mask_rows(scores, place, tile):
    row = lax.broadcasted_iota(jnp.int32, scores.shape, 0) % 64 + place * 64
    key = lax.broadcasted_iota(jnp.int32, scores.shape, 1) + tile * TILE
    return jnp.where(key <= row, scores, -1e30)


def over_tiles(rank_ref, step, carry):
    first = jnp.int32(0)
    for count in (4, 3, 2, 1):
        last = rank_ref[count - 1] // 4
        carry = lax.fori_loop(first, last, functools.partial(step, count=count, masked=False), carry)
        carry = lax.cond(
            first <= last,
            functools.partial(step, last, count=count, masked=True),
            lambda value: value,
            carry,
        )
        first = last + 1
    return carry


def stack_blocks(rank_ref, ref, target_ref, uppers):
    for rank in range(4):
        rows = ref[pl.ds(pl.multiple_of(rank_ref[4 + rank] * 64, 64), 64), :]
        for head in range(3):
            target_ref[head, rank * 192 : rank * 192 + 192, :] = stack_heads(rows, head, uppers[head])


def attend_kernel(
    spot_ref, rank_ref, side_ref, q_ref, near_ref, far_ref,
    out_ref, log_ref, sorted_ref, low_ref, score_ref, stack_ref, top_ref, sum_ref, total_ref,
):
    def put(index, carry):
        here = pl.ds(pl.multiple_of(index * 64, 64), 64)
        sorted_ref[pl.ds(pl.multiple_of(spot_ref[index] * 64, 64), 64), :] = near_ref[here, :]
        sorted_ref[pl.ds(pl.multiple_of(spot_ref[index + 32] * 64, 64), 64), :] = far_ref[here, :]
        return carry

    lax.fori_loop(0, 32, put, 0)
    stack_blocks(rank_ref, q_ref, stack_ref, K_UPPER)
    top_ref[...] = jnp.full(top_ref.shape, -1e30, F32)

    def score(tile, base, count, masked):
        span = pl.ds(pl.multiple_of(tile * TILE, TILE), TILE)
        for head in range(3):
            keys = sorted_ref[span, K_GROUP[head] : K_GROUP[head] + 128]
            for rank in range(count):
                rows = slice(rank * 192, rank * 192 + 192)
                scores = lax.dot_general(
                    stack_ref[head, rows, :], keys, NT, preferred_element_type=F32
                )
                if masked:
                    scores = mask_rows(scores, rank_ref[rank], tile)
                score_ref[head, base + rank] = scores
                top_ref[head, rows, :] = jnp.maximum(
                    top_ref[head, rows, :], jnp.maximum(scores[:, :128], scores[:, 128:])
                )
        return base + count

    over_tiles(rank_ref, score, jnp.int32(0))
    for head in range(3):
        top_ref[head] = jnp.broadcast_to(jnp.max(top_ref[head], axis=1, keepdims=True), (768, 128))
    sum_ref[...] = jnp.zeros(sum_ref.shape, F32)
    total_ref[...] = jnp.zeros(total_ref.shape, F32)

    def weigh(tile, base, count, masked):
        span = pl.ds(pl.multiple_of(tile * TILE, TILE), TILE)
        for head in range(3):
            values = sorted_ref[span, V_GROUP[head] : V_GROUP[head] + 128]
            for rank in range(count):
                rows = slice(rank * 192, rank * 192 + 192)
                scores = score_ref[head, base + rank]
                top = top_ref[head, rows, :]
                left = jnp.exp(scores[:, :128] - top)
                right = jnp.exp(scores[:, 128:] - top)
                total_ref[head, rows, :] += left + right
                weights = jnp.concatenate([left.astype(BF), right.astype(BF)], axis=1)
                sum_ref[head, rows, :] += jnp.dot(weights, values, preferred_element_type=F32)
        return base + count

    over_tiles(rank_ref, weigh, jnp.int32(0))
    for head in range(3):
        row_total = jnp.sum(total_ref[head], axis=1, keepdims=True)
        log_ref[head] = top_ref[head] + jnp.log(row_total)
        result = sum_ref[head] / row_total
        side = result[:, 64:] if V_UPPER[head] else result[:, :64]
        for rank in range(4):
            rows = pl.ds(pl.multiple_of(rank_ref[4 + rank] * 64, 64), 64)
            for group in range(3):
                start = (head * 3 + group) * HEAD
                row = rank * 192 + group * 64
                out_ref[rows, start : start + HEAD] = side[row : row + 64]
    side = side_ref[0]
    for copy in range(4):
        for block in range(2):
            start = pl.multiple_of(copy * 256 + (block ^ side) * 128, 128)
            low_ref[pl.ds(start, 128), 0:576] = out_ref[block * 128 : block * 128 + 128, :].astype(BF)
            low_ref[pl.ds(start, 128), 576:640] = jnp.zeros((128, 64), BF)


def attend_back_kernel(
    spot_ref, rank_ref, q_ref, sorted_ref, out_ref, log_ref, own_ref, pair_ref, part_ref,
    dq_ref, near_ref, far_ref,
    total_ref, rows_ref, grad_ref, stack_ref, grads_ref, delta_ref, prob_ref, dscore_ref, dq_sum_ref,
):
    rows_ref[0:128, :] = own_ref[...]
    rows_ref[128:256, :] = pair_ref[...]
    grad_ref[...] = jnp.dot(rows_ref[...], part_ref[...], preferred_element_type=F32).astype(BF)
    total_ref[...] = jnp.zeros_like(total_ref)
    dq_sum_ref[...] = jnp.zeros_like(dq_sum_ref)
    stack_blocks(rank_ref, q_ref, stack_ref, K_UPPER)
    stack_blocks(rank_ref, grad_ref, grads_ref, V_UPPER)
    for rank in range(4):
        rows = pl.ds(pl.multiple_of(rank_ref[4 + rank] * 64, 64), 64)
        products = grad_ref[rows, :].astype(F32) * out_ref[rows, :]
        for head in range(3):
            delta_ref[head, rank * 192 : rank * 192 + 192, :] = jnp.broadcast_to(
                jnp.sum(stack_heads(products, head, False), axis=1, keepdims=True), (192, 128)
            )

    def step(tile, carry, count, masked):
        span = pl.ds(pl.multiple_of(tile * TILE, TILE), TILE)
        size = count * 192
        for head in range(3):
            k_lanes = slice(K_GROUP[head], K_GROUP[head] + 128)
            v_lanes = slice(V_GROUP[head], V_GROUP[head] + 128)
            keys, values = sorted_ref[span, k_lanes], sorted_ref[span, v_lanes]
            scores_all = lax.dot_general(stack_ref[head, :size, :], keys, NT, preferred_element_type=F32)
            grad_all = lax.dot_general(grads_ref[head, :size, :], values, NT, preferred_element_type=F32)
            for rank in range(count):
                rows = slice(rank * 192, rank * 192 + 192)
                scores = scores_all[rows]
                if masked:
                    scores = mask_rows(scores, rank_ref[rank], tile)
                logs, delta = log_ref[head, rows, :], delta_ref[head, rows, :]
                for lane in (0, 128):
                    lanes = slice(lane, lane + 128)
                    prob = jnp.exp(scores[:, lanes] - logs)
                    prob_ref[head, rows, lanes] = prob.astype(BF)
                    dscore_ref[head, rows, lanes] = (prob * (grad_all[rows, lanes] - delta)).astype(BF)
        for head in range(3):
            k_lanes = slice(K_GROUP[head], K_GROUP[head] + 128)
            v_lanes = slice(V_GROUP[head], V_GROUP[head] + 128)
            keys = sorted_ref[span, k_lanes]
            dq_sum_ref[head, :size, :] += jnp.dot(
                dscore_ref[head, :size, :], keys, preferred_element_type=F32
            )
            total_ref[span, v_lanes] += lax.dot_general(
                prob_ref[head, :size, :], grads_ref[head, :size, :], TN, preferred_element_type=F32
            )
            total_ref[span, k_lanes] += lax.dot_general(
                dscore_ref[head, :size, :], stack_ref[head, :size, :], TN, preferred_element_type=F32
            )
        return carry

    over_tiles(rank_ref, step, jnp.int32(0))
    for head in range(3):
        for rank in range(4):
            rows = pl.ds(pl.multiple_of(rank_ref[4 + rank] * 64, 64), 64)
            for group in range(3):
                start = (head * 3 + group) * HEAD
                row = rank * 192 + group * 64
                block = dq_sum_ref[head, row : row + 64, :] * 0.125
                side = block[:, 64:] if K_UPPER[head] else block[:, :64]
                dq_ref[rows, start : start + HEAD] = side

    def put(index, carry):
        there = pl.ds(pl.multiple_of(index * 64, 64), 64)
        origin = pl.ds(pl.multiple_of(spot_ref[index] * 64, 64), 64)
        near_ref[there, :] = total_ref[origin, :].astype(BF)
        origin = pl.ds(pl.multiple_of(spot_ref[index + 32] * 64, 64), 64)
        far_ref[there, :] = total_ref[origin, :].astype(BF)
        return carry

    lax.fori_loop(0, 32, put, 0)


def rows_kernel(x_ref, grad_ref, order_ref, out_ref):
    for side, rows_ref in enumerate((x_ref, grad_ref)):
        out_ref[:, side * DIM : side * DIM + DIM] = jnp.dot(
            rows_ref[...], order_ref[...], preferred_element_type=F32
        ).astype(BF)


def ffn_kernel(
    z_ref, rows0_ref, rows1_ref, rows2_ref, rows3_ref, heads_ref, gain_ref,
    w0_ref, w1_ref, w2_ref, w3_ref, w4_ref, w5_ref, w6_ref, w7_ref,
    dn_ref, out0_ref, out1_ref, out2_ref, out3_ref, own_ref, grad_own_ref,
    grad_out, hidden_out, dgate_out, dup_out, normed_out, part_ref, gain_grad_ref,
    grad_ref, hidden_ref, dgate_ref, dup_ref, normed_ref, w_ref, scaled_ref, heads_all_ref, h1_ref, dn_sum_ref, out_sum_ref, gate_ref, up_ref, dh_ref, sems,
):
    pieces = (w0_ref, w1_ref, w2_ref, w3_ref, w4_ref, w5_ref, w6_ref, w7_ref)
    copies = [
        pltpu.make_async_copy(
            piece.at[:, pl.ds(lane, width)],
            w_ref.at[pl.ds(index * 144, 144), pl.ds(lane, width)],
            sems.at[8 * turn + index],
        )
        for turn, (lane, width) in enumerate(((2304, 1152), (0, 2304)))
        for index, piece in enumerate(pieces)
    ]
    for copy in copies:
        copy.start()
    z = z_ref[0]
    for slot, rows_ref in enumerate((rows0_ref, rows1_ref, rows2_ref, rows3_ref)):
        here = pl.ds(pl.multiple_of((z ^ slot) * 128, 128), 128)
        h1_ref[here, :] = rows_ref[:, 0:DIM].astype(F32)
        grad_ref[here, :] = rows_ref[:, DIM:]
    for side in range(2):
        for half in range(2):
            start = (2 * side + half) * 256
            heads_all_ref[side * 256 : side * 256 + 256, half * 576 : half * 576 + 576] = heads_ref[
                start : start + 256, 0:576
            ]
    for copy in copies[:8]:
        copy.wait()
    heads = heads_all_ref[...]
    for start in range(0, DIM, 384):
        h1_ref[:, start : start + 384] += lax.dot_general(
            heads, w_ref[start : start + 384, 2304:3456], NT, preferred_element_type=F32
        )

    def norm(index, carry):
        here = pl.ds(pl.multiple_of(index * 64, 64), 64)
        rows = h1_ref[here, :]
        inverse = lax.rsqrt(jnp.mean(rows * rows, axis=-1, keepdims=True) + EPS)
        scaled = rows * inverse
        scaled_ref[here, :] = scaled.astype(BF)
        normed_ref[here, :] = (scaled * gain_ref[1:2, :]).astype(BF)
        return carry

    lax.fori_loop(0, 8, norm, 0)
    here = pl.ds(pl.multiple_of(z * 128, 128), 128)
    own_ref[...] = h1_ref[here, :]
    grad_own_ref[...] = grad_ref[here, :]
    for copy in copies[8:]:
        copy.wait()
    outs = [
        pltpu.make_async_copy(here_ref, there_ref, sems.at[16 + index])
        for index, (here_ref, there_ref) in enumerate(
            (
                (normed_ref, normed_out),
                (grad_ref, grad_out),
                (hidden_ref, hidden_out),
                (dgate_ref, dgate_out),
                (dup_ref, dup_out),
            )
        )
    ]
    outs[0].start()
    outs[1].start()
    normed, grads = normed_ref[...], grad_ref[...]
    for index in range(3):
        start = index * 256
        gate_ref[index] = jnp.dot(normed, w_ref[:, start : start + 256], preferred_element_type=F32)
        up_ref[index] = jnp.dot(normed, w_ref[:, start + 768 : start + 1024], preferred_element_type=F32)
        dh_ref[index] = jnp.dot(grads, w_ref[:, start + 1536 : start + 1792], preferred_element_type=F32)
        there = slice(start, start + 256)
        for block in range(8):
            rows = slice(block * 64, block * 64 + 64)
            gate, up, grad = gate_ref[index, rows, :], up_ref[index, rows, :], dh_ref[index, rows, :]
            sigmoid = jax.nn.sigmoid(gate)
            active = gate * sigmoid
            hidden_ref[rows, there] = (active * up).astype(BF)
            dgate_ref[rows, there] = (grad * up * sigmoid * (1.0 + gate * (1.0 - sigmoid))).astype(BF)
            dup_ref[rows, there] = (grad * active).astype(BF)
    for copy in outs[2:]:
        copy.start()
    hidden, dgate, dup = hidden_ref[...], dgate_ref[...], dup_ref[...]
    for first in range(0, DIM, 384):
        rows = slice(first, first + 384)
        dn_sum_ref[:, rows] = lax.dot_general(
            dgate, w_ref[rows, 0:768], NT, preferred_element_type=F32
        ) + lax.dot_general(dup, w_ref[rows, 768:1536], NT, preferred_element_type=F32)
        out_sum_ref[:, rows] = lax.dot_general(
            hidden, w_ref[rows, 1536:2304], NT, preferred_element_type=F32
        )

    def finish(index, total):
        here = pl.ds(pl.multiple_of(index * 64, 64), 64)
        grad = dn_sum_ref[here, :]
        dn_ref[here, :] = grad.astype(BF)
        terms = grad * scaled_ref[here, :].astype(F32)
        return total + jnp.sum(terms.reshape(8, 8, DIM), axis=0)

    gain_grad_ref[...] = lax.fori_loop(0, 8, finish, jnp.zeros((8, DIM), F32))

    out0_ref[...] = own_ref[...] + out_sum_ref[here, :]
    for step, out_ref in enumerate((out1_ref, out2_ref, out3_ref)):
        there = pl.ds(pl.multiple_of(((z + step + 1) % 4) * 128, 128), 128)
        out_ref[...] = out_sum_ref[there, :].astype(BF)

    @pl.when(z % 2 == 0)
    def _():
        part_ref[...] = w_ref[:, 2304:2880]

    @pl.when(z % 2 == 1)
    def _():
        part_ref[...] = w_ref[:, 2880:3456]

    for copy in outs:
        copy.wait()


def outer_products(lefts, rights, near_ref, far_ref, extra=None):
    for start in range(0, DIM, 128):
        lane = 0
        for left, right in zip(lefts, rights):
            block = lax.dot_general(
                left[:, start : start + 128], right[...], TN, preferred_element_type=F32
            )
            if extra is not None:
                block = extra(start, block)
            block = block.astype(near_ref.dtype)
            width = block.shape[1]
            lanes = slice(lane, lane + width)
            if start < 512:
                near_ref[start : start + 128, lanes] = block
            elif start == 512:
                near_ref[512:576, lanes] = block[:64]
                far_ref[0:64, lanes] = block[64:].astype(BF)
            else:
                far_ref[start - 576 : start - 448, lanes] = block.astype(BF)
            lane += width


def ffn_grad_kernel(normed_ref, grad_ref, hidden_ref, dgate_ref, dup_ref, near_ref, far_ref):
    outer_products(
        (normed_ref, normed_ref, grad_ref), (dgate_ref, dup_ref, hidden_ref), near_ref, far_ref
    )


def output_grad_kernel(own_ref, pair_ref, heads_ref, near_ref, far_ref, rows_ref):
    rows_ref[0:128, :] = own_ref[...]
    rows_ref[128:256, :] = pair_ref[...]
    outer_products((rows_ref,), (heads_ref,), near_ref, far_ref)


def merge_kernel(*refs):
    count = len(refs) // 2 - 2
    targets = refs[2 * count :]
    for index in range(4):
        lane = 0
        for near_ref, far_ref in zip(refs[:count], refs[count : 2 * count]):
            width = near_ref.shape[1]
            rows = slice(index * 144, index * 144 + 144)
            total = near_ref[rows, :].astype(F32) + far_ref[rows, :].astype(F32)
            targets[index][:, lane : lane + width] = total.astype(targets[index].dtype)
            lane += width


def spread_kernel(order_ref, *refs):
    targets = refs[-4:]
    first = 0
    for group in range(2):
        near_ref, *others = refs[4 * group : 4 * group + 4]
        count = near_ref.shape[1]
        for start in range(0, count, 512):
            lanes = slice(start, min(start + 512, count))
            total = near_ref[:, lanes]
            for other_ref in others:
                total = total + other_ref[:, lanes].astype(F32)
            parts = lax.dot_general(order_ref[...], total.astype(BF), TN, preferred_element_type=F32)
            there = slice(first + lanes.start, first + lanes.stop)
            for index in range(4):
                targets[index][:, there] = parts[index * 40 : index * 40 + 40].astype(BF)
        first += count
        if first % 128:
            for target in targets:
                target[:, first : first + 64] = jnp.zeros((40, 64), BF)
            first += 64


def split_kernel(order_ref, near_ref, a_ref, b_ref, c_ref, target):
    lasts = []
    for start in range(0, PIECES, 512):
        lanes = slice(start, min(start + 512, PIECES))
        total = near_ref[:, lanes].astype(F32) + a_ref[:, lanes].astype(F32)
        total = total + b_ref[:, lanes].astype(F32) + c_ref[:, lanes].astype(F32)
        parts = lax.dot_general(order_ref[...], total.astype(BF), TN, preferred_element_type=F32)
        rows = jnp.concatenate([parts[part * 16 : part * 16 + 8] for part in range(4)], axis=0)
        target[:, lanes] = rows.astype(BF)
        last = jnp.concatenate([parts[part * 16 + 8 : part * 16 + 9] for part in range(4)], axis=0)
        rest = 512 - last.shape[1]
        if rest:
            last = jnp.concatenate([last, jnp.zeros((4, rest), F32)], axis=1)
        lasts.append(last)
    tail = jnp.concatenate([last[part : part + 1] for part in range(4) for last in lasts], axis=0)
    target[:, PIECES:] = tail.astype(BF)


def core_sum_kernel(near_ref, far_ref, out_ref):
    out_ref[...] = (near_ref[...].astype(F32) + far_ref[...].astype(F32)).astype(BF)


def branch_kernel(terms_ref, own_ref, grad_ref, gain_ref, full_ref, low_ref):
    grad = terms_ref[0:128, :].astype(F32)
    for part in range(1, 4):
        grad = grad + terms_ref[part * 128 : part * 128 + 128, :].astype(F32)
    rows = own_ref[...]
    inverse = lax.rsqrt(jnp.mean(rows * rows, axis=-1, keepdims=True) + EPS)
    scaled = rows * inverse
    grad = grad * gain_ref[1:2, :]
    grad = inverse * (grad - scaled * jnp.mean(grad * scaled, axis=-1, keepdims=True))
    grad = grad + grad_ref[...].astype(F32)
    full_ref[...] = grad
    low_ref[...] = grad.astype(BF)


def out_kernel(own_ref, a_ref, b_ref, c_ref, out_ref):
    total = own_ref[...] + a_ref[...].astype(F32)
    out_ref[...] = (total + b_ref[...].astype(F32) + c_ref[...].astype(F32)).astype(BF)


def attn_grad_kernel(
    dq_ref, dkv_ref, cos_ref, sin_ref, normed_ref, half_ref, other_ref, x_ref, gain_ref, ffn_gain_ref,
    near_ref, far_ref, own_ref, pair_ref, grad_ref, weight_ref,
):
    weight_ref[0:576, :] = half_ref[...]
    weight_ref[576:1152, :] = other_ref[...]
    cos_table, sin_table = cos_ref[...], sin_ref[...]

    def turn(block):
        return block * cos_table - swap_halves(block) * sin_table

    def summed(start):
        total = dkv_ref[0:256, start : start + 128].astype(F32)
        for part in range(1, 8):
            total = total + dkv_ref[part * 256 : part * 256 + 256, start : start + 128].astype(F32)
        return total

    for start in range(0, 512, 128):
        grad_ref[:, start : start + 128] = turn(dq_ref[:, start : start + 128]).astype(BF)
    tail = dq_ref[:, 512:576]
    wide = jnp.concatenate([tail, jnp.zeros_like(tail)], axis=1)
    grad_ref[:, 512:640] = turn(wide).astype(BF)
    grad_ref[:, 640:768] = turn(summed(0)).astype(BF)
    block = summed(128)
    lane = lax.broadcasted_iota(jnp.int32, block.shape, 1)
    grad_ref[:, 768:896] = jnp.where(lane < HEAD, turn(block), block).astype(BF)
    grad_ref[:, 896:1024] = summed(256).astype(BF)
    grads = lax.dot_general(grad_ref[...], weight_ref[...], NT, preferred_element_type=F32)
    own_ref[...] = grads[:128]
    pair_ref[...] = grads[128:].astype(BF)
    rows = x_ref[...].astype(F32)
    inverse = lax.rsqrt(jnp.mean(rows * rows, axis=-1, keepdims=True) + EPS)
    attn_terms = jnp.sum(grads * (rows * inverse), axis=0, keepdims=True)
    ffn_terms = jnp.sum(ffn_gain_ref[...], axis=0, keepdims=True)
    parts = []
    for terms in (attn_terms, ffn_terms):
        high = terms.astype(BF)
        parts.append(high.astype(F32))
        parts.append(terms - high.astype(F32))
    row = lax.broadcasted_iota(jnp.int32, (16, DIM), 0)
    gains = jnp.zeros((16, DIM), F32)
    for index, part in enumerate(parts):
        gains = jnp.where(row == index, part, gains)
    gains = gains.astype(BF)
    place_row = lax.broadcasted_iota(jnp.int32, (16, 128), 0)
    place_lane = lax.broadcasted_iota(jnp.int32, (16, 128), 1)
    places = ((place_lane == 64 + place_row // 2) & (place_row < 4)).astype(BF)

    def extra(start, block):
        columns = lax.dot_general(
            gains[:, start : start + 128], places, TN, preferred_element_type=F32
        )
        return jnp.concatenate([block[:, :512], block[:, 512:640] + columns, block[:, 640:]], axis=1)

    outer_products((normed_ref,), (grad_ref,), near_ref, far_ref, extra)


def token_kernel(own_ref, pair_ref, x_ref, gain_ref, full_ref, out_ref):
    grad = own_ref[...] + pair_ref[...].astype(F32)
    rows = x_ref[0:128, :].astype(F32)
    inverse = lax.rsqrt(jnp.mean(rows * rows, axis=-1, keepdims=True) + EPS)
    scaled = rows * inverse
    grad = grad * gain_ref[0:1, :]
    grad = inverse * (grad - scaled * jnp.mean(grad * scaled, axis=-1, keepdims=True))
    out_ref[...] = (full_ref[...] + grad).astype(BF)


def finish_kernel(pieces_ref, gain_ref, q_ref, k_ref, v_ref, o_ref, gate_ref, up_ref, down_ref):
    wholes = []
    pieces = pieces_ref[...].astype(F32)
    for part in range(4):
        rows = pieces[part * 8 : part * 8 + 8]
        last = jnp.concatenate([rows[index : index + 1, PIECES:] for index in range(8)], axis=1)
        wholes.append(jnp.concatenate([rows[:, :PIECES], last[:, :PIECES]], axis=0))
    for side in range(2):
        total = wholes[side][:, :1600] + wholes[side + 2][:, :1600]
        q_ref[:, side * 576 : side * 576 + 576] = total[:, 0:576]
        k_ref[:, side * 192 : side * 192 + 192] = total[:, 640:832]
        v_ref[:, side * 192 : side * 192 + 192] = total[:, 832:1024]
        o_ref[:, side * 576 : side * 576 + 576] = total[:, 1024:1600]
        if side == 0:
            gain_ref[...] = total[:, 512:640]
        else:
            gain_ref[...] += total[:, 512:640]
    for part in range(4):
        lanes = slice(part * FF_PART, part * FF_PART + FF_PART)
        gate_ref[:, lanes] = wholes[part][:, 1664:2432]
        up_ref[:, lanes] = wholes[part][:, 2432:3200]
        down_ref[:, lanes] = wholes[part][:, 3200:3968]


VMEM = pl.BlockSpec(memory_space=pltpu.VMEM)
SMEM = pl.BlockSpec(memory_space=pltpu.SMEM)
HBM = pl.BlockSpec(memory_space=pltpu.HBM)


def takes(microseconds):
    return pl.CostEstimate(flops=int(microseconds * 6e8), bytes_accessed=1 << 20, transcendentals=0)


def shapes(*sizes):
    return tuple(jax.ShapeDtypeStruct(size[:-1], size[-1]) for size in sizes)


def kernel_call(kernel, ins, outs, scalars=0, scratch=(), micros=3, far=(), sems=0, far_outs=(), room=6, late=()):
    specs = [SMEM if index < scalars else HBM if index in far else VMEM for index in range(len(ins))]
    scratch_shapes = [pltpu.VMEM(size[:-1], size[-1]) for size in scratch]
    if sems:
        scratch_shapes.append(pltpu.SemaphoreType.DMA((sems,)))
    scratch_shapes += [pltpu.VMEM(size[:-1], size[-1]) for size in late]
    return pl.pallas_call(
        kernel,
        out_shape=shapes(*outs),
        in_specs=specs,
        out_specs=tuple(HBM if index in far_outs else VMEM for index in range(len(outs))),
        scratch_shapes=scratch_shapes,
        compiler_params=pltpu.CompilerParams(vmem_limit_bytes=room * 1024 * 1024),
        cost_estimate=takes(micros),
    )(*ins)


def pack(z, *weights):
    return kernel_call(
        pack_kernel,
        (z,) + weights,
        ((512, DIM, BF),) + ((16, FFN, BF),) * 4,
        scalars=1,
        scratch=[weight.shape + (BF,) for weight in weights],
        far=range(1, 9),
        sems=8,
        room=60,
        late=((32, QKV, BF),),
    )


def feed_forward(*ins):
    return kernel_call(
        ffn_kernel,
        ins,
        (
            (512, DIM, BF),
            (128, DIM, F32),
            (128, DIM, BF),
            (128, DIM, BF),
            (128, DIM, BF),
            (128, DIM, F32),
            (128, DIM, BF),
            (512, DIM, BF),
            (512, FF_PART, BF),
            (512, FF_PART, BF),
            (512, FF_PART, BF),
            (512, DIM, BF),
            (DIM, HALF_Q, BF),
            (8, DIM, F32),
        ),
        scalars=1,
        scratch=(
            (512, DIM, BF),
            (512, FF_PART, BF),
            (512, FF_PART, BF),
            (512, FF_PART, BF),
            (512, DIM, BF),
            (DIM, FFN, BF),
            (512, DIM, BF),
            (512, DIM, BF),
            (512, DIM, F32),
            (512, DIM, F32),
            (512, DIM, F32),
            (3, 512, 256, F32),
            (3, 512, 256, F32),
            (3, 512, 256, F32),
        ),
        far=range(7, 15),
        far_outs=range(7, 12),
        sems=21,
        micros=15,
        room=60,
    )


def project(*ins):
    return kernel_call(
        qkv_kernel,
        ins,
        (
            (256, DIM, BF),
            (256, DIM, BF),
            (256, HALF_Q, BF),
            (2048, KV, BF),
            (8, DIM, F32),
        ),
        scratch=((DIM, QKV, BF),),
        room=60,
    )


def attend(*ins):
    return kernel_call(
        attend_kernel,
        ins,
        ((256, HALF_Q, F32), (3, 768, 128, F32), (4096, KV, BF), (1024, 640, BF)),
        scalars=3,
        scratch=((3, 34, 192, TILE, F32), (3, 768, 128, BF)) + ((3, 768, 128, F32),) * 3,
        micros=20,
        room=30,
    )


def attend_back(*ins):
    return kernel_call(
        attend_back_kernel,
        ins,
        ((256, HALF_Q, F32), (2048, KV, BF), (2048, KV, BF)),
        scalars=2,
        scratch=(
            (4096, KV, F32),
            (256, DIM, BF),
            (256, HALF_Q, BF),
            (3, 768, 128, BF),
            (3, 768, 128, BF),
            (3, 768, 128, F32),
            (3, 768, TILE, BF),
            (3, 768, TILE, BF),
            (3, 768, 128, F32),
        ),
        micros=40,
        room=20,
    )


def pick(matrix, value):
    return jnp.dot(matrix, value, preferred_element_type=F32).astype(BF)


def send_turn(block, first):
    return [send(block, turn_by(step, first)) for step in (1, 3, 2)]


def merge_cores(nears, fars):
    width = sum(near.shape[1] for near in nears)
    near, *rest = kernel_call(
        merge_kernel, tuple(nears) + tuple(fars), ((144, width, F32),) + ((144, width, BF),) * 3
    )
    return near, rest


def send_back(parts):
    return [send(part, turn_by(-step, False)) for part, step in zip(parts, (1, 3, 2))]


def scatter_rows(groups, inner_order):
    near, *rest = kernel_call(
        spread_kernel, (inner_order, *groups), ((40, PIECES, BF),) * 4
    )
    return [near] + [send(part, turn_by(-step, True)) for part, step in zip(rest, (1, 3, 2))]


def rope_tables(positions):
    lane = jnp.arange(128, dtype=jnp.int32)
    inverse = 1.0 / 10000.0 ** ((lane % 32).astype(F32) * (2.0 / HEAD))
    angles = positions.astype(F32)[:, None] * inverse[None, :]
    sign = jnp.where(lane % HEAD < HEAD // 2, -1.0, 1.0)
    return (jnp.cos(angles), jnp.sin(angles) * sign[None, :])


def after(value, *others):
    return lax.optimization_barrier((value,) + others)[0]


def one_hot(rows, columns):
    return (rows == columns).astype(BF)


def body(
    tokens,
    grad_out,
    pair_order,
    attn_gain,
    query_weight,
    key_weight,
    value_weight,
    output_weight,
    ffn_gain,
    gate_weight,
    up_weight,
    down_weight,
):
    dp, ctx = lax.axis_index("dp"), lax.axis_index("ctx")
    l, c = dp // 2, dp % 2
    h, x, z = ctx // 16, (ctx // 4) % 4, ctx % 4
    y, b = 2 * h + l, z % 2
    even = b == 0

    local = jnp.arange(DIM, dtype=jnp.int32)
    from_c = (local // 576) ^ (z // 2)
    turns = jnp.array([0, 1, 3, 2], jnp.int32)
    outer, inner = turns[(local // 144) % 4], turns[(local // 36) % 4]
    from_x = (x - jnp.where(from_c == 0, outer, inner)) % 4
    from_y = (y - jnp.where(from_c == 0, inner, outer)) % 4
    from_z = (local // 9) % 4
    owner = (2 * (from_y % 2) + from_c) * 32 + (4 * (from_y // 2) + from_x) * 4 + from_z
    natural = owner * 9 + local % 9
    order = one_hot(jnp.arange(DIM, dtype=jnp.int32)[:, None], natural[None, :])
    rows40 = jnp.arange(40, dtype=jnp.int32)
    z_order = one_hot(
        jnp.where(rows40 < 36, (rows40 // 9) * 16 + rows40 % 9, -1)[:, None],
        jnp.arange(64, dtype=jnp.int32)[None, :],
    )
    z_arrival = one_hot(
        jnp.where(rows40 < 36, ((z - rows40 // 9) % 4) * 16 + rows40 % 9, -1)[:, None],
        jnp.arange(64, dtype=jnp.int32)[None, :],
    )
    rows144 = jnp.arange(144, dtype=jnp.int32)
    inner_order = one_hot(
        ((rows144 // 36) * 40 + rows144 % 36)[:, None], jnp.arange(160, dtype=jnp.int32)[None, :]
    )
    chunk = jnp.arange(64, dtype=jnp.int32)
    chunk_ctx = (
        ((chunk // 4) % 8) * 4
        + 2 * ((chunk // 32) ^ c)
        + ((chunk // 2) % 2 ^ b)
    )
    ctx_match = chunk_ctx[:, None] == jnp.arange(32, dtype=jnp.int32)[None, :]
    chunk_pair = jnp.sum(jnp.where(ctx_match, pair_order[None, :], 0), axis=1)
    spot = jnp.where(chunk % 2 == 0, chunk_pair, 63 - chunk_pair)
    place = lax.dynamic_slice_in_dim(spot, (4 * h + x) * 4, 4)
    ahead = jnp.sum((place[None, :] > place[:, None]).astype(jnp.int32), axis=1)
    at_rank = ahead[None, :] == jnp.arange(4, dtype=jnp.int32)[:, None]
    rank = jnp.concatenate(
        [
            jnp.sum(jnp.where(at_rank, place[None, :], 0), axis=1),
            jnp.sum(jnp.where(at_rank, jnp.arange(4, dtype=jnp.int32)[None, :], 0), axis=1),
        ]
    )
    positions = (place[:, None] * 64 + jnp.arange(64, dtype=jnp.int32)[None, :]).reshape(256)
    cos_table, sin_table = rope_tables(positions)


    z_own = jnp.reshape(z, (1,))
    attn_send, *ffn_send = pack(
        z_own,
        jnp.stack([attn_gain, ffn_gain], axis=1),
        query_weight,
        key_weight,
        value_weight,
        output_weight,
        gate_weight,
        up_weight,
        down_weight,
    )
    rows_both = kernel_call(
        rows_kernel, (after(tokens[0], attn_send), grad_out[0], order), ((128, 2 * DIM, BF),)
    )[0]
    rows_near = [send(rows_both, home(flip)) for flip in (0, 1)]
    ffn_all = [ffn_send[0]] + [send(ffn_send[step], to_z(step)) for step in (1, 2, 3)]
    attn_all = lax.all_to_all(attn_send, ALL, 0, 0, tiled=True, axis_index_groups=CHIP_GROUPS)
    chip = jnp.arange(64, dtype=jnp.int32)
    far_x, far_y = (x - chip // 16) % 4, (y - (chip // 4) % 4) % 4
    turn_x, turn_y = turns[far_x], turns[far_y]
    target = jnp.where(c == 0, turn_x * 4 + turn_y, turn_y * 4 + turn_x) * 36 + (chip % 4) * 9
    first_rows = (target[:, None] + jnp.arange(8, dtype=jnp.int32)[None, :]).reshape(512)
    rows576 = jnp.arange(576, dtype=jnp.int32)[:, None]
    attn_half = kernel_call(
        unpack_kernel,
        (
            after(attn_all, cos_table, sin_table, *rows_near),
            one_hot(rows576, first_rows[None, :]),
            one_hot(rows576, (target + 8)[None, :]),
        ),
        ((576, QKV, BF),),
        scratch=((512, 128, F32),),
    )[0]
    ffn_half = after(pick(z_arrival, jnp.concatenate(ffn_all, axis=0)), attn_all)
    rows_both = after(rows_both, attn_all)
    rows_far = [send(rows_both, home(flip)) for flip in (2, 3)]

    attn_other = send(attn_half, other_core)
    inputs, normed_a, queries, kv_send, gains = project(
        *rows_near,
        attn_half,
        attn_other,
        cos_table,
        sin_table,
    )
    kv = after(exchange(kv_send, HX_GROUPS), ffn_half, *rows_far)
    ffn_half = after(ffn_half, kv)
    ffn_half = [ffn_half] + send_turn(ffn_half, True)
    heads_out, logs, kv_sorted, heads_send = attend(
        spot, rank, jnp.reshape(b, (1,)), queries, kv, send(kv, other_core)
    )
    heads_low = heads_out.astype(BF)
    ffn_half = [after(piece, heads_send) for piece in ffn_half]
    ffn_half = pick(inner_order, jnp.concatenate(ffn_half, axis=0))
    ffn_near = [ffn_half] + send_turn(ffn_half, False)
    heads_all = exchange(heads_send, Z_GROUPS)
    ffn_far = [send(ffn_near[0], other_core)]
    ffn_far += [send(after(piece, heads_all), other_core) for piece in ffn_near[1:]]

    (
        normed_grad,
        out_own,
        *out_terms,
        hidden_own,
        grad_own,
        grad_local,
        hidden,
        dgate,
        dup,
        normed_f,
        output_part,
        ffn_gain_terms,
    ) = feed_forward(
        z_own, *rows_near, *rows_far, heads_all, gains, *ffn_near, *ffn_far
    )
    normed_grad = exchange(normed_grad, Z_GROUPS)
    ffn_near, ffn_far = kernel_call(
        ffn_grad_kernel,
        (normed_f, grad_local, hidden, dgate, dup),
        ((576, 2304, BF), (576, 2304, BF)),
        micros=6,
        room=60,
    )
    grad_hidden_one, grad_branch = kernel_call(
        branch_kernel, (normed_grad, hidden_own, grad_own, gains), ((128, DIM, F32), (128, DIM, BF))
    )
    grad_pair = send(grad_branch, z_pair)
    ffn_far = send(after(ffn_far, grad_branch), other_core)
    ffn_near, ffn_rest = merge_cores([ffn_near], [ffn_far])
    ffn_rest = send_back(ffn_rest)

    output_near, output_far = kernel_call(
        output_grad_kernel,
        (grad_branch, grad_pair, heads_low),
        ((576, HALF_Q, BF), (576, HALF_Q, BF)),
        scratch=((256, DIM, BF),),
    )
    output_far = send(output_far, other_core)
    dq, dkv, dkv_far = attend_back(
        spot, rank, queries, kv_sorted, heads_out, logs, after(grad_branch, ffn_near), grad_pair, output_part
    )
    out_terms = [after(terms, dq) for terms in out_terms]
    out_terms = [send(terms, to_z(step)) for step, terms in enumerate(out_terms, 1)]
    dkv = kernel_call(core_sum_kernel, (dkv, send(after(dkv_far, *ffn_rest), other_core)), ((2048, KV, BF),))[0]
    dkv = exchange(dkv, HX_GROUPS)
    block_out = kernel_call(out_kernel, (out_own, *out_terms), ((128, DIM, BF),))[0]
    block_out = unpick_columns(send(block_out, home(0)), order)
    attn_near, attn_far, grad_own, grad_pair = kernel_call(
        attn_grad_kernel,
        (after(dq, *out_terms), dkv, cos_table, sin_table, normed_a, attn_half, attn_other, inputs, gains, ffn_gain_terms),
        ((576, QKV, BF), (576, QKV, BF), (128, DIM, F32), (128, DIM, BF)),
        scratch=((256, QKV, BF), (DIM, QKV, BF)),
        room=60,
    )
    attn_far = send(attn_far, other_core)
    grad_pair = send(grad_pair, z_pair)
    attn_near, attn_rest = merge_cores([attn_near, output_near], [attn_far, output_far])
    attn_rest = send_back(attn_rest)
    grad_inputs = kernel_call(
        token_kernel,
        (grad_own, grad_pair, inputs, gains, grad_hidden_one),
        ((128, DIM, BF),),
    )[0]
    grad_inputs = unpick_columns(send(grad_inputs, home(0)), order)
    parts = scatter_rows((attn_near, *attn_rest, ffn_near, *ffn_rest), inner_order)

    pieces = kernel_call(split_kernel, (z_order, *parts), ((32, PIECES + 512, BF),))[0]
    pieces = exchange(pieces, Z_GROUPS)
    gain_grads, *weight_grads = kernel_call(
        finish_kernel,
        (pieces,),
        ((9, 128, F32), (9, DIM, F32), (9, KV, F32), (9, KV, F32), (9, DIM, F32)) + ((9, 3072, F32),) * 3,
    )

    return (
        block_out[None],
        grad_inputs[None],
        gain_grads[:, 64],
        *weight_grads[:4],
        gain_grads[:, 65],
        *weight_grads[4:],
    )


def unpick_columns(rows, order):
    return jnp.einsum("tk,dk->td", rows, order, preferred_element_type=F32).astype(BF)


def solution(mesh):
    weights = P(ALL, None)
    rows = P("dp", "ctx", None)
    return jax.shard_map(
        body,
        mesh=mesh,
        in_specs=(rows, rows, P(), P(ALL), weights, weights, weights, weights, P(ALL), weights, weights, weights),
        out_specs=(rows, rows, P(ALL), weights, weights, weights, weights, P(ALL), weights, weights, weights),
        check_vma=False,
    )
```

```python
import functools
import itertools

import jax
import jax.numpy as jnp
from jax import lax
from jax.experimental import pallas as pl
from jax.experimental.pallas import tpu as pltpu
from jax.sharding import PartitionSpec as P

ALL = ("dp", "ctx")
EPS = 1e-05
DIM = 1152
HEAD = 64
HALF_Q = 576
KV = 384
QKV = 1024
FF_PART = 768
FFN = 3456
PIECES = 3968
TILE = 256
BF = jnp.bfloat16
F32 = jnp.float32


def flat(l, c, h, x, z):
    return (2 * l + c) * 32 + (4 * h + x) * 4 + z


def moves(target):
    places = itertools.product(range(2), range(2), range(2), range(4), range(4))
    return [(flat(*place), flat(*target(*place))) for place in places]


def send(value, target):
    return lax.ppermute(value, ALL, moves(target))


def to_z(step):
    return lambda l, c, h, x, z: (l, c, h, x, (z + step) % 4)


def turn_by(step, first):
    def target(l, c, h, x, z):
        y = 2 * h + l
        if (c == 0) == first:
            y = (y + step) % 4
        else:
            x = (x + step) % 4
        return (y % 2, c, y // 2, x, z)

    return target


def other_core(l, c, h, x, z):
    return (l, 1 - c, h, x, z)


def z_pair(l, c, h, x, z):
    return (l, c, h, x, z ^ 1)


def home(flip):
    return lambda l, c, h, x, z: (l, z // 2, h, x, (2 * c + z % 2) ^ flip)


Z_GROUPS = [[ring * 4 + z for z in range(4)] for ring in range(8)]
CHIP_GROUPS = [
    [flat(y % 2, c, y // 2, x, z) for x in range(4) for y in range(4) for z in range(4)] for c in range(2)
]
HX_GROUPS = [[place * 4 + z for place in range(8)] for z in range(4)]


def exchange(parts, groups):
    return lax.all_to_all(parts, "ctx", 0, 0, tiled=True, axis_index_groups=groups)


def swap_halves(block):
    lane = lax.broadcasted_iota(jnp.int32, block.shape, 1) % HEAD
    return jnp.where(
        lane < HEAD // 2, pltpu.roll(block, 128 - HEAD // 2, 1), pltpu.roll(block, HEAD // 2, 1)
    )


def fill(ref, row, lane, value):
    ref[row : row + value.shape[0], lane : lane + value.shape[1]] = value


def pack_kernel(z_ref, *refs):
    arrived, sems = refs[13:21], refs[21]
    copies = [
        pltpu.make_async_copy(here, there, sems.at[index])
        for index, (here, there) in enumerate(zip(refs[:8], arrived))
    ]
    for copy in copies:
        copy.start()
    for copy in copies:
        copy.wait()
    gain_ref, q_ref, k_ref, v_ref, o_ref, gate_ref, up_ref, down_ref = arrived
    attn_ref, wide_ref = refs[8], refs[22]
    wide_ref[...] = jnp.zeros(wide_ref.shape, BF)
    for side in range(2):
        row = side * 16
        fill(wide_ref, row, 0, q_ref[:, side * 576 : side * 576 + 576])
        fill(wide_ref, row, 576, gain_ref[...])
        fill(wide_ref, row, 640, k_ref[:, side * 192 : side * 192 + 192])
        fill(wide_ref, row, 832, v_ref[:, side * 192 : side * 192 + 192])
    chunks = []
    for side in range(2):
        rows = wide_ref[side * 16 : side * 16 + 16, :].astype(F32)
        last = jnp.concatenate([rows[8:9, part * 128 : part * 128 + 128] for part in range(8)], axis=0)
        chunks.append(jnp.concatenate([rows[:8], last], axis=1))
    both = jnp.concatenate(chunks, axis=0).astype(BF)

    def copy_both(index, carry):
        attn_ref[pl.ds(pl.multiple_of(index * 16, 16), 16), :] = both
        return carry

    lax.fori_loop(0, 32, copy_both, 0)
    for step in range(4):
        ffn_ref = refs[9 + step]
        ffn_ref[...] = jnp.zeros((16, FFN), BF)
        start = pl.multiple_of(((z_ref[0] + step) % 4) * FF_PART, FF_PART)
        fill(ffn_ref, 0, 0, gate_ref[:, pl.ds(start, FF_PART)])
        fill(ffn_ref, 0, 768, up_ref[:, pl.ds(start, FF_PART)])
        fill(ffn_ref, 0, 1536, down_ref[:, pl.ds(start, FF_PART)])
        fill(ffn_ref, 0, 2304, o_ref[...])


def unpack_kernel(all_ref, order_ref, last_order_ref, out_ref, tail_ref):
    tail_ref[...] = all_ref[:, QKV:].astype(F32)
    last = jnp.concatenate([tail_ref[pl.ds(part, 64, stride=8), :] for part in range(8)], axis=1)
    out_ref[...] = (
        jnp.dot(order_ref[...], all_ref[:, :QKV], preferred_element_type=F32)
        + jnp.dot(last_order_ref[...], last.astype(BF), preferred_element_type=F32)
    ).astype(BF)


def qkv_kernel(
    own_ref, pair_ref, half_ref, other_ref, cos_ref, sin_ref,
    x_ref, normed_ref, q_ref, kv_ref, gain_ref, weight_ref,
):
    x_ref[0:128, :] = own_ref[:, 0:DIM]
    x_ref[128:256, :] = pair_ref[:, 0:DIM]
    weight_ref[0:576, :] = half_ref[...]
    weight_ref[576:1152, :] = other_ref[...]
    inputs = x_ref[...].astype(F32)
    lane = lax.broadcasted_iota(jnp.int32, (8, 128), 1)
    row = lax.broadcasted_iota(jnp.int32, (8, 128), 0)
    gains = lax.dot_general(
        (lane == row + 64).astype(BF), weight_ref[:, 512:640], NT, preferred_element_type=F32
    )
    gain_ref[...] = gains
    inverse = lax.rsqrt(jnp.mean(inputs * inputs, axis=-1, keepdims=True) + EPS)
    normed = (inputs * inverse * gains[0:1]).astype(BF)
    normed_ref[...] = normed
    proj = jnp.dot(normed, weight_ref[...], preferred_element_type=F32)
    cos_table, sin_table = cos_ref[...], sin_ref[...]
    kv_parts = []
    for start in range(0, QKV, 128):
        block = proj[:, start : start + 128]
        turned = block * cos_table + swap_halves(block) * sin_table
        if start < 512:
            q_ref[:, start : start + 128] = (turned * 0.125).astype(BF)
        elif start == 512:
            q_ref[:, 512:576] = (turned[:, :64] * 0.125).astype(BF)
        elif start == 640:
            kv_parts.append(turned.astype(BF))
        elif start == 768:
            side = lax.broadcasted_iota(jnp.int32, block.shape, 1)
            kv_parts.append(jnp.where(side < HEAD, turned, block).astype(BF))
        else:
            kv_parts.append(block.astype(BF))
    for copy in range(8):
        for part in range(3):
            fill(kv_ref, copy * 256, part * 128, kv_parts[part])


def stack_heads(block, kv_head, upper):
    parts = []
    for group in range(3):
        start = (kv_head * 3 + group) * HEAD
        parts.append(block[:, start : start + HEAD])
    rows = jnp.concatenate(parts, axis=0)
    zeros = jnp.zeros_like(rows)
    return jnp.concatenate([zeros, rows] if upper else [rows, zeros], axis=1)


K_GROUP = (0, 0, 128)
K_UPPER = (False, True, False)
V_GROUP = (128, 256, 256)
V_UPPER = (True, False, True)
NT = (((1,), (1,)), ((), ()))
TN = (((0,), (0,)), ((), ()))


def mask_rows(scores, place, tile):
    row = lax.broadcasted_iota(jnp.int32, scores.shape, 0) % 64 + place * 64
    key = lax.broadcasted_iota(jnp.int32, scores.shape, 1) + tile * TILE
    return jnp.where(key <= row, scores, -1e30)


def over_tiles(rank_ref, step, carry):
    first = jnp.int32(0)
    for count in (4, 3, 2, 1):
        last = rank_ref[count - 1] // 4
        carry = lax.fori_loop(first, last, functools.partial(step, count=count, masked=False), carry)
        carry = lax.cond(
            first <= last,
            functools.partial(step, last, count=count, masked=True),
            lambda value: value,
            carry,
        )
        first = last + 1
    return carry


def stack_blocks(rank_ref, ref, target_ref, uppers):
    for rank in range(4):
        rows = ref[pl.ds(pl.multiple_of(rank_ref[4 + rank] * 64, 64), 64), :]
        for head in range(3):
            target_ref[head, rank * 192 : rank * 192 + 192, :] = stack_heads(rows, head, uppers[head])


def attend_kernel(
    spot_ref, rank_ref, side_ref, q_ref, near_ref, far_ref,
    out_ref, log_ref, sorted_ref, low_ref, score_ref, stack_ref, top_ref, sum_ref, total_ref,
):
    def put(index, carry):
        here = pl.ds(pl.multiple_of(index * 64, 64), 64)
        sorted_ref[pl.ds(pl.multiple_of(spot_ref[index] * 64, 64), 64), :] = near_ref[here, :]
        sorted_ref[pl.ds(pl.multiple_of(spot_ref[index + 32] * 64, 64), 64), :] = far_ref[here, :]
        return carry

    lax.fori_loop(0, 32, put, 0, unroll=4)
    stack_blocks(rank_ref, q_ref, stack_ref, K_UPPER)
    top_ref[...] = jnp.full(top_ref.shape, -1e30, F32)

    def score(tile, base, count, masked):
        span = pl.ds(pl.multiple_of(tile * TILE, TILE), TILE)
        for head in range(3):
            keys = sorted_ref[span, K_GROUP[head] : K_GROUP[head] + 128]
            for rank in range(count):
                rows = slice(rank * 192, rank * 192 + 192)
                scores = lax.dot_general(
                    stack_ref[head, rows, :], keys, NT, preferred_element_type=F32
                )
                if masked:
                    scores = mask_rows(scores, rank_ref[rank], tile)
                score_ref[head, base + rank] = scores
                top_ref[head, rows, :] = jnp.maximum(
                    top_ref[head, rows, :], jnp.maximum(scores[:, :128], scores[:, 128:])
                )
        return base + count

    over_tiles(rank_ref, score, jnp.int32(0))
    for head in range(3):
        top_ref[head] = jnp.broadcast_to(jnp.max(top_ref[head], axis=1, keepdims=True), (768, 128))
    sum_ref[...] = jnp.zeros(sum_ref.shape, F32)
    total_ref[...] = jnp.zeros(total_ref.shape, F32)

    def weigh(tile, base, count, masked):
        span = pl.ds(pl.multiple_of(tile * TILE, TILE), TILE)
        for head in range(3):
            values = sorted_ref[span, V_GROUP[head] : V_GROUP[head] + 128]
            for rank in range(count):
                rows = slice(rank * 192, rank * 192 + 192)
                scores = score_ref[head, base + rank]
                top = top_ref[head, rows, :]
                left = jnp.exp(scores[:, :128] - top)
                right = jnp.exp(scores[:, 128:] - top)
                total_ref[head, rows, :] += left + right
                weights = jnp.concatenate([left.astype(BF), right.astype(BF)], axis=1)
                sum_ref[head, rows, :] += jnp.dot(weights, values, preferred_element_type=F32)
        return base + count

    over_tiles(rank_ref, weigh, jnp.int32(0))
    for head in range(3):
        row_total = jnp.sum(total_ref[head], axis=1, keepdims=True)
        log_ref[head] = top_ref[head] + jnp.log(row_total)
        result = sum_ref[head] / row_total
        side = result[:, 64:] if V_UPPER[head] else result[:, :64]
        for rank in range(4):
            rows = pl.ds(pl.multiple_of(rank_ref[4 + rank] * 64, 64), 64)
            for group in range(3):
                start = (head * 3 + group) * HEAD
                row = rank * 192 + group * 64
                out_ref[rows, start : start + HEAD] = side[row : row + 64]
    side = side_ref[0]
    for copy in range(4):
        for block in range(2):
            start = pl.multiple_of(copy * 256 + (block ^ side) * 128, 128)
            low_ref[pl.ds(start, 128), 0:576] = out_ref[block * 128 : block * 128 + 128, :].astype(BF)
            low_ref[pl.ds(start, 128), 576:640] = jnp.zeros((128, 64), BF)


def attend_back_kernel(
    spot_ref, rank_ref, q_ref, sorted_ref, out_ref, log_ref, own_ref, pair_ref, part_ref,
    dq_ref, near_ref, far_ref,
    total_ref, rows_ref, grad_ref, stack_ref, grads_ref, delta_ref, prob_ref, dscore_ref, dq_sum_ref,
):
    rows_ref[0:128, :] = own_ref[...]
    rows_ref[128:256, :] = pair_ref[...]
    grad_ref[...] = jnp.dot(rows_ref[...], part_ref[...], preferred_element_type=F32).astype(BF)
    total_ref[...] = jnp.zeros_like(total_ref)
    dq_sum_ref[...] = jnp.zeros_like(dq_sum_ref)
    stack_blocks(rank_ref, q_ref, stack_ref, K_UPPER)
    stack_blocks(rank_ref, grad_ref, grads_ref, V_UPPER)
    for rank in range(4):
        rows = pl.ds(pl.multiple_of(rank_ref[4 + rank] * 64, 64), 64)
        products = grad_ref[rows, :].astype(F32) * out_ref[rows, :]
        for head in range(3):
            delta_ref[head, rank * 192 : rank * 192 + 192, :] = jnp.broadcast_to(
                jnp.sum(stack_heads(products, head, False), axis=1, keepdims=True), (192, 128)
            )

    def step(tile, carry, count, masked):
        span = pl.ds(pl.multiple_of(tile * TILE, TILE), TILE)
        size = count * 192
        for head in range(3):
            k_lanes = slice(K_GROUP[head], K_GROUP[head] + 128)
            v_lanes = slice(V_GROUP[head], V_GROUP[head] + 128)
            keys, values = sorted_ref[span, k_lanes], sorted_ref[span, v_lanes]
            scores_all = lax.dot_general(stack_ref[head, :size, :], keys, NT, preferred_element_type=F32)
            grad_all = lax.dot_general(grads_ref[head, :size, :], values, NT, preferred_element_type=F32)
            for rank in range(count):
                rows = slice(rank * 192, rank * 192 + 192)
                scores = scores_all[rows]
                if masked:
                    scores = mask_rows(scores, rank_ref[rank], tile)
                logs, delta = log_ref[head, rows, :], delta_ref[head, rows, :]
                for lane in (0, 128):
                    lanes = slice(lane, lane + 128)
                    prob = jnp.exp(scores[:, lanes] - logs)
                    prob_ref[head, rows, lanes] = prob.astype(BF)
                    dscore_ref[head, rows, lanes] = (prob * (grad_all[rows, lanes] - delta)).astype(BF)
        for head in range(3):
            k_lanes = slice(K_GROUP[head], K_GROUP[head] + 128)
            v_lanes = slice(V_GROUP[head], V_GROUP[head] + 128)
            keys = sorted_ref[span, k_lanes]
            dq_sum_ref[head, :size, :] += jnp.dot(
                dscore_ref[head, :size, :], keys, preferred_element_type=F32
            )
            total_ref[span, v_lanes] += lax.dot_general(
                prob_ref[head, :size, :], grads_ref[head, :size, :], TN, preferred_element_type=F32
            )
            total_ref[span, k_lanes] += lax.dot_general(
                dscore_ref[head, :size, :], stack_ref[head, :size, :], TN, preferred_element_type=F32
            )
        return carry

    over_tiles(rank_ref, step, jnp.int32(0))
    for head in range(3):
        for rank in range(4):
            rows = pl.ds(pl.multiple_of(rank_ref[4 + rank] * 64, 64), 64)
            for group in range(3):
                start = (head * 3 + group) * HEAD
                row = rank * 192 + group * 64
                block = dq_sum_ref[head, row : row + 64, :] * 0.125
                side = block[:, 64:] if K_UPPER[head] else block[:, :64]
                dq_ref[rows, start : start + HEAD] = side

    def put(index, carry):
        there = pl.ds(pl.multiple_of(index * 64, 64), 64)
        origin = pl.ds(pl.multiple_of(spot_ref[index] * 64, 64), 64)
        near_ref[there, :] = total_ref[origin, :].astype(BF)
        origin = pl.ds(pl.multiple_of(spot_ref[index + 32] * 64, 64), 64)
        far_ref[there, :] = total_ref[origin, :].astype(BF)
        return carry

    lax.fori_loop(0, 32, put, 0, unroll=4)


def rows_kernel(x_ref, grad_ref, order_ref, out_ref):
    for side, rows_ref in enumerate((x_ref, grad_ref)):
        out_ref[:, side * DIM : side * DIM + DIM] = jnp.dot(
            rows_ref[...], order_ref[...], preferred_element_type=F32
        ).astype(BF)


def ffn_kernel(
    z_ref, rows0_ref, rows1_ref, rows2_ref, rows3_ref, heads_ref, gain_ref,
    w0_ref, w1_ref, w2_ref, w3_ref, w4_ref, w5_ref, w6_ref, w7_ref,
    dn_ref, out0_ref, out1_ref, out2_ref, out3_ref, own_ref, grad_own_ref,
    grad_out, hidden_out, dgate_out, dup_out, normed_out, part_ref, gain_grad_ref,
    grad_ref, hidden_ref, dgate_ref, dup_ref, normed_ref, w_ref, scaled_ref, heads_all_ref, h1_ref, dn_sum_ref, out_sum_ref, gate_ref, up_ref, dh_ref, sems,
):
    pieces = (w0_ref, w1_ref, w2_ref, w3_ref, w4_ref, w5_ref, w6_ref, w7_ref)
    copies = [
        pltpu.make_async_copy(
            piece.at[:, pl.ds(lane, width)],
            w_ref.at[pl.ds(index * 144, 144), pl.ds(lane, width)],
            sems.at[8 * turn + index],
        )
        for turn, (lane, width) in enumerate(((2304, 1152), (0, 2304)))
        for index, piece in enumerate(pieces)
    ]
    for copy in copies:
        copy.start()
    z = z_ref[0]
    for slot, rows_ref in enumerate((rows0_ref, rows1_ref, rows2_ref, rows3_ref)):
        here = pl.ds(pl.multiple_of((z ^ slot) * 128, 128), 128)
        h1_ref[here, :] = rows_ref[:, 0:DIM].astype(F32)
        grad_ref[here, :] = rows_ref[:, DIM:]
    for side in range(2):
        for half in range(2):
            start = (2 * side + half) * 256
            heads_all_ref[side * 256 : side * 256 + 256, half * 576 : half * 576 + 576] = heads_ref[
                start : start + 256, 0:576
            ]
    for copy in copies[:8]:
        copy.wait()
    heads = heads_all_ref[...]
    h1_ref[...] += lax.dot_general(heads, w_ref[:, 2304:3456], NT, preferred_element_type=F32)

    def norm(index, carry):
        here = pl.ds(pl.multiple_of(index * 64, 64), 64)
        rows = h1_ref[here, :]
        inverse = lax.rsqrt(jnp.mean(rows * rows, axis=-1, keepdims=True) + EPS)
        scaled = rows * inverse
        scaled_ref[here, :] = scaled.astype(BF)
        normed_ref[here, :] = (scaled * gain_ref[1:2, :]).astype(BF)
        return carry

    lax.fori_loop(0, 8, norm, 0)
    here = pl.ds(pl.multiple_of(z * 128, 128), 128)
    own_ref[...] = h1_ref[here, :]
    grad_own_ref[...] = grad_ref[here, :]
    for copy in copies[8:]:
        copy.wait()
    outs = [
        pltpu.make_async_copy(here_ref, there_ref, sems.at[16 + index])
        for index, (here_ref, there_ref) in enumerate(
            (
                (normed_ref, normed_out),
                (grad_ref, grad_out),
                (hidden_ref, hidden_out),
                (dgate_ref, dgate_out),
                (dup_ref, dup_out),
            )
        )
    ]
    outs[0].start()
    outs[1].start()
    normed, grads = normed_ref[...], grad_ref[...]
    for index in range(3):
        start = index * 256
        gate_ref[index] = jnp.dot(normed, w_ref[:, start : start + 256], preferred_element_type=F32)
        up_ref[index] = jnp.dot(normed, w_ref[:, start + 768 : start + 1024], preferred_element_type=F32)
        dh_ref[index] = jnp.dot(grads, w_ref[:, start + 1536 : start + 1792], preferred_element_type=F32)
        there = slice(start, start + 256)
        for block in range(8):
            rows = slice(block * 64, block * 64 + 64)
            gate, up, grad = gate_ref[index, rows, :], up_ref[index, rows, :], dh_ref[index, rows, :]
            sigmoid = jax.nn.sigmoid(gate)
            active = gate * sigmoid
            hidden_ref[rows, there] = (active * up).astype(BF)
            dgate_ref[rows, there] = (grad * up * sigmoid * (1.0 + gate * (1.0 - sigmoid))).astype(BF)
            dup_ref[rows, there] = (grad * active).astype(BF)
    for copy in outs[2:]:
        copy.start()
    hidden, dgate, dup = hidden_ref[...], dgate_ref[...], dup_ref[...]
    for first in range(0, DIM, 1152):
        rows = slice(first, first + 1152)
        dn_sum_ref[:, rows] = lax.dot_general(
            dgate, w_ref[rows, 0:768], NT, preferred_element_type=F32
        ) + lax.dot_general(dup, w_ref[rows, 768:1536], NT, preferred_element_type=F32)
        out_sum_ref[:, rows] = lax.dot_general(
            hidden, w_ref[rows, 1536:2304], NT, preferred_element_type=F32
        )

    def finish(index, total):
        here = pl.ds(pl.multiple_of(index * 64, 64), 64)
        grad = dn_sum_ref[here, :]
        dn_ref[here, :] = grad.astype(BF)
        terms = grad * scaled_ref[here, :].astype(F32)
        return total + jnp.sum(terms.reshape(8, 8, DIM), axis=0)

    gain_grad_ref[...] = lax.fori_loop(0, 8, finish, jnp.zeros((8, DIM), F32))

    out0_ref[...] = own_ref[...] + out_sum_ref[here, :]
    for step, out_ref in enumerate((out1_ref, out2_ref, out3_ref)):
        there = pl.ds(pl.multiple_of(((z + step + 1) % 4) * 128, 128), 128)
        out_ref[...] = out_sum_ref[there, :].astype(BF)

    @pl.when(z % 2 == 0)
    def _():
        part_ref[...] = w_ref[:, 2304:2880]

    @pl.when(z % 2 == 1)
    def _():
        part_ref[...] = w_ref[:, 2880:3456]

    for copy in outs:
        copy.wait()


def outer_products(lefts, rights, near_ref, far_ref, extra=None):
    for start in range(0, DIM, 128):
        lane = 0
        for left, right in zip(lefts, rights):
            block = lax.dot_general(
                left[:, start : start + 128], right[...], TN, preferred_element_type=F32
            )
            if extra is not None:
                block = extra(start, block)
            block = block.astype(near_ref.dtype)
            width = block.shape[1]
            lanes = slice(lane, lane + width)
            if start < 512:
                near_ref[start : start + 128, lanes] = block
            elif start == 512:
                near_ref[512:576, lanes] = block[:64]
                far_ref[0:64, lanes] = block[64:].astype(BF)
            else:
                far_ref[start - 576 : start - 448, lanes] = block.astype(BF)
            lane += width


def ffn_grad_kernel(normed_ref, grad_ref, hidden_ref, dgate_ref, dup_ref, near_ref, far_ref):
    outer_products(
        (normed_ref, normed_ref, grad_ref), (dgate_ref, dup_ref, hidden_ref), near_ref, far_ref
    )


def output_grad_kernel(own_ref, pair_ref, heads_ref, near_ref, far_ref, rows_ref):
    rows_ref[0:128, :] = own_ref[...]
    rows_ref[128:256, :] = pair_ref[...]
    outer_products((rows_ref,), (heads_ref,), near_ref, far_ref)


def merge_kernel(*refs):
    count = len(refs) // 2 - 2
    targets = refs[2 * count :]
    for index in range(4):
        lane = 0
        for near_ref, far_ref in zip(refs[:count], refs[count : 2 * count]):
            width = near_ref.shape[1]
            rows = slice(index * 144, index * 144 + 144)
            total = near_ref[rows, :].astype(F32) + far_ref[rows, :].astype(F32)
            targets[index][:, lane : lane + width] = total.astype(targets[index].dtype)
            lane += width


def spread_kernel(order_ref, *refs):
    targets = refs[-4:]
    first = 0
    for group in range(2):
        near_ref, *others = refs[4 * group : 4 * group + 4]
        count = near_ref.shape[1]
        for start in range(0, count, 512):
            lanes = slice(start, min(start + 512, count))
            total = near_ref[:, lanes]
            for other_ref in others:
                total = total + other_ref[:, lanes].astype(F32)
            parts = lax.dot_general(order_ref[...], total.astype(BF), TN, preferred_element_type=F32)
            there = slice(first + lanes.start, first + lanes.stop)
            for index in range(4):
                targets[index][:, there] = parts[index * 40 : index * 40 + 40].astype(BF)
        first += count
        if first % 128:
            for target in targets:
                target[:, first : first + 64] = jnp.zeros((40, 64), BF)
            first += 64


def split_kernel(order_ref, near_ref, a_ref, b_ref, c_ref, target):
    lasts = []
    for start in range(0, PIECES, 512):
        lanes = slice(start, min(start + 512, PIECES))
        total = near_ref[:, lanes].astype(F32) + a_ref[:, lanes].astype(F32)
        total = total + b_ref[:, lanes].astype(F32) + c_ref[:, lanes].astype(F32)
        parts = lax.dot_general(order_ref[...], total.astype(BF), TN, preferred_element_type=F32)
        rows = jnp.concatenate([parts[part * 16 : part * 16 + 8] for part in range(4)], axis=0)
        target[:, lanes] = rows.astype(BF)
        last = jnp.concatenate([parts[part * 16 + 8 : part * 16 + 9] for part in range(4)], axis=0)
        rest = 512 - last.shape[1]
        if rest:
            last = jnp.concatenate([last, jnp.zeros((4, rest), F32)], axis=1)
        lasts.append(last)
    tail = jnp.concatenate([last[part : part + 1] for part in range(4) for last in lasts], axis=0)
    target[:, PIECES:] = tail.astype(BF)


def core_sum_kernel(near_ref, far_ref, out_ref):
    out_ref[...] = (near_ref[...].astype(F32) + far_ref[...].astype(F32)).astype(BF)


def branch_kernel(terms_ref, own_ref, grad_ref, gain_ref, full_ref, low_ref):
    grad = terms_ref[0:128, :].astype(F32)
    for part in range(1, 4):
        grad = grad + terms_ref[part * 128 : part * 128 + 128, :].astype(F32)
    rows = own_ref[...]
    inverse = lax.rsqrt(jnp.mean(rows * rows, axis=-1, keepdims=True) + EPS)
    scaled = rows * inverse
    grad = grad * gain_ref[1:2, :]
    grad = inverse * (grad - scaled * jnp.mean(grad * scaled, axis=-1, keepdims=True))
    grad = grad + grad_ref[...].astype(F32)
    full_ref[...] = grad
    low_ref[...] = grad.astype(BF)


def out_kernel(own_ref, a_ref, b_ref, c_ref, out_ref):
    total = own_ref[...] + a_ref[...].astype(F32)
    out_ref[...] = (total + b_ref[...].astype(F32) + c_ref[...].astype(F32)).astype(BF)


def attn_grad_kernel(
    dq_ref, dkv_ref, cos_ref, sin_ref, normed_ref, half_ref, other_ref, x_ref, gain_ref, ffn_gain_ref,
    near_ref, far_ref, own_ref, pair_ref, grad_ref, weight_ref,
):
    weight_ref[0:576, :] = half_ref[...]
    weight_ref[576:1152, :] = other_ref[...]
    cos_table, sin_table = cos_ref[...], sin_ref[...]

    def turn(block):
        return block * cos_table - swap_halves(block) * sin_table

    def summed(start):
        total = dkv_ref[0:256, start : start + 128].astype(F32)
        for part in range(1, 8):
            total = total + dkv_ref[part * 256 : part * 256 + 256, start : start + 128].astype(F32)
        return total

    for start in range(0, 512, 128):
        grad_ref[:, start : start + 128] = turn(dq_ref[:, start : start + 128]).astype(BF)
    tail = dq_ref[:, 512:576]
    wide = jnp.concatenate([tail, jnp.zeros_like(tail)], axis=1)
    grad_ref[:, 512:640] = turn(wide).astype(BF)
    grad_ref[:, 640:768] = turn(summed(0)).astype(BF)
    block = summed(128)
    lane = lax.broadcasted_iota(jnp.int32, block.shape, 1)
    grad_ref[:, 768:896] = jnp.where(lane < HEAD, turn(block), block).astype(BF)
    grad_ref[:, 896:1024] = summed(256).astype(BF)
    grads = lax.dot_general(grad_ref[...], weight_ref[...], NT, preferred_element_type=F32)
    own_ref[...] = grads[:128]
    pair_ref[...] = grads[128:].astype(BF)
    rows = x_ref[...].astype(F32)
    inverse = lax.rsqrt(jnp.mean(rows * rows, axis=-1, keepdims=True) + EPS)
    attn_terms = jnp.sum(grads * (rows * inverse), axis=0, keepdims=True)
    ffn_terms = jnp.sum(ffn_gain_ref[...], axis=0, keepdims=True)
    parts = []
    for terms in (attn_terms, ffn_terms):
        high = terms.astype(BF)
        parts.append(high.astype(F32))
        parts.append(terms - high.astype(F32))
    row = lax.broadcasted_iota(jnp.int32, (16, DIM), 0)
    gains = jnp.zeros((16, DIM), F32)
    for index, part in enumerate(parts):
        gains = jnp.where(row == index, part, gains)
    gains = gains.astype(BF)
    place_row = lax.broadcasted_iota(jnp.int32, (16, 128), 0)
    place_lane = lax.broadcasted_iota(jnp.int32, (16, 128), 1)
    places = ((place_lane == 64 + place_row // 2) & (place_row < 4)).astype(BF)

    def extra(start, block):
        columns = lax.dot_general(
            gains[:, start : start + 128], places, TN, preferred_element_type=F32
        )
        return jnp.concatenate([block[:, :512], block[:, 512:640] + columns, block[:, 640:]], axis=1)

    outer_products((normed_ref,), (grad_ref,), near_ref, far_ref, extra)


def token_kernel(own_ref, pair_ref, x_ref, gain_ref, full_ref, out_ref):
    grad = own_ref[...] + pair_ref[...].astype(F32)
    rows = x_ref[0:128, :].astype(F32)
    inverse = lax.rsqrt(jnp.mean(rows * rows, axis=-1, keepdims=True) + EPS)
    scaled = rows * inverse
    grad = grad * gain_ref[0:1, :]
    grad = inverse * (grad - scaled * jnp.mean(grad * scaled, axis=-1, keepdims=True))
    out_ref[...] = (full_ref[...] + grad).astype(BF)


def finish_kernel(pieces_ref, gain_ref, q_ref, k_ref, v_ref, o_ref, gate_ref, up_ref, down_ref):
    wholes = []
    pieces = pieces_ref[...].astype(F32)
    for part in range(4):
        rows = pieces[part * 8 : part * 8 + 8]
        last = jnp.concatenate([rows[index : index + 1, PIECES:] for index in range(8)], axis=1)
        wholes.append(jnp.concatenate([rows[:, :PIECES], last[:, :PIECES]], axis=0))
    for side in range(2):
        total = wholes[side][:, :1600] + wholes[side + 2][:, :1600]
        q_ref[:, side * 576 : side * 576 + 576] = total[:, 0:576]
        k_ref[:, side * 192 : side * 192 + 192] = total[:, 640:832]
        v_ref[:, side * 192 : side * 192 + 192] = total[:, 832:1024]
        o_ref[:, side * 576 : side * 576 + 576] = total[:, 1024:1600]
        if side == 0:
            gain_ref[...] = total[:, 512:640]
        else:
            gain_ref[...] += total[:, 512:640]
    for part in range(4):
        lanes = slice(part * FF_PART, part * FF_PART + FF_PART)
        gate_ref[:, lanes] = wholes[part][:, 1664:2432]
        up_ref[:, lanes] = wholes[part][:, 2432:3200]
        down_ref[:, lanes] = wholes[part][:, 3200:3968]


VMEM = pl.BlockSpec(memory_space=pltpu.VMEM)
SMEM = pl.BlockSpec(memory_space=pltpu.SMEM)
HBM = pl.BlockSpec(memory_space=pltpu.HBM)


def takes(microseconds):
    return pl.CostEstimate(flops=int(microseconds * 6e8), bytes_accessed=1 << 20, transcendentals=0)


def shapes(*sizes):
    return tuple(jax.ShapeDtypeStruct(size[:-1], size[-1]) for size in sizes)


def kernel_call(kernel, ins, outs, scalars=0, scratch=(), micros=3, far=(), sems=0, far_outs=(), room=6, late=()):
    specs = [SMEM if index < scalars else HBM if index in far else VMEM for index in range(len(ins))]
    scratch_shapes = [pltpu.VMEM(size[:-1], size[-1]) for size in scratch]
    if sems:
        scratch_shapes.append(pltpu.SemaphoreType.DMA((sems,)))
    scratch_shapes += [pltpu.VMEM(size[:-1], size[-1]) for size in late]
    return pl.pallas_call(
        kernel,
        out_shape=shapes(*outs),
        in_specs=specs,
        out_specs=tuple(HBM if index in far_outs else VMEM for index in range(len(outs))),
        scratch_shapes=scratch_shapes,
        compiler_params=pltpu.CompilerParams(vmem_limit_bytes=room * 1024 * 1024),
        cost_estimate=takes(micros),
    )(*ins)


def pack(z, *weights):
    return kernel_call(
        pack_kernel,
        (z,) + weights,
        ((512, DIM, BF),) + ((16, FFN, BF),) * 4,
        scalars=1,
        scratch=[weight.shape + (BF,) for weight in weights],
        far=range(1, 9),
        sems=8,
        room=60,
        late=((32, QKV, BF),),
    )


def feed_forward(*ins):
    return kernel_call(
        ffn_kernel,
        ins,
        (
            (512, DIM, BF),
            (128, DIM, F32),
            (128, DIM, BF),
            (128, DIM, BF),
            (128, DIM, BF),
            (128, DIM, F32),
            (128, DIM, BF),
            (512, DIM, BF),
            (512, FF_PART, BF),
            (512, FF_PART, BF),
            (512, FF_PART, BF),
            (512, DIM, BF),
            (DIM, HALF_Q, BF),
            (8, DIM, F32),
        ),
        scalars=1,
        scratch=(
            (512, DIM, BF),
            (512, FF_PART, BF),
            (512, FF_PART, BF),
            (512, FF_PART, BF),
            (512, DIM, BF),
            (DIM, FFN, BF),
            (512, DIM, BF),
            (512, DIM, BF),
            (512, DIM, F32),
            (512, DIM, F32),
            (512, DIM, F32),
            (3, 512, 256, F32),
            (3, 512, 256, F32),
            (3, 512, 256, F32),
        ),
        far=range(7, 15),
        far_outs=range(7, 12),
        sems=21,
        micros=15,
        room=60,
    )


def project(*ins):
    return kernel_call(
        qkv_kernel,
        ins,
        (
            (256, DIM, BF),
            (256, DIM, BF),
            (256, HALF_Q, BF),
            (2048, KV, BF),
            (8, DIM, F32),
        ),
        scratch=((DIM, QKV, BF),),
        room=60,
    )


def attend(*ins):
    return kernel_call(
        attend_kernel,
        ins,
        ((256, HALF_Q, F32), (3, 768, 128, F32), (4096, KV, BF), (1024, 640, BF)),
        scalars=3,
        scratch=((3, 34, 192, TILE, F32), (3, 768, 128, BF)) + ((3, 768, 128, F32),) * 3,
        micros=20,
        room=30,
    )


def attend_back(*ins):
    return kernel_call(
        attend_back_kernel,
        ins,
        ((256, HALF_Q, F32), (2048, KV, BF), (2048, KV, BF)),
        scalars=2,
        scratch=(
            (4096, KV, F32),
            (256, DIM, BF),
            (256, HALF_Q, BF),
            (3, 768, 128, BF),
            (3, 768, 128, BF),
            (3, 768, 128, F32),
            (3, 768, TILE, BF),
            (3, 768, TILE, BF),
            (3, 768, 128, F32),
        ),
        micros=40,
        room=20,
    )


def pick(matrix, value):
    return jnp.dot(matrix, value, preferred_element_type=F32).astype(BF)


def send_turn(block, first):
    return [send(block, turn_by(step, first)) for step in (1, 3, 2)]


def merge_cores(nears, fars):
    width = sum(near.shape[1] for near in nears)
    near, *rest = kernel_call(
        merge_kernel, tuple(nears) + tuple(fars), ((144, width, F32),) + ((144, width, BF),) * 3
    )
    return near, rest


def send_back(parts):
    return [send(part, turn_by(-step, False)) for part, step in zip(parts, (1, 3, 2))]


def scatter_rows(groups, inner_order):
    near, *rest = kernel_call(
        spread_kernel, (inner_order, *groups), ((40, PIECES, BF),) * 4
    )
    return [near] + [send(part, turn_by(-step, True)) for part, step in zip(rest, (1, 3, 2))]


def rope_tables(positions):
    lane = jnp.arange(128, dtype=jnp.int32)
    inverse = 1.0 / 10000.0 ** ((lane % 32).astype(F32) * (2.0 / HEAD))
    angles = positions.astype(F32)[:, None] * inverse[None, :]
    sign = jnp.where(lane % HEAD < HEAD // 2, -1.0, 1.0)
    return (jnp.cos(angles), jnp.sin(angles) * sign[None, :])


def after(value, *others):
    return lax.optimization_barrier((value,) + others)[0]


def one_hot(rows, columns):
    return (rows == columns).astype(BF)


def body(
    tokens,
    grad_out,
    pair_order,
    attn_gain,
    query_weight,
    key_weight,
    value_weight,
    output_weight,
    ffn_gain,
    gate_weight,
    up_weight,
    down_weight,
):
    dp, ctx = lax.axis_index("dp"), lax.axis_index("ctx")
    l, c = dp // 2, dp % 2
    h, x, z = ctx // 16, (ctx // 4) % 4, ctx % 4
    y, b = 2 * h + l, z % 2
    even = b == 0

    local = jnp.arange(DIM, dtype=jnp.int32)
    from_c = (local // 576) ^ (z // 2)
    turns = jnp.array([0, 1, 3, 2], jnp.int32)
    outer, inner = turns[(local // 144) % 4], turns[(local // 36) % 4]
    from_x = (x - jnp.where(from_c == 0, outer, inner)) % 4
    from_y = (y - jnp.where(from_c == 0, inner, outer)) % 4
    from_z = (local // 9) % 4
    owner = (2 * (from_y % 2) + from_c) * 32 + (4 * (from_y // 2) + from_x) * 4 + from_z
    natural = owner * 9 + local % 9
    order = one_hot(jnp.arange(DIM, dtype=jnp.int32)[:, None], natural[None, :])
    rows40 = jnp.arange(40, dtype=jnp.int32)
    z_order = one_hot(
        jnp.where(rows40 < 36, (rows40 // 9) * 16 + rows40 % 9, -1)[:, None],
        jnp.arange(64, dtype=jnp.int32)[None, :],
    )
    z_arrival = one_hot(
        jnp.where(rows40 < 36, ((z - rows40 // 9) % 4) * 16 + rows40 % 9, -1)[:, None],
        jnp.arange(64, dtype=jnp.int32)[None, :],
    )
    rows144 = jnp.arange(144, dtype=jnp.int32)
    inner_order = one_hot(
        ((rows144 // 36) * 40 + rows144 % 36)[:, None], jnp.arange(160, dtype=jnp.int32)[None, :]
    )
    chunk = jnp.arange(64, dtype=jnp.int32)
    chunk_ctx = (
        ((chunk // 4) % 8) * 4
        + 2 * ((chunk // 32) ^ c)
        + ((chunk // 2) % 2 ^ b)
    )
    ctx_match = chunk_ctx[:, None] == jnp.arange(32, dtype=jnp.int32)[None, :]
    chunk_pair = jnp.sum(jnp.where(ctx_match, pair_order[None, :], 0), axis=1)
    spot = jnp.where(chunk % 2 == 0, chunk_pair, 63 - chunk_pair)
    place = lax.dynamic_slice_in_dim(spot, (4 * h + x) * 4, 4)
    ahead = jnp.sum((place[None, :] > place[:, None]).astype(jnp.int32), axis=1)
    at_rank = ahead[None, :] == jnp.arange(4, dtype=jnp.int32)[:, None]
    rank = jnp.concatenate(
        [
            jnp.sum(jnp.where(at_rank, place[None, :], 0), axis=1),
            jnp.sum(jnp.where(at_rank, jnp.arange(4, dtype=jnp.int32)[None, :], 0), axis=1),
        ]
    )
    positions = (place[:, None] * 64 + jnp.arange(64, dtype=jnp.int32)[None, :]).reshape(256)
    cos_table, sin_table = rope_tables(positions)


    z_own = jnp.reshape(z, (1,))
    attn_send, *ffn_send = pack(
        z_own,
        jnp.stack([attn_gain, ffn_gain], axis=1),
        query_weight,
        key_weight,
        value_weight,
        output_weight,
        gate_weight,
        up_weight,
        down_weight,
    )
    rows_both = kernel_call(
        rows_kernel, (after(tokens[0], attn_send), grad_out[0], order), ((128, 2 * DIM, BF),)
    )[0]
    rows_near = [send(rows_both, home(flip)) for flip in (0, 1)]
    ffn_all = [ffn_send[0]] + [send(ffn_send[step], to_z(step)) for step in (1, 2, 3)]
    attn_all = lax.all_to_all(attn_send, ALL, 0, 0, tiled=True, axis_index_groups=CHIP_GROUPS)
    chip = jnp.arange(64, dtype=jnp.int32)
    far_x, far_y = (x - chip // 16) % 4, (y - (chip // 4) % 4) % 4
    turn_x, turn_y = turns[far_x], turns[far_y]
    target = jnp.where(c == 0, turn_x * 4 + turn_y, turn_y * 4 + turn_x) * 36 + (chip % 4) * 9
    first_rows = (target[:, None] + jnp.arange(8, dtype=jnp.int32)[None, :]).reshape(512)
    rows576 = jnp.arange(576, dtype=jnp.int32)[:, None]
    attn_half = kernel_call(
        unpack_kernel,
        (
            after(attn_all, cos_table, sin_table, *rows_near),
            one_hot(rows576, first_rows[None, :]),
            one_hot(rows576, (target + 8)[None, :]),
        ),
        ((576, QKV, BF),),
        scratch=((512, 128, F32),),
    )[0]
    ffn_half = after(pick(z_arrival, jnp.concatenate(ffn_all, axis=0)), attn_all)
    rows_both = after(rows_both, attn_all)
    rows_far = [send(rows_both, home(flip)) for flip in (2, 3)]

    attn_other = send(attn_half, other_core)
    inputs, normed_a, queries, kv_send, gains = project(
        *rows_near,
        attn_half,
        attn_other,
        cos_table,
        sin_table,
    )
    kv = after(exchange(kv_send, HX_GROUPS), ffn_half, *rows_far)
    ffn_half = after(ffn_half, kv)
    ffn_half = [ffn_half] + send_turn(ffn_half, True)
    heads_out, logs, kv_sorted, heads_send = attend(
        spot, rank, jnp.reshape(b, (1,)), queries, kv, send(kv, other_core)
    )
    heads_low = heads_out.astype(BF)
    ffn_half = [after(piece, heads_send) for piece in ffn_half]
    ffn_half = pick(inner_order, jnp.concatenate(ffn_half, axis=0))
    ffn_near = [ffn_half] + send_turn(ffn_half, False)
    heads_all = exchange(heads_send, Z_GROUPS)
    ffn_far = [send(ffn_near[0], other_core)]
    ffn_far += [send(after(piece, heads_all), other_core) for piece in ffn_near[1:]]

    (
        normed_grad,
        out_own,
        *out_terms,
        hidden_own,
        grad_own,
        grad_local,
        hidden,
        dgate,
        dup,
        normed_f,
        output_part,
        ffn_gain_terms,
    ) = feed_forward(
        z_own, *rows_near, *rows_far, heads_all, gains, *ffn_near, *ffn_far
    )
    normed_grad = exchange(normed_grad, Z_GROUPS)
    ffn_near, ffn_far = kernel_call(
        ffn_grad_kernel,
        (normed_f, grad_local, hidden, dgate, dup),
        ((576, 2304, BF), (576, 2304, BF)),
        micros=6,
        room=60,
    )
    grad_hidden_one, grad_branch = kernel_call(
        branch_kernel,
        (normed_grad, hidden_own, grad_own, gains),
        ((128, DIM, F32), (128, DIM, BF)),
    )
    grad_pair = send(grad_branch, z_pair)
    ffn_far = send(after(ffn_far, normed_grad), other_core)
    ffn_near, ffn_rest = merge_cores([ffn_near], [ffn_far])
    ffn_rest = send_back(ffn_rest)

    output_near, output_far = kernel_call(
        output_grad_kernel,
        (grad_branch, grad_pair, heads_low),
        ((576, HALF_Q, BF), (576, HALF_Q, BF)),
        scratch=((256, DIM, BF),),
    )
    output_far = send(output_far, other_core)
    dq, dkv, dkv_far = attend_back(
        spot, rank, queries, kv_sorted, heads_out, logs, after(grad_branch, ffn_near), grad_pair, output_part
    )
    out_terms = [after(terms, dq) for terms in out_terms]
    out_terms = [send(terms, to_z(step)) for step, terms in enumerate(out_terms, 1)]
    dkv = kernel_call(core_sum_kernel, (dkv, send(after(dkv_far, *ffn_rest), other_core)), ((2048, KV, BF),))[0]
    dkv = exchange(dkv, HX_GROUPS)
    block_out = kernel_call(out_kernel, (out_own, *out_terms), ((128, DIM, BF),))[0]
    block_out = unpick_columns(send(block_out, home(0)), order)
    attn_near, attn_far, grad_own, grad_pair = kernel_call(
        attn_grad_kernel,
        (after(dq, output_far, *out_terms), dkv, cos_table, sin_table, normed_a, attn_half, attn_other, inputs, gains, ffn_gain_terms),
        ((576, QKV, BF), (576, QKV, BF), (128, DIM, F32), (128, DIM, BF)),
        scratch=((256, QKV, BF), (DIM, QKV, BF)),
        room=60,
    )
    attn_far = send(attn_far, other_core)
    grad_pair = send(grad_pair, z_pair)
    attn_near, attn_rest = merge_cores([attn_near, output_near], [attn_far, output_far])
    attn_rest = send_back(attn_rest)
    grad_inputs = kernel_call(
        token_kernel,
        (grad_own, grad_pair, inputs, gains, grad_hidden_one),
        ((128, DIM, BF),),
    )[0]
    grad_inputs = unpick_columns(send(grad_inputs, home(0)), order)
    parts = scatter_rows((attn_near, *attn_rest, ffn_near, *ffn_rest), inner_order)

    pieces = kernel_call(split_kernel, (z_order, *parts), ((32, PIECES + 512, BF),))[0]
    pieces = exchange(pieces, Z_GROUPS)
    gain_grads, *weight_grads = kernel_call(
        finish_kernel,
        (pieces,),
        ((9, 128, F32), (9, DIM, F32), (9, KV, F32), (9, KV, F32), (9, DIM, F32)) + ((9, 3072, F32),) * 3,
    )

    return (
        block_out[None],
        grad_inputs[None],
        gain_grads[:, 64],
        *weight_grads[:4],
        gain_grads[:, 65],
        *weight_grads[4:],
    )


def unpick_columns(rows, order):
    return jnp.einsum("tk,dk->td", rows, order, preferred_element_type=F32).astype(BF)


def solution(mesh):
    weights = P(ALL, None)
    rows = P("dp", "ctx", None)
    return jax.shard_map(
        body,
        mesh=mesh,
        in_specs=(rows, rows, P(), P(ALL), weights, weights, weights, weights, P(ALL), weights, weights, weights),
        out_specs=(rows, rows, P(ALL), weights, weights, weights, weights, P(ALL), weights, weights, weights),
        check_vma=False,
    )
```

```python
import functools
import itertools

import jax
import jax.numpy as jnp
from jax import lax
from jax.experimental import pallas as pl
from jax.experimental.pallas import tpu as pltpu
from jax.sharding import PartitionSpec as P

ALL = ("dp", "ctx")
EPS = 1e-05
DIM = 1152
HEAD = 64
HALF_Q = 576
KV = 384
QKV = 1024
FF_PART = 768
FFN = 3456
PIECES = 3968
TILE = 256
WIDE_TILE = 512
BF = jnp.bfloat16
F32 = jnp.float32


def flat(l, c, h, x, z):
    return (2 * l + c) * 32 + (4 * h + x) * 4 + z


def moves(target):
    places = itertools.product(range(2), range(2), range(2), range(4), range(4))
    return [(flat(*place), flat(*target(*place))) for place in places]


def send(value, target):
    return lax.ppermute(value, ALL, moves(target))


def to_z(step):
    return lambda l, c, h, x, z: (l, c, h, x, (z + step) % 4)


def turn_by(step, first):
    def target(l, c, h, x, z):
        y = 2 * h + l
        if (c == 0) == first:
            y = (y + step) % 4
        else:
            x = (x + step) % 4
        return (y % 2, c, y // 2, x, z)

    return target


def other_core(l, c, h, x, z):
    return (l, 1 - c, h, x, z)


def z_pair(l, c, h, x, z):
    return (l, c, h, x, z ^ 1)


def home(flip):
    return lambda l, c, h, x, z: (l, z // 2, h, x, (2 * c + z % 2) ^ flip)


Z_GROUPS = [[ring * 4 + z for z in range(4)] for ring in range(8)]
CHIP_GROUPS = [
    [flat(y % 2, c, y // 2, x, z) for x in range(4) for y in range(4) for z in range(4)] for c in range(2)
]
HX_GROUPS = [[place * 4 + z for place in range(8)] for z in range(4)]


def exchange(parts, groups):
    return lax.all_to_all(parts, "ctx", 0, 0, tiled=True, axis_index_groups=groups)


def swap_halves(block):
    lane = lax.broadcasted_iota(jnp.int32, block.shape, 1) % HEAD
    return jnp.where(
        lane < HEAD // 2, pltpu.roll(block, 128 - HEAD // 2, 1), pltpu.roll(block, HEAD // 2, 1)
    )


def fill(ref, row, lane, value):
    ref[row : row + value.shape[0], lane : lane + value.shape[1]] = value


def pack_kernel(z_ref, *refs):
    arrived, sems = refs[13:21], refs[21]
    copies = [
        pltpu.make_async_copy(here, there, sems.at[index])
        for index, (here, there) in enumerate(zip(refs[:8], arrived))
    ]
    for copy in copies:
        copy.start()
    for copy in copies:
        copy.wait()
    gain_ref, q_ref, k_ref, v_ref, o_ref, gate_ref, up_ref, down_ref = arrived
    attn_ref, wide_ref = refs[8], refs[22]
    wide_ref[...] = jnp.zeros(wide_ref.shape, BF)
    for side in range(2):
        row = side * 16
        fill(wide_ref, row, 0, q_ref[:, side * 576 : side * 576 + 576])
        fill(wide_ref, row, 576, gain_ref[...])
        fill(wide_ref, row, 640, k_ref[:, side * 192 : side * 192 + 192])
        fill(wide_ref, row, 832, v_ref[:, side * 192 : side * 192 + 192])
    chunks = []
    for side in range(2):
        rows = wide_ref[side * 16 : side * 16 + 16, :].astype(F32)
        last = jnp.concatenate([rows[8:9, part * 128 : part * 128 + 128] for part in range(8)], axis=0)
        chunks.append(jnp.concatenate([rows[:8], last], axis=1))
    both = jnp.concatenate(chunks, axis=0).astype(BF)

    def copy_both(index, carry):
        attn_ref[pl.ds(pl.multiple_of(index * 16, 16), 16), :] = both
        return carry

    lax.fori_loop(0, 32, copy_both, 0)
    for step in range(4):
        ffn_ref = refs[9 + step]
        ffn_ref[...] = jnp.zeros((16, FFN), BF)
        start = pl.multiple_of(((z_ref[0] + step) % 4) * FF_PART, FF_PART)
        fill(ffn_ref, 0, 0, gate_ref[:, pl.ds(start, FF_PART)])
        fill(ffn_ref, 0, 768, up_ref[:, pl.ds(start, FF_PART)])
        fill(ffn_ref, 0, 1536, down_ref[:, pl.ds(start, FF_PART)])
        fill(ffn_ref, 0, 2304, o_ref[...])


def unpack_kernel(all_ref, order_ref, last_order_ref, out_ref, tail_ref):
    tail_ref[...] = all_ref[:, QKV:].astype(F32)
    last = jnp.concatenate([tail_ref[pl.ds(part, 64, stride=8), :] for part in range(8)], axis=1)
    out_ref[...] = (
        jnp.dot(order_ref[...], all_ref[:, :QKV], preferred_element_type=F32)
        + jnp.dot(last_order_ref[...], last.astype(BF), preferred_element_type=F32)
    ).astype(BF)


def qkv_kernel(
    own_ref, pair_ref, half_ref, other_ref, cos_ref, sin_ref,
    x_ref, normed_ref, q_ref, kv_ref, gain_ref, weight_ref,
):
    x_ref[0:128, :] = own_ref[:, 0:DIM]
    x_ref[128:256, :] = pair_ref[:, 0:DIM]
    weight_ref[0:576, :] = half_ref[...]
    weight_ref[576:1152, :] = other_ref[...]
    inputs = x_ref[...].astype(F32)
    lane = lax.broadcasted_iota(jnp.int32, (8, 128), 1)
    row = lax.broadcasted_iota(jnp.int32, (8, 128), 0)
    gains = lax.dot_general(
        (lane == row + 64).astype(BF), weight_ref[:, 512:640], NT, preferred_element_type=F32
    )
    gain_ref[...] = gains
    inverse = lax.rsqrt(jnp.mean(inputs * inputs, axis=-1, keepdims=True) + EPS)
    normed = (inputs * inverse * gains[0:1]).astype(BF)
    normed_ref[...] = normed
    proj = jnp.dot(normed, weight_ref[...], preferred_element_type=F32)
    cos_table, sin_table = cos_ref[...], sin_ref[...]
    kv_parts = []
    for start in range(0, QKV, 128):
        block = proj[:, start : start + 128]
        turned = block * cos_table + swap_halves(block) * sin_table
        if start < 512:
            q_ref[:, start : start + 128] = (turned * 0.125).astype(BF)
        elif start == 512:
            q_ref[:, 512:576] = (turned[:, :64] * 0.125).astype(BF)
        elif start == 640:
            kv_parts.append(turned.astype(BF))
        elif start == 768:
            side = lax.broadcasted_iota(jnp.int32, block.shape, 1)
            kv_parts.append(jnp.where(side < HEAD, turned, block).astype(BF))
        else:
            kv_parts.append(block.astype(BF))
    for copy in range(8):
        for part in range(3):
            fill(kv_ref, copy * 256, part * 128, kv_parts[part])


def stack_heads(block, kv_head, upper):
    parts = []
    for group in range(3):
        start = (kv_head * 3 + group) * HEAD
        parts.append(block[:, start : start + HEAD])
    rows = jnp.concatenate(parts, axis=0)
    zeros = jnp.zeros_like(rows)
    return jnp.concatenate([zeros, rows] if upper else [rows, zeros], axis=1)


K_GROUP = (0, 0, 128)
K_UPPER = (False, True, False)
V_GROUP = (128, 256, 256)
V_UPPER = (True, False, True)
NT = (((1,), (1,)), ((), ()))
TN = (((0,), (0,)), ((), ()))


def mask_rows(scores, place, tile):
    row = lax.broadcasted_iota(jnp.int32, scores.shape, 0) % 64 + place * 64
    key = lax.broadcasted_iota(jnp.int32, scores.shape, 1) + tile * scores.shape[1]
    return jnp.where(key <= row, scores, -1e30)


def over_tiles(rank_ref, step, carry, size):
    first = jnp.int32(0)
    for count in (4, 3, 2, 1):
        last = rank_ref[count - 1] // (size // 64)
        carry = lax.fori_loop(first, last, functools.partial(step, count=count, masked=False), carry)
        carry = lax.cond(
            first <= last,
            functools.partial(step, last, count=count, masked=True),
            lambda value: value,
            carry,
        )
        first = last + 1
    return carry


def stack_blocks(rank_ref, ref, target_ref, uppers):
    for rank in range(4):
        rows = ref[pl.ds(pl.multiple_of(rank_ref[4 + rank] * 64, 64), 64), :]
        for head in range(3):
            target_ref[head, rank * 192 : rank * 192 + 192, :] = stack_heads(rows, head, uppers[head])


def attend_kernel(
    spot_ref, rank_ref, side_ref, q_ref, near_ref, far_ref,
    out_ref, log_ref, sorted_ref, low_ref, score_ref, stack_ref, top_ref, sum_ref, total_ref,
):
    def put(index, carry):
        here = pl.ds(pl.multiple_of(index * 64, 64), 64)
        sorted_ref[pl.ds(pl.multiple_of(spot_ref[index] * 64, 64), 64), :] = near_ref[here, :]
        sorted_ref[pl.ds(pl.multiple_of(spot_ref[index + 32] * 64, 64), 64), :] = far_ref[here, :]
        return carry

    lax.fori_loop(0, 32, put, 0, unroll=4)
    stack_blocks(rank_ref, q_ref, stack_ref, K_UPPER)
    top_ref[...] = jnp.full(top_ref.shape, -1e30, F32)

    def score(tile, base, count, masked):
        span = pl.ds(pl.multiple_of(tile * WIDE_TILE, WIDE_TILE), WIDE_TILE)
        for head in range(3):
            keys = sorted_ref[span, K_GROUP[head] : K_GROUP[head] + 128]
            for rank in range(count):
                rows = slice(rank * 192, rank * 192 + 192)
                scores = lax.dot_general(
                    stack_ref[head, rows, :], keys, NT, preferred_element_type=F32
                )
                if masked:
                    scores = mask_rows(scores, rank_ref[rank], tile)
                score_ref[head, base + rank] = scores
                best = top_ref[head, rows, :]
                for lane in range(0, WIDE_TILE, 128):
                    best = jnp.maximum(best, scores[:, lane : lane + 128])
                top_ref[head, rows, :] = best
        return base + count

    over_tiles(rank_ref, score, jnp.int32(0), WIDE_TILE)
    for head in range(3):
        top_ref[head] = jnp.broadcast_to(jnp.max(top_ref[head], axis=1, keepdims=True), (768, 128))
    sum_ref[...] = jnp.zeros(sum_ref.shape, F32)
    total_ref[...] = jnp.zeros(total_ref.shape, F32)

    def weigh(tile, base, count, masked):
        span = pl.ds(pl.multiple_of(tile * WIDE_TILE, WIDE_TILE), WIDE_TILE)
        for head in range(3):
            values = sorted_ref[span, V_GROUP[head] : V_GROUP[head] + 128]
            for rank in range(count):
                rows = slice(rank * 192, rank * 192 + 192)
                scores = score_ref[head, base + rank]
                top = top_ref[head, rows, :]
                parts = [jnp.exp(scores[:, lane : lane + 128] - top) for lane in range(0, WIDE_TILE, 128)]
                total_ref[head, rows, :] += sum(parts[1:], parts[0])
                weights = jnp.concatenate([part.astype(BF) for part in parts], axis=1)
                sum_ref[head, rows, :] += jnp.dot(weights, values, preferred_element_type=F32)
        return base + count

    over_tiles(rank_ref, weigh, jnp.int32(0), WIDE_TILE)
    for head in range(3):
        row_total = jnp.sum(total_ref[head], axis=1, keepdims=True)
        log_ref[head] = top_ref[head] + jnp.log(row_total)
        result = sum_ref[head] / row_total
        side = result[:, 64:] if V_UPPER[head] else result[:, :64]
        for rank in range(4):
            rows = pl.ds(pl.multiple_of(rank_ref[4 + rank] * 64, 64), 64)
            for group in range(3):
                start = (head * 3 + group) * HEAD
                row = rank * 192 + group * 64
                out_ref[rows, start : start + HEAD] = side[row : row + 64]
    side = side_ref[0]
    for block in range(2):
        low = out_ref[block * 128 : block * 128 + 128, :].astype(BF)
        for copy in range(4):
            start = pl.multiple_of(copy * 256 + (block ^ side) * 128, 128)
            low_ref[pl.ds(start, 128), 0:576] = low
            low_ref[pl.ds(start, 128), 576:640] = jnp.zeros((128, 64), BF)


def attend_back_kernel(
    spot_ref, rank_ref, q_ref, sorted_ref, out_ref, log_ref, own_ref, pair_ref, part_ref,
    dq_ref, near_ref, far_ref,
    total_ref, rows_ref, grad_ref, stack_ref, grads_ref, delta_ref, prob_ref, dscore_ref, dq_sum_ref,
):
    rows_ref[0:128, :] = own_ref[...]
    rows_ref[128:256, :] = pair_ref[...]
    grad_ref[...] = jnp.dot(rows_ref[...], part_ref[...], preferred_element_type=F32).astype(BF)
    total_ref[...] = jnp.zeros_like(total_ref)
    dq_sum_ref[...] = jnp.zeros_like(dq_sum_ref)
    stack_blocks(rank_ref, q_ref, stack_ref, K_UPPER)
    stack_blocks(rank_ref, grad_ref, grads_ref, V_UPPER)
    for rank in range(4):
        rows = pl.ds(pl.multiple_of(rank_ref[4 + rank] * 64, 64), 64)
        products = grad_ref[rows, :].astype(F32) * out_ref[rows, :]
        for head in range(3):
            delta_ref[head, rank * 192 : rank * 192 + 192, :] = jnp.broadcast_to(
                jnp.sum(stack_heads(products, head, False), axis=1, keepdims=True), (192, 128)
            )

    def step(tile, carry, count, masked):
        span = pl.ds(pl.multiple_of(tile * TILE, TILE), TILE)
        size = count * 192
        for head in range(3):
            k_lanes = slice(K_GROUP[head], K_GROUP[head] + 128)
            v_lanes = slice(V_GROUP[head], V_GROUP[head] + 128)
            keys, values = sorted_ref[span, k_lanes], sorted_ref[span, v_lanes]
            scores_all = lax.dot_general(stack_ref[head, :size, :], keys, NT, preferred_element_type=F32)
            grad_all = lax.dot_general(grads_ref[head, :size, :], values, NT, preferred_element_type=F32)
            for rank in range(count):
                rows = slice(rank * 192, rank * 192 + 192)
                scores = scores_all[rows]
                if masked:
                    scores = mask_rows(scores, rank_ref[rank], tile)
                logs, delta = log_ref[head, rows, :], delta_ref[head, rows, :]
                for lane in (0, 128):
                    lanes = slice(lane, lane + 128)
                    prob = jnp.exp(scores[:, lanes] - logs)
                    prob_ref[head, rows, lanes] = prob.astype(BF)
                    dscore_ref[head, rows, lanes] = (prob * (grad_all[rows, lanes] - delta)).astype(BF)
        for head in range(3):
            k_lanes = slice(K_GROUP[head], K_GROUP[head] + 128)
            v_lanes = slice(V_GROUP[head], V_GROUP[head] + 128)
            keys = sorted_ref[span, k_lanes]
            dq_sum_ref[head, :size, :] += jnp.dot(
                dscore_ref[head, :size, :], keys, preferred_element_type=F32
            )
            total_ref[span, v_lanes] += lax.dot_general(
                prob_ref[head, :size, :], grads_ref[head, :size, :], TN, preferred_element_type=F32
            )
            total_ref[span, k_lanes] += lax.dot_general(
                dscore_ref[head, :size, :], stack_ref[head, :size, :], TN, preferred_element_type=F32
            )
        return carry

    over_tiles(rank_ref, step, jnp.int32(0), TILE)
    for head in range(3):
        for rank in range(4):
            rows = pl.ds(pl.multiple_of(rank_ref[4 + rank] * 64, 64), 64)
            for group in range(3):
                start = (head * 3 + group) * HEAD
                row = rank * 192 + group * 64
                block = dq_sum_ref[head, row : row + 64, :] * 0.125
                side = block[:, 64:] if K_UPPER[head] else block[:, :64]
                dq_ref[rows, start : start + HEAD] = side

    def put(index, carry):
        there = pl.ds(pl.multiple_of(index * 64, 64), 64)
        origin = pl.ds(pl.multiple_of(spot_ref[index] * 64, 64), 64)
        near_ref[there, :] = total_ref[origin, :].astype(BF)
        origin = pl.ds(pl.multiple_of(spot_ref[index + 32] * 64, 64), 64)
        far_ref[there, :] = total_ref[origin, :].astype(BF)
        return carry

    lax.fori_loop(0, 32, put, 0, unroll=4)


def rows_kernel(x_ref, grad_ref, order_ref, out_ref):
    for side, rows_ref in enumerate((x_ref, grad_ref)):
        out_ref[:, side * DIM : side * DIM + DIM] = jnp.dot(
            rows_ref[...], order_ref[...], preferred_element_type=F32
        ).astype(BF)


def ffn_kernel(
    z_ref, rows0_ref, rows1_ref, rows2_ref, rows3_ref, heads_ref, gain_ref,
    w0_ref, w1_ref, w2_ref, w3_ref, w4_ref, w5_ref, w6_ref, w7_ref,
    dn_ref, out0_ref, out1_ref, out2_ref, out3_ref, own_ref, grad_own_ref,
    grad_out, hidden_out, dgate_out, dup_out, normed_out, part_ref, gain_grad_ref,
    grad_ref, hidden_ref, dgate_ref, dup_ref, normed_ref, w_ref, scaled_ref, heads_all_ref, h1_ref, dn_sum_ref, out_sum_ref, gate_ref, up_ref, dh_ref, sems,
):
    pieces = (w0_ref, w1_ref, w2_ref, w3_ref, w4_ref, w5_ref, w6_ref, w7_ref)
    copies = [
        pltpu.make_async_copy(
            piece.at[:, pl.ds(lane, width)],
            w_ref.at[pl.ds(index * 144, 144), pl.ds(lane, width)],
            sems.at[8 * turn + index],
        )
        for turn, (lane, width) in enumerate(((2304, 1152), (0, 2304)))
        for index, piece in enumerate(pieces)
    ]
    for copy in copies:
        copy.start()
    z = z_ref[0]
    for slot, rows_ref in enumerate((rows0_ref, rows1_ref, rows2_ref, rows3_ref)):
        here = pl.ds(pl.multiple_of((z ^ slot) * 128, 128), 128)
        h1_ref[here, :] = rows_ref[:, 0:DIM].astype(F32)
        grad_ref[here, :] = rows_ref[:, DIM:]
    for side in range(2):
        for half in range(2):
            start = (2 * side + half) * 256
            heads_all_ref[side * 256 : side * 256 + 256, half * 576 : half * 576 + 576] = heads_ref[
                start : start + 256, 0:576
            ]
    for copy in copies[:8]:
        copy.wait()
    heads = heads_all_ref[...]
    h1_ref[...] += lax.dot_general(heads, w_ref[:, 2304:3456], NT, preferred_element_type=F32)

    def norm(index, carry):
        here = pl.ds(pl.multiple_of(index * 64, 64), 64)
        rows = h1_ref[here, :]
        inverse = lax.rsqrt(jnp.mean(rows * rows, axis=-1, keepdims=True) + EPS)
        scaled = rows * inverse
        scaled_ref[here, :] = scaled.astype(BF)
        normed_ref[here, :] = (scaled * gain_ref[1:2, :]).astype(BF)
        return carry

    lax.fori_loop(0, 8, norm, 0)
    here = pl.ds(pl.multiple_of(z * 128, 128), 128)
    own_ref[...] = h1_ref[here, :]
    grad_own_ref[...] = grad_ref[here, :]
    for copy in copies[8:]:
        copy.wait()
    outs = [
        pltpu.make_async_copy(here_ref, there_ref, sems.at[16 + index])
        for index, (here_ref, there_ref) in enumerate(
            (
                (normed_ref, normed_out),
                (grad_ref, grad_out),
                (hidden_ref, hidden_out),
                (dgate_ref, dgate_out),
                (dup_ref, dup_out),
            )
        )
    ]
    outs[0].start()
    outs[1].start()
    normed, grads = normed_ref[...], grad_ref[...]
    for index in range(3):
        start = index * 256
        gate_ref[index] = jnp.dot(normed, w_ref[:, start : start + 256], preferred_element_type=F32)
        up_ref[index] = jnp.dot(normed, w_ref[:, start + 768 : start + 1024], preferred_element_type=F32)
        dh_ref[index] = jnp.dot(grads, w_ref[:, start + 1536 : start + 1792], preferred_element_type=F32)
        there = slice(start, start + 256)
        for block in range(8):
            rows = slice(block * 64, block * 64 + 64)
            gate, up, grad = gate_ref[index, rows, :], up_ref[index, rows, :], dh_ref[index, rows, :]
            sigmoid = jax.nn.sigmoid(gate)
            active = gate * sigmoid
            hidden_ref[rows, there] = (active * up).astype(BF)
            dgate_ref[rows, there] = (grad * up * sigmoid * (1.0 + gate * (1.0 - sigmoid))).astype(BF)
            dup_ref[rows, there] = (grad * active).astype(BF)
    for copy in outs[2:]:
        copy.start()
    hidden, dgate, dup = hidden_ref[...], dgate_ref[...], dup_ref[...]
    for first in range(0, DIM, 1152):
        rows = slice(first, first + 1152)
        dn_sum_ref[:, rows] = lax.dot_general(
            dgate, w_ref[rows, 0:768], NT, preferred_element_type=F32
        ) + lax.dot_general(dup, w_ref[rows, 768:1536], NT, preferred_element_type=F32)
        out_sum_ref[:, rows] = lax.dot_general(
            hidden, w_ref[rows, 1536:2304], NT, preferred_element_type=F32
        )

    def finish(index, total):
        here = pl.ds(pl.multiple_of(index * 64, 64), 64)
        grad = dn_sum_ref[here, :]
        dn_ref[here, :] = grad.astype(BF)
        terms = grad * scaled_ref[here, :].astype(F32)
        return total + jnp.sum(terms.reshape(8, 8, DIM), axis=0)

    gain_grad_ref[...] = lax.fori_loop(0, 8, finish, jnp.zeros((8, DIM), F32))

    out0_ref[...] = own_ref[...] + out_sum_ref[here, :]
    for step, out_ref in enumerate((out1_ref, out2_ref, out3_ref)):
        there = pl.ds(pl.multiple_of(((z + step + 1) % 4) * 128, 128), 128)
        out_ref[...] = out_sum_ref[there, :].astype(BF)

    @pl.when(z % 2 == 0)
    def _():
        part_ref[...] = w_ref[:, 2304:2880]

    @pl.when(z % 2 == 1)
    def _():
        part_ref[...] = w_ref[:, 2880:3456]

    for copy in outs:
        copy.wait()


def outer_products(lefts, rights, near_ref, far_ref, extra=None):
    for start in range(0, DIM, 128):
        lane = 0
        for left, right in zip(lefts, rights):
            block = lax.dot_general(
                left[:, start : start + 128], right[...], TN, preferred_element_type=F32
            )
            if extra is not None:
                block = extra(start, block)
            block = block.astype(near_ref.dtype)
            width = block.shape[1]
            lanes = slice(lane, lane + width)
            if start < 512:
                near_ref[start : start + 128, lanes] = block
            elif start == 512:
                near_ref[512:576, lanes] = block[:64]
                far_ref[0:64, lanes] = block[64:].astype(BF)
            else:
                far_ref[start - 576 : start - 448, lanes] = block.astype(BF)
            lane += width


def ffn_grad_kernel(normed_ref, grad_ref, hidden_ref, dgate_ref, dup_ref, near_ref, far_ref):
    outer_products(
        (normed_ref, normed_ref, grad_ref), (dgate_ref, dup_ref, hidden_ref), near_ref, far_ref
    )


def output_grad_kernel(own_ref, pair_ref, heads_ref, near_ref, far_ref, rows_ref):
    rows_ref[0:128, :] = own_ref[...]
    rows_ref[128:256, :] = pair_ref[...]
    outer_products((rows_ref,), (heads_ref,), near_ref, far_ref)


def merge_kernel(*refs):
    count = len(refs) // 2 - 2
    targets = refs[2 * count :]
    for index in range(4):
        lane = 0
        for near_ref, far_ref in zip(refs[:count], refs[count : 2 * count]):
            width = near_ref.shape[1]
            rows = slice(index * 144, index * 144 + 144)
            total = near_ref[rows, :].astype(F32) + far_ref[rows, :].astype(F32)
            targets[index][:, lane : lane + width] = total.astype(targets[index].dtype)
            lane += width


def spread_kernel(order_ref, *refs):
    targets = refs[-4:]
    first = 0
    for group in range(2):
        near_ref, *others = refs[4 * group : 4 * group + 4]
        count = near_ref.shape[1]
        for start in range(0, count, 512):
            lanes = slice(start, min(start + 512, count))
            total = near_ref[:, lanes]
            for other_ref in others:
                total = total + other_ref[:, lanes].astype(F32)
            parts = lax.dot_general(order_ref[...], total.astype(BF), TN, preferred_element_type=F32)
            there = slice(first + lanes.start, first + lanes.stop)
            for index in range(4):
                targets[index][:, there] = parts[index * 40 : index * 40 + 40].astype(BF)
        first += count
        if first % 128:
            for target in targets:
                target[:, first : first + 64] = jnp.zeros((40, 64), BF)
            first += 64


def split_kernel(order_ref, near_ref, a_ref, b_ref, c_ref, target):
    lasts = []
    for start in range(0, PIECES, 512):
        lanes = slice(start, min(start + 512, PIECES))
        total = near_ref[:, lanes].astype(F32) + a_ref[:, lanes].astype(F32)
        total = total + b_ref[:, lanes].astype(F32) + c_ref[:, lanes].astype(F32)
        parts = lax.dot_general(order_ref[...], total.astype(BF), TN, preferred_element_type=F32)
        rows = jnp.concatenate([parts[part * 16 : part * 16 + 8] for part in range(4)], axis=0)
        target[:, lanes] = rows.astype(BF)
        last = jnp.concatenate([parts[part * 16 + 8 : part * 16 + 9] for part in range(4)], axis=0)
        rest = 512 - last.shape[1]
        if rest:
            last = jnp.concatenate([last, jnp.zeros((4, rest), F32)], axis=1)
        lasts.append(last)
    tail = jnp.concatenate([last[part : part + 1] for part in range(4) for last in lasts], axis=0)
    target[:, PIECES:] = tail.astype(BF)


def core_sum_kernel(near_ref, far_ref, out_ref):
    out_ref[...] = (near_ref[...].astype(F32) + far_ref[...].astype(F32)).astype(BF)


def branch_kernel(terms_ref, own_ref, grad_ref, gain_ref, full_ref, low_ref):
    grad = terms_ref[0:128, :].astype(F32)
    for part in range(1, 4):
        grad = grad + terms_ref[part * 128 : part * 128 + 128, :].astype(F32)
    rows = own_ref[...]
    inverse = lax.rsqrt(jnp.mean(rows * rows, axis=-1, keepdims=True) + EPS)
    scaled = rows * inverse
    grad = grad * gain_ref[1:2, :]
    grad = inverse * (grad - scaled * jnp.mean(grad * scaled, axis=-1, keepdims=True))
    grad = grad + grad_ref[...].astype(F32)
    full_ref[...] = grad
    low_ref[...] = grad.astype(BF)


def out_kernel(own_ref, a_ref, b_ref, c_ref, out_ref):
    total = own_ref[...] + a_ref[...].astype(F32)
    out_ref[...] = (total + b_ref[...].astype(F32) + c_ref[...].astype(F32)).astype(BF)


def attn_grad_kernel(
    dq_ref, dkv_ref, cos_ref, sin_ref, normed_ref, half_ref, other_ref, x_ref, gain_ref, ffn_gain_ref,
    near_ref, far_ref, own_ref, pair_ref, grad_ref, weight_ref,
):
    weight_ref[0:576, :] = half_ref[...]
    weight_ref[576:1152, :] = other_ref[...]
    cos_table, sin_table = cos_ref[...], sin_ref[...]

    def turn(block):
        return block * cos_table - swap_halves(block) * sin_table

    def summed(start):
        total = dkv_ref[0:256, start : start + 128].astype(F32)
        for part in range(1, 8):
            total = total + dkv_ref[part * 256 : part * 256 + 256, start : start + 128].astype(F32)
        return total

    for start in range(0, 512, 128):
        grad_ref[:, start : start + 128] = turn(dq_ref[:, start : start + 128]).astype(BF)
    tail = dq_ref[:, 512:576]
    wide = jnp.concatenate([tail, jnp.zeros_like(tail)], axis=1)
    grad_ref[:, 512:640] = turn(wide).astype(BF)
    grad_ref[:, 640:768] = turn(summed(0)).astype(BF)
    block = summed(128)
    lane = lax.broadcasted_iota(jnp.int32, block.shape, 1)
    grad_ref[:, 768:896] = jnp.where(lane < HEAD, turn(block), block).astype(BF)
    grad_ref[:, 896:1024] = summed(256).astype(BF)
    grads = lax.dot_general(grad_ref[...], weight_ref[...], NT, preferred_element_type=F32)
    own_ref[...] = grads[:128]
    pair_ref[...] = grads[128:].astype(BF)
    rows = x_ref[...].astype(F32)
    inverse = lax.rsqrt(jnp.mean(rows * rows, axis=-1, keepdims=True) + EPS)
    attn_terms = jnp.sum(grads * (rows * inverse), axis=0, keepdims=True)
    ffn_terms = jnp.sum(ffn_gain_ref[...], axis=0, keepdims=True)
    parts = []
    for terms in (attn_terms, ffn_terms):
        high = terms.astype(BF)
        parts.append(high.astype(F32))
        parts.append(terms - high.astype(F32))
    row = lax.broadcasted_iota(jnp.int32, (16, DIM), 0)
    gains = jnp.zeros((16, DIM), F32)
    for index, part in enumerate(parts):
        gains = jnp.where(row == index, part, gains)
    gains = gains.astype(BF)
    place_row = lax.broadcasted_iota(jnp.int32, (16, 128), 0)
    place_lane = lax.broadcasted_iota(jnp.int32, (16, 128), 1)
    places = ((place_lane == 64 + place_row // 2) & (place_row < 4)).astype(BF)

    def extra(start, block):
        columns = lax.dot_general(
            gains[:, start : start + 128], places, TN, preferred_element_type=F32
        )
        return jnp.concatenate([block[:, :512], block[:, 512:640] + columns, block[:, 640:]], axis=1)

    outer_products((normed_ref,), (grad_ref,), near_ref, far_ref, extra)


def token_kernel(own_ref, pair_ref, x_ref, gain_ref, full_ref, out_ref):
    grad = own_ref[...] + pair_ref[...].astype(F32)
    rows = x_ref[0:128, :].astype(F32)
    inverse = lax.rsqrt(jnp.mean(rows * rows, axis=-1, keepdims=True) + EPS)
    scaled = rows * inverse
    grad = grad * gain_ref[0:1, :]
    grad = inverse * (grad - scaled * jnp.mean(grad * scaled, axis=-1, keepdims=True))
    out_ref[...] = (full_ref[...] + grad).astype(BF)


def finish_kernel(pieces_ref, gain_ref, q_ref, k_ref, v_ref, o_ref, gate_ref, up_ref, down_ref):
    wholes = []
    pieces = pieces_ref[...].astype(F32)
    for part in range(4):
        rows = pieces[part * 8 : part * 8 + 8]
        last = jnp.concatenate([rows[index : index + 1, PIECES:] for index in range(8)], axis=1)
        wholes.append(jnp.concatenate([rows[:, :PIECES], last[:, :PIECES]], axis=0))
    for side in range(2):
        total = wholes[side][:, :1600] + wholes[side + 2][:, :1600]
        q_ref[:, side * 576 : side * 576 + 576] = total[:, 0:576]
        k_ref[:, side * 192 : side * 192 + 192] = total[:, 640:832]
        v_ref[:, side * 192 : side * 192 + 192] = total[:, 832:1024]
        o_ref[:, side * 576 : side * 576 + 576] = total[:, 1024:1600]
        if side == 0:
            gain_ref[...] = total[:, 512:640]
        else:
            gain_ref[...] += total[:, 512:640]
    for part in range(4):
        lanes = slice(part * FF_PART, part * FF_PART + FF_PART)
        gate_ref[:, lanes] = wholes[part][:, 1664:2432]
        up_ref[:, lanes] = wholes[part][:, 2432:3200]
        down_ref[:, lanes] = wholes[part][:, 3200:3968]


VMEM = pl.BlockSpec(memory_space=pltpu.VMEM)
SMEM = pl.BlockSpec(memory_space=pltpu.SMEM)
HBM = pl.BlockSpec(memory_space=pltpu.HBM)


def takes(microseconds):
    return pl.CostEstimate(flops=int(microseconds * 6e8), bytes_accessed=1 << 20, transcendentals=0)


def shapes(*sizes):
    return tuple(jax.ShapeDtypeStruct(size[:-1], size[-1]) for size in sizes)


def kernel_call(kernel, ins, outs, scalars=0, scratch=(), micros=3, far=(), sems=0, far_outs=(), room=6, late=()):
    specs = [SMEM if index < scalars else HBM if index in far else VMEM for index in range(len(ins))]
    scratch_shapes = [pltpu.VMEM(size[:-1], size[-1]) for size in scratch]
    if sems:
        scratch_shapes.append(pltpu.SemaphoreType.DMA((sems,)))
    scratch_shapes += [pltpu.VMEM(size[:-1], size[-1]) for size in late]
    return pl.pallas_call(
        kernel,
        out_shape=shapes(*outs),
        in_specs=specs,
        out_specs=tuple(HBM if index in far_outs else VMEM for index in range(len(outs))),
        scratch_shapes=scratch_shapes,
        compiler_params=pltpu.CompilerParams(vmem_limit_bytes=room * 1024 * 1024),
        cost_estimate=takes(micros),
    )(*ins)


def pack(z, *weights):
    return kernel_call(
        pack_kernel,
        (z,) + weights,
        ((512, DIM, BF),) + ((16, FFN, BF),) * 4,
        scalars=1,
        scratch=[weight.shape + (BF,) for weight in weights],
        far=range(1, 9),
        sems=8,
        room=60,
        late=((32, QKV, BF),),
    )


def feed_forward(*ins):
    return kernel_call(
        ffn_kernel,
        ins,
        (
            (512, DIM, BF),
            (128, DIM, F32),
            (128, DIM, BF),
            (128, DIM, BF),
            (128, DIM, BF),
            (128, DIM, F32),
            (128, DIM, BF),
            (512, DIM, BF),
            (512, FF_PART, BF),
            (512, FF_PART, BF),
            (512, FF_PART, BF),
            (512, DIM, BF),
            (DIM, HALF_Q, BF),
            (8, DIM, F32),
        ),
        scalars=1,
        scratch=(
            (512, DIM, BF),
            (512, FF_PART, BF),
            (512, FF_PART, BF),
            (512, FF_PART, BF),
            (512, DIM, BF),
            (DIM, FFN, BF),
            (512, DIM, BF),
            (512, DIM, BF),
            (512, DIM, F32),
            (512, DIM, F32),
            (512, DIM, F32),
            (3, 512, 256, F32),
            (3, 512, 256, F32),
            (3, 512, 256, F32),
        ),
        far=range(7, 15),
        far_outs=range(7, 12),
        sems=21,
        micros=15,
        room=60,
    )


def project(*ins):
    return kernel_call(
        qkv_kernel,
        ins,
        (
            (256, DIM, BF),
            (256, DIM, BF),
            (256, HALF_Q, BF),
            (2048, KV, BF),
            (8, DIM, F32),
        ),
        scratch=((DIM, QKV, BF),),
        room=60,
    )


def attend(*ins):
    return kernel_call(
        attend_kernel,
        ins,
        ((256, HALF_Q, F32), (3, 768, 128, F32), (4096, KV, BF), (1024, 640, BF)),
        scalars=3,
        scratch=((3, 18, 192, WIDE_TILE, F32), (3, 768, 128, BF)) + ((3, 768, 128, F32),) * 3,
        micros=20,
        room=36,
    )


def attend_back(*ins):
    return kernel_call(
        attend_back_kernel,
        ins,
        ((256, HALF_Q, F32), (2048, KV, BF), (2048, KV, BF)),
        scalars=2,
        scratch=(
            (4096, KV, F32),
            (256, DIM, BF),
            (256, HALF_Q, BF),
            (3, 768, 128, BF),
            (3, 768, 128, BF),
            (3, 768, 128, F32),
            (3, 768, TILE, BF),
            (3, 768, TILE, BF),
            (3, 768, 128, F32),
        ),
        micros=40,
        room=20,
    )


def pick(matrix, value):
    return jnp.dot(matrix, value, preferred_element_type=F32).astype(BF)


def send_turn(block, first):
    return [send(block, turn_by(step, first)) for step in (1, 3, 2)]


def merge_cores(nears, fars):
    width = sum(near.shape[1] for near in nears)
    near, *rest = kernel_call(
        merge_kernel, tuple(nears) + tuple(fars), ((144, width, F32),) + ((144, width, BF),) * 3
    )
    return near, rest


def send_back(parts):
    return [send(part, turn_by(-step, False)) for part, step in zip(parts, (1, 3, 2))]


def scatter_rows(groups, inner_order):
    near, *rest = kernel_call(
        spread_kernel, (inner_order, *groups), ((40, PIECES, BF),) * 4
    )
    return [near] + [send(part, turn_by(-step, True)) for part, step in zip(rest, (1, 3, 2))]


def rope_tables(positions):
    lane = jnp.arange(128, dtype=jnp.int32)
    inverse = 1.0 / 10000.0 ** ((lane % 32).astype(F32) * (2.0 / HEAD))
    angles = positions.astype(F32)[:, None] * inverse[None, :]
    sign = jnp.where(lane % HEAD < HEAD // 2, -1.0, 1.0)
    return (jnp.cos(angles), jnp.sin(angles) * sign[None, :])


def after(value, *others):
    return lax.optimization_barrier((value,) + others)[0]


def one_hot(rows, columns):
    return (rows == columns).astype(BF)


def body(
    tokens,
    grad_out,
    pair_order,
    attn_gain,
    query_weight,
    key_weight,
    value_weight,
    output_weight,
    ffn_gain,
    gate_weight,
    up_weight,
    down_weight,
):
    dp, ctx = lax.axis_index("dp"), lax.axis_index("ctx")
    l, c = dp // 2, dp % 2
    h, x, z = ctx // 16, (ctx // 4) % 4, ctx % 4
    y, b = 2 * h + l, z % 2
    even = b == 0

    local = jnp.arange(DIM, dtype=jnp.int32)
    from_c = (local // 576) ^ (z // 2)
    turns = jnp.array([0, 1, 3, 2], jnp.int32)
    outer, inner = turns[(local // 144) % 4], turns[(local // 36) % 4]
    from_x = (x - jnp.where(from_c == 0, outer, inner)) % 4
    from_y = (y - jnp.where(from_c == 0, inner, outer)) % 4
    from_z = (local // 9) % 4
    owner = (2 * (from_y % 2) + from_c) * 32 + (4 * (from_y // 2) + from_x) * 4 + from_z
    natural = owner * 9 + local % 9
    order = one_hot(jnp.arange(DIM, dtype=jnp.int32)[:, None], natural[None, :])
    rows40 = jnp.arange(40, dtype=jnp.int32)
    z_order = one_hot(
        jnp.where(rows40 < 36, (rows40 // 9) * 16 + rows40 % 9, -1)[:, None],
        jnp.arange(64, dtype=jnp.int32)[None, :],
    )
    z_arrival = one_hot(
        jnp.where(rows40 < 36, ((z - rows40 // 9) % 4) * 16 + rows40 % 9, -1)[:, None],
        jnp.arange(64, dtype=jnp.int32)[None, :],
    )
    rows144 = jnp.arange(144, dtype=jnp.int32)
    inner_order = one_hot(
        ((rows144 // 36) * 40 + rows144 % 36)[:, None], jnp.arange(160, dtype=jnp.int32)[None, :]
    )
    chunk = jnp.arange(64, dtype=jnp.int32)
    chunk_ctx = (
        ((chunk // 4) % 8) * 4
        + 2 * ((chunk // 32) ^ c)
        + ((chunk // 2) % 2 ^ b)
    )
    ctx_match = chunk_ctx[:, None] == jnp.arange(32, dtype=jnp.int32)[None, :]
    chunk_pair = jnp.sum(jnp.where(ctx_match, pair_order[None, :], 0), axis=1)
    spot = jnp.where(chunk % 2 == 0, chunk_pair, 63 - chunk_pair)
    place = lax.dynamic_slice_in_dim(spot, (4 * h + x) * 4, 4)
    ahead = jnp.sum((place[None, :] > place[:, None]).astype(jnp.int32), axis=1)
    at_rank = ahead[None, :] == jnp.arange(4, dtype=jnp.int32)[:, None]
    rank = jnp.concatenate(
        [
            jnp.sum(jnp.where(at_rank, place[None, :], 0), axis=1),
            jnp.sum(jnp.where(at_rank, jnp.arange(4, dtype=jnp.int32)[None, :], 0), axis=1),
        ]
    )
    positions = (place[:, None] * 64 + jnp.arange(64, dtype=jnp.int32)[None, :]).reshape(256)
    cos_table, sin_table = rope_tables(positions)


    z_own = jnp.reshape(z, (1,))
    attn_send, *ffn_send = pack(
        z_own,
        jnp.stack([attn_gain, ffn_gain], axis=1),
        query_weight,
        key_weight,
        value_weight,
        output_weight,
        gate_weight,
        up_weight,
        down_weight,
    )
    rows_both = kernel_call(
        rows_kernel, (after(tokens[0], attn_send), grad_out[0], order), ((128, 2 * DIM, BF),)
    )[0]
    rows_near = [send(rows_both, home(flip)) for flip in (0, 1)]
    ffn_all = [ffn_send[0]] + [send(ffn_send[step], to_z(step)) for step in (1, 2, 3)]
    attn_all = lax.all_to_all(attn_send, ALL, 0, 0, tiled=True, axis_index_groups=CHIP_GROUPS)
    chip = jnp.arange(64, dtype=jnp.int32)
    far_x, far_y = (x - chip // 16) % 4, (y - (chip // 4) % 4) % 4
    turn_x, turn_y = turns[far_x], turns[far_y]
    target = jnp.where(c == 0, turn_x * 4 + turn_y, turn_y * 4 + turn_x) * 36 + (chip % 4) * 9
    first_rows = (target[:, None] + jnp.arange(8, dtype=jnp.int32)[None, :]).reshape(512)
    rows576 = jnp.arange(576, dtype=jnp.int32)[:, None]
    attn_half = kernel_call(
        unpack_kernel,
        (
            after(attn_all, cos_table, sin_table, *rows_near),
            one_hot(rows576, first_rows[None, :]),
            one_hot(rows576, (target + 8)[None, :]),
        ),
        ((576, QKV, BF),),
        scratch=((512, 128, F32),),
    )[0]
    ffn_half = after(pick(z_arrival, jnp.concatenate(ffn_all, axis=0)), attn_all)
    rows_both = after(rows_both, attn_all)
    rows_far = [send(rows_both, home(flip)) for flip in (2, 3)]

    attn_other = send(attn_half, other_core)
    inputs, normed_a, queries, kv_send, gains = project(
        *rows_near,
        attn_half,
        attn_other,
        cos_table,
        sin_table,
    )
    kv = after(exchange(kv_send, HX_GROUPS), ffn_half, *rows_far)
    ffn_half = after(ffn_half, kv)
    ffn_half = [ffn_half] + send_turn(ffn_half, True)
    heads_out, logs, kv_sorted, heads_send = attend(
        spot, rank, jnp.reshape(b, (1,)), queries, kv, send(kv, other_core)
    )
    heads_low = heads_out.astype(BF)
    ffn_half = [after(piece, heads_send) for piece in ffn_half]
    ffn_half = pick(inner_order, jnp.concatenate(ffn_half, axis=0))
    ffn_near = [ffn_half] + send_turn(ffn_half, False)
    heads_all = exchange(heads_send, Z_GROUPS)
    ffn_far = [send(ffn_near[0], other_core)]
    ffn_far += [send(after(piece, heads_all), other_core) for piece in ffn_near[1:]]

    (
        normed_grad,
        out_own,
        *out_terms,
        hidden_own,
        grad_own,
        grad_local,
        hidden,
        dgate,
        dup,
        normed_f,
        output_part,
        ffn_gain_terms,
    ) = feed_forward(
        z_own, *rows_near, *rows_far, heads_all, gains, *ffn_near, *ffn_far
    )
    normed_grad = exchange(normed_grad, Z_GROUPS)
    ffn_near, ffn_far = kernel_call(
        ffn_grad_kernel,
        (normed_f, grad_local, hidden, dgate, dup),
        ((576, 2304, BF), (576, 2304, BF)),
        micros=6,
        room=60,
    )
    grad_hidden_one, grad_branch = kernel_call(
        branch_kernel,
        (normed_grad, hidden_own, grad_own, gains),
        ((128, DIM, F32), (128, DIM, BF)),
    )
    grad_pair = send(grad_branch, z_pair)
    ffn_far = send(after(ffn_far, normed_grad), other_core)
    ffn_near, ffn_rest = merge_cores([ffn_near], [ffn_far])
    ffn_rest = send_back(ffn_rest)

    output_near, output_far = kernel_call(
        output_grad_kernel,
        (grad_branch, grad_pair, heads_low),
        ((576, HALF_Q, BF), (576, HALF_Q, BF)),
        scratch=((256, DIM, BF),),
    )
    output_far = send(output_far, other_core)
    dq, dkv, dkv_far = attend_back(
        spot, rank, queries, kv_sorted, heads_out, logs, after(grad_branch, ffn_near), grad_pair, output_part
    )
    out_terms = [after(terms, dq) for terms in out_terms]
    out_terms = [send(terms, to_z(step)) for step, terms in enumerate(out_terms, 1)]
    dkv = kernel_call(core_sum_kernel, (dkv, send(after(dkv_far, *ffn_rest), other_core)), ((2048, KV, BF),))[0]
    dkv = exchange(dkv, HX_GROUPS)
    block_out = kernel_call(out_kernel, (out_own, *out_terms), ((128, DIM, BF),))[0]
    block_out = unpick_columns(send(block_out, home(0)), order)
    attn_near, attn_far, grad_own, grad_pair = kernel_call(
        attn_grad_kernel,
        (after(dq, output_far, *out_terms), dkv, cos_table, sin_table, normed_a, attn_half, attn_other, inputs, gains, ffn_gain_terms),
        ((576, QKV, BF), (576, QKV, BF), (128, DIM, F32), (128, DIM, BF)),
        scratch=((256, QKV, BF), (DIM, QKV, BF)),
        room=60,
    )
    attn_far = send(attn_far, other_core)
    grad_pair = send(grad_pair, z_pair)
    attn_near, attn_rest = merge_cores([attn_near, output_near], [attn_far, output_far])
    attn_rest = send_back(attn_rest)
    grad_inputs = kernel_call(
        token_kernel,
        (grad_own, grad_pair, inputs, gains, grad_hidden_one),
        ((128, DIM, BF),),
    )[0]
    grad_inputs = unpick_columns(send(grad_inputs, home(0)), order)
    parts = scatter_rows((attn_near, *attn_rest, ffn_near, *ffn_rest), inner_order)

    pieces = kernel_call(split_kernel, (z_order, *parts), ((32, PIECES + 512, BF),))[0]
    pieces = exchange(pieces, Z_GROUPS)
    gain_grads, *weight_grads = kernel_call(
        finish_kernel,
        (pieces,),
        ((9, 128, F32), (9, DIM, F32), (9, KV, F32), (9, KV, F32), (9, DIM, F32)) + ((9, 3072, F32),) * 3,
    )

    return (
        block_out[None],
        grad_inputs[None],
        gain_grads[:, 64],
        *weight_grads[:4],
        gain_grads[:, 65],
        *weight_grads[4:],
    )


def unpick_columns(rows, order):
    return jnp.einsum("tk,dk->td", rows, order, preferred_element_type=F32).astype(BF)


def solution(mesh):
    weights = P(ALL, None)
    rows = P("dp", "ctx", None)
    return jax.shard_map(
        body,
        mesh=mesh,
        in_specs=(rows, rows, P(), P(ALL), weights, weights, weights, weights, P(ALL), weights, weights, weights),
        out_specs=(rows, rows, P(ALL), weights, weights, weights, weights, P(ALL), weights, weights, weights),
        check_vma=False,
    )
```

```python
import functools
import itertools

import jax
import jax.numpy as jnp
from jax import lax
from jax.experimental import pallas as pl
from jax.experimental.pallas import tpu as pltpu
from jax.sharding import PartitionSpec as P

ALL = ("dp", "ctx")
EPS = 1e-05
DIM = 1152
HEAD = 64
HALF_Q = 576
KV = 384
QKV = 1024
FF_PART = 768
FFN = 3456
PIECES = 3968
TILE = 256
WIDE_TILE = 512
BF = jnp.bfloat16
F32 = jnp.float32


def flat(l, c, h, x, z):
    return (2 * l + c) * 32 + (4 * h + x) * 4 + z


def moves(target):
    places = itertools.product(range(2), range(2), range(2), range(4), range(4))
    return [(flat(*place), flat(*target(*place))) for place in places]


def send(value, target):
    return lax.ppermute(value, ALL, moves(target))


def to_z(step):
    return lambda l, c, h, x, z: (l, c, h, x, (z + step) % 4)


def turn_by(step, first):
    def target(l, c, h, x, z):
        y = 2 * h + l
        if (c == 0) == first:
            y = (y + step) % 4
        else:
            x = (x + step) % 4
        return (y % 2, c, y // 2, x, z)

    return target


def other_core(l, c, h, x, z):
    return (l, 1 - c, h, x, z)


def z_pair(l, c, h, x, z):
    return (l, c, h, x, z ^ 1)


def home(flip):
    return lambda l, c, h, x, z: (l, z // 2, h, x, (2 * c + z % 2) ^ flip)


Z_GROUPS = [[ring * 4 + z for z in range(4)] for ring in range(8)]
CHIP_GROUPS = [
    [flat(y % 2, c, y // 2, x, z) for x in range(4) for y in range(4) for z in range(4)] for c in range(2)
]
HX_GROUPS = [[place * 4 + z for place in range(8)] for z in range(4)]


def exchange(parts, groups):
    return lax.all_to_all(parts, "ctx", 0, 0, tiled=True, axis_index_groups=groups)


def swap_halves(block):
    lane = lax.broadcasted_iota(jnp.int32, block.shape, 1) % HEAD
    return jnp.where(
        lane < HEAD // 2, pltpu.roll(block, 128 - HEAD // 2, 1), pltpu.roll(block, HEAD // 2, 1)
    )


def fill(ref, row, lane, value):
    ref[row : row + value.shape[0], lane : lane + value.shape[1]] = value


def pack_kernel(z_ref, *refs):
    arrived, sems = refs[13:21], refs[21]
    copies = [
        pltpu.make_async_copy(here, there, sems.at[index])
        for index, (here, there) in enumerate(zip(refs[:8], arrived))
    ]
    for copy in copies:
        copy.start()
    for copy in copies:
        copy.wait()
    gain_ref, q_ref, k_ref, v_ref, o_ref, gate_ref, up_ref, down_ref = arrived
    attn_ref, wide_ref = refs[8], refs[22]
    wide_ref[...] = jnp.zeros(wide_ref.shape, BF)
    across = lax.broadcasted_iota(jnp.int32, (9, 9), 1)
    down = lax.broadcasted_iota(jnp.int32, (9, 9), 0)
    gain_rows = gain_ref[...].astype(F32)
    gains = jnp.concatenate(
        [
            jnp.sum(jnp.where(across == down, gain_rows[side : side + 1], 0.0), axis=1, keepdims=True)
            for side in range(2)
        ],
        axis=1,
    ).astype(BF)
    for side in range(2):
        row = side * 16
        fill(wide_ref, row, 0, q_ref[:, side * 576 : side * 576 + 576])
        fill(wide_ref, row, 576, gains)
        fill(wide_ref, row, 640, k_ref[:, side * 192 : side * 192 + 192])
        fill(wide_ref, row, 832, v_ref[:, side * 192 : side * 192 + 192])
    chunks = []
    for side in range(2):
        rows = wide_ref[side * 16 : side * 16 + 16, :].astype(F32)
        last = jnp.concatenate([rows[8:9, part * 128 : part * 128 + 128] for part in range(8)], axis=0)
        chunks.append(jnp.concatenate([rows[:8], last], axis=1))
    both = jnp.concatenate(chunks, axis=0).astype(BF)

    def copy_both(index, carry):
        attn_ref[pl.ds(pl.multiple_of(index * 16, 16), 16), :] = both
        return carry

    lax.fori_loop(0, 32, copy_both, 0)
    for step in range(4):
        ffn_ref = refs[9 + step]
        ffn_ref[...] = jnp.zeros((16, FFN), BF)
        start = pl.multiple_of(((z_ref[0] + step) % 4) * FF_PART, FF_PART)
        fill(ffn_ref, 0, 0, gate_ref[:, pl.ds(start, FF_PART)])
        fill(ffn_ref, 0, 768, up_ref[:, pl.ds(start, FF_PART)])
        fill(ffn_ref, 0, 1536, down_ref[:, pl.ds(start, FF_PART)])
        fill(ffn_ref, 0, 2304, o_ref[...])


def unpack_kernel(all_ref, order_ref, last_order_ref, out_ref, tail_ref):
    tail_ref[...] = all_ref[:, QKV:].astype(F32)
    last = jnp.concatenate([tail_ref[pl.ds(part, 64, stride=8), :] for part in range(8)], axis=1)
    out_ref[...] = (
        jnp.dot(order_ref[...], all_ref[:, :QKV], preferred_element_type=F32)
        + jnp.dot(last_order_ref[...], last.astype(BF), preferred_element_type=F32)
    ).astype(BF)


def qkv_kernel(
    own_ref, pair_ref, half_ref, other_ref, cos_ref, sin_ref,
    x_ref, normed_ref, q_ref, kv_ref, gain_ref, weight_ref,
):
    x_ref[0:128, :] = own_ref[:, 0:DIM]
    x_ref[128:256, :] = pair_ref[:, 0:DIM]
    weight_ref[0:576, :] = half_ref[...]
    weight_ref[576:1152, :] = other_ref[...]
    inputs = x_ref[...].astype(F32)
    lane = lax.broadcasted_iota(jnp.int32, (8, 128), 1)
    row = lax.broadcasted_iota(jnp.int32, (8, 128), 0)
    gains = lax.dot_general(
        (lane == row + 64).astype(BF), weight_ref[:, 512:640], NT, preferred_element_type=F32
    )
    gain_ref[...] = gains
    inverse = lax.rsqrt(jnp.mean(inputs * inputs, axis=-1, keepdims=True) + EPS)
    normed = (inputs * inverse * gains[0:1]).astype(BF)
    normed_ref[...] = normed
    proj = jnp.dot(normed, weight_ref[...], preferred_element_type=F32)
    cos_table, sin_table = cos_ref[...], sin_ref[...]
    kv_parts = []
    for start in range(0, QKV, 128):
        block = proj[:, start : start + 128]
        turned = block * cos_table + swap_halves(block) * sin_table
        if start < 512:
            q_ref[:, start : start + 128] = (turned * 0.125).astype(BF)
        elif start == 512:
            q_ref[:, 512:576] = (turned[:, :64] * 0.125).astype(BF)
        elif start == 640:
            kv_parts.append(turned.astype(BF))
        elif start == 768:
            side = lax.broadcasted_iota(jnp.int32, block.shape, 1)
            kv_parts.append(jnp.where(side < HEAD, turned, block).astype(BF))
        else:
            kv_parts.append(block.astype(BF))
    for copy in range(8):
        for part in range(3):
            fill(kv_ref, copy * 256, part * 128, kv_parts[part])


def stack_heads(block, kv_head, upper):
    parts = []
    for group in range(3):
        start = (kv_head * 3 + group) * HEAD
        parts.append(block[:, start : start + HEAD])
    rows = jnp.concatenate(parts, axis=0)
    zeros = jnp.zeros_like(rows)
    return jnp.concatenate([zeros, rows] if upper else [rows, zeros], axis=1)


K_GROUP = (0, 0, 128)
K_UPPER = (False, True, False)
V_GROUP = (128, 256, 256)
V_UPPER = (True, False, True)
NT = (((1,), (1,)), ((), ()))
TN = (((0,), (0,)), ((), ()))


def mask_rows(scores, place, tile):
    row = lax.broadcasted_iota(jnp.int32, scores.shape, 0) % 64 + place * 64
    key = lax.broadcasted_iota(jnp.int32, scores.shape, 1) + tile * scores.shape[1]
    return jnp.where(key <= row, scores, -1e30)


def over_tiles(rank_ref, step, carry, size):
    first = jnp.int32(0)
    for count in (4, 3, 2, 1):
        last = rank_ref[count - 1] // (size // 64)
        carry = lax.fori_loop(first, last, functools.partial(step, count=count, masked=False), carry)
        carry = lax.cond(
            first <= last,
            functools.partial(step, last, count=count, masked=True),
            lambda value: value,
            carry,
        )
        first = last + 1
    return carry


def stack_blocks(rank_ref, ref, target_ref, uppers):
    for rank in range(4):
        rows = ref[pl.ds(pl.multiple_of(rank_ref[4 + rank] * 64, 64), 64), :]
        for head in range(3):
            target_ref[head, rank * 192 : rank * 192 + 192, :] = stack_heads(rows, head, uppers[head])


def attend_kernel(
    spot_ref, rank_ref, side_ref, q_ref, near_ref, far_ref,
    out_ref, log_ref, sorted_ref, low_ref, score_ref, stack_ref, top_ref, sum_ref, total_ref,
):
    def put(index, carry):
        here = pl.ds(pl.multiple_of(index * 64, 64), 64)
        sorted_ref[pl.ds(pl.multiple_of(spot_ref[index] * 64, 64), 64), :] = near_ref[here, :]
        sorted_ref[pl.ds(pl.multiple_of(spot_ref[index + 32] * 64, 64), 64), :] = far_ref[here, :]
        return carry

    lax.fori_loop(0, 32, put, 0, unroll=4)
    stack_blocks(rank_ref, q_ref, stack_ref, K_UPPER)
    top_ref[...] = jnp.full(top_ref.shape, -1e30, F32)

    def score(tile, base, count, masked):
        span = pl.ds(pl.multiple_of(tile * WIDE_TILE, WIDE_TILE), WIDE_TILE)
        for head in range(3):
            keys = sorted_ref[span, K_GROUP[head] : K_GROUP[head] + 128]
            for rank in range(count):
                rows = slice(rank * 192, rank * 192 + 192)
                scores = lax.dot_general(
                    stack_ref[head, rows, :], keys, NT, preferred_element_type=F32
                )
                if masked:
                    scores = mask_rows(scores, rank_ref[rank], tile)
                score_ref[head, base + rank] = scores
                best = top_ref[head, rows, :]
                for lane in range(0, WIDE_TILE, 128):
                    best = jnp.maximum(best, scores[:, lane : lane + 128])
                top_ref[head, rows, :] = best
        return base + count

    over_tiles(rank_ref, score, jnp.int32(0), WIDE_TILE)
    for head in range(3):
        top_ref[head] = jnp.broadcast_to(jnp.max(top_ref[head], axis=1, keepdims=True), (768, 128))
    sum_ref[...] = jnp.zeros(sum_ref.shape, F32)
    total_ref[...] = jnp.zeros(total_ref.shape, F32)

    def weigh(tile, base, count, masked):
        span = pl.ds(pl.multiple_of(tile * WIDE_TILE, WIDE_TILE), WIDE_TILE)
        for head in range(3):
            values = sorted_ref[span, V_GROUP[head] : V_GROUP[head] + 128]
            for rank in range(count):
                rows = slice(rank * 192, rank * 192 + 192)
                scores = score_ref[head, base + rank]
                top = top_ref[head, rows, :]
                parts = [jnp.exp(scores[:, lane : lane + 128] - top) for lane in range(0, WIDE_TILE, 128)]
                total_ref[head, rows, :] += sum(parts[1:], parts[0])
                weights = jnp.concatenate([part.astype(BF) for part in parts], axis=1)
                sum_ref[head, rows, :] += jnp.dot(weights, values, preferred_element_type=F32)
        return base + count

    over_tiles(rank_ref, weigh, jnp.int32(0), WIDE_TILE)
    for head in range(3):
        row_total = jnp.sum(total_ref[head], axis=1, keepdims=True)
        log_ref[head] = top_ref[head] + jnp.log(row_total)
        result = sum_ref[head] / row_total
        side = result[:, 64:] if V_UPPER[head] else result[:, :64]
        for rank in range(4):
            rows = pl.ds(pl.multiple_of(rank_ref[4 + rank] * 64, 64), 64)
            for group in range(3):
                start = (head * 3 + group) * HEAD
                row = rank * 192 + group * 64
                out_ref[rows, start : start + HEAD] = side[row : row + 64]
    side = side_ref[0]
    for block in range(2):
        low = out_ref[block * 128 : block * 128 + 128, :].astype(BF)
        for copy in range(4):
            start = pl.multiple_of(copy * 256 + (block ^ side) * 128, 128)
            low_ref[pl.ds(start, 128), 0:576] = low
            low_ref[pl.ds(start, 128), 576:640] = jnp.zeros((128, 64), BF)


def attend_back_kernel(
    spot_ref, rank_ref, q_ref, sorted_ref, out_ref, log_ref, own_ref, pair_ref, part_ref,
    dq_ref, near_ref, far_ref,
    total_ref, rows_ref, grad_ref, stack_ref, grads_ref, delta_ref, prob_ref, dscore_ref, dq_sum_ref,
):
    rows_ref[0:128, :] = own_ref[...]
    rows_ref[128:256, :] = pair_ref[...]
    grad_ref[...] = jnp.dot(rows_ref[...], part_ref[...], preferred_element_type=F32).astype(BF)
    total_ref[...] = jnp.zeros_like(total_ref)
    dq_sum_ref[...] = jnp.zeros_like(dq_sum_ref)
    stack_blocks(rank_ref, q_ref, stack_ref, K_UPPER)
    stack_blocks(rank_ref, grad_ref, grads_ref, V_UPPER)
    for rank in range(4):
        rows = pl.ds(pl.multiple_of(rank_ref[4 + rank] * 64, 64), 64)
        products = grad_ref[rows, :].astype(F32) * out_ref[rows, :]
        for head in range(3):
            delta_ref[head, rank * 192 : rank * 192 + 192, :] = jnp.broadcast_to(
                jnp.sum(stack_heads(products, head, False), axis=1, keepdims=True), (192, 128)
            )

    def step(tile, carry, count, masked):
        span = pl.ds(pl.multiple_of(tile * TILE, TILE), TILE)
        size = count * 192
        for head in range(3):
            k_lanes = slice(K_GROUP[head], K_GROUP[head] + 128)
            v_lanes = slice(V_GROUP[head], V_GROUP[head] + 128)
            keys, values = sorted_ref[span, k_lanes], sorted_ref[span, v_lanes]
            scores_all = lax.dot_general(stack_ref[head, :size, :], keys, NT, preferred_element_type=F32)
            grad_all = lax.dot_general(grads_ref[head, :size, :], values, NT, preferred_element_type=F32)
            for rank in range(count):
                rows = slice(rank * 192, rank * 192 + 192)
                scores = scores_all[rows]
                if masked:
                    scores = mask_rows(scores, rank_ref[rank], tile)
                logs, delta = log_ref[head, rows, :], delta_ref[head, rows, :]
                for lane in (0, 128):
                    lanes = slice(lane, lane + 128)
                    prob = jnp.exp(scores[:, lanes] - logs)
                    prob_ref[head, rows, lanes] = prob.astype(BF)
                    dscore_ref[head, rows, lanes] = (prob * (grad_all[rows, lanes] - delta)).astype(BF)
        for head in range(3):
            k_lanes = slice(K_GROUP[head], K_GROUP[head] + 128)
            v_lanes = slice(V_GROUP[head], V_GROUP[head] + 128)
            keys = sorted_ref[span, k_lanes]
            dq_sum_ref[head, :size, :] += jnp.dot(
                dscore_ref[head, :size, :], keys, preferred_element_type=F32
            )
            total_ref[span, v_lanes] += lax.dot_general(
                prob_ref[head, :size, :], grads_ref[head, :size, :], TN, preferred_element_type=F32
            )
            total_ref[span, k_lanes] += lax.dot_general(
                dscore_ref[head, :size, :], stack_ref[head, :size, :], TN, preferred_element_type=F32
            )
        return carry

    over_tiles(rank_ref, step, jnp.int32(0), TILE)
    for head in range(3):
        for rank in range(4):
            rows = pl.ds(pl.multiple_of(rank_ref[4 + rank] * 64, 64), 64)
            for group in range(3):
                start = (head * 3 + group) * HEAD
                row = rank * 192 + group * 64
                block = dq_sum_ref[head, row : row + 64, :] * 0.125
                side = block[:, 64:] if K_UPPER[head] else block[:, :64]
                dq_ref[rows, start : start + HEAD] = side

    def put(index, carry):
        there = pl.ds(pl.multiple_of(index * 64, 64), 64)
        origin = pl.ds(pl.multiple_of(spot_ref[index] * 64, 64), 64)
        near_ref[there, :] = total_ref[origin, :].astype(BF)
        origin = pl.ds(pl.multiple_of(spot_ref[index + 32] * 64, 64), 64)
        far_ref[there, :] = total_ref[origin, :].astype(BF)
        return carry

    lax.fori_loop(0, 32, put, 0, unroll=4)


def rows_kernel(x_ref, grad_ref, natural_ref, out_ref):
    order = (
        lax.broadcasted_iota(jnp.int32, (DIM, DIM), 0) == natural_ref[...]
    ).astype(F32).astype(BF)
    for side, rows_ref in enumerate((x_ref, grad_ref)):
        out_ref[:, side * DIM : side * DIM + DIM] = jnp.dot(
            rows_ref[...], order, preferred_element_type=F32
        ).astype(BF)


def ffn_kernel(
    z_ref, rows0_ref, rows1_ref, rows2_ref, rows3_ref, heads_ref, gain_ref,
    w0_ref, w1_ref, w2_ref, w3_ref, w4_ref, w5_ref, w6_ref, w7_ref,
    dn_ref, out0_ref, out1_ref, out2_ref, out3_ref, own_ref, grad_own_ref,
    grad_out, hidden_out, dgate_out, dup_out, normed_out, part_ref, gain_grad_ref,
    grad_ref, hidden_ref, dgate_ref, dup_ref, normed_ref, w_ref, scaled_ref, heads_all_ref, h1_ref, dn_sum_ref, out_sum_ref, gate_ref, up_ref, dh_ref, sems,
):
    pieces = (w0_ref, w1_ref, w2_ref, w3_ref, w4_ref, w5_ref, w6_ref, w7_ref)
    copies = [
        pltpu.make_async_copy(
            piece.at[:, pl.ds(lane, width)],
            w_ref.at[pl.ds(index * 144, 144), pl.ds(lane, width)],
            sems.at[8 * turn + index],
        )
        for turn, (lane, width) in enumerate(((2304, 1152), (0, 2304)))
        for index, piece in enumerate(pieces)
    ]
    for copy in copies:
        copy.start()
    z = z_ref[0]
    for slot, rows_ref in enumerate((rows0_ref, rows1_ref, rows2_ref, rows3_ref)):
        here = pl.ds(pl.multiple_of((z ^ slot) * 128, 128), 128)
        h1_ref[here, :] = rows_ref[:, 0:DIM].astype(F32)
        grad_ref[here, :] = rows_ref[:, DIM:]
    for side in range(2):
        for half in range(2):
            start = (2 * side + half) * 256
            heads_all_ref[side * 256 : side * 256 + 256, half * 576 : half * 576 + 576] = heads_ref[
                start : start + 256, 0:576
            ]
    for copy in copies[:8]:
        copy.wait()
    heads = heads_all_ref[...]
    h1_ref[...] += lax.dot_general(heads, w_ref[:, 2304:3456], NT, preferred_element_type=F32)

    def norm(index, carry):
        here = pl.ds(pl.multiple_of(index * 64, 64), 64)
        rows = h1_ref[here, :]
        inverse = lax.rsqrt(jnp.mean(rows * rows, axis=-1, keepdims=True) + EPS)
        scaled = rows * inverse
        scaled_ref[here, :] = scaled.astype(BF)
        normed_ref[here, :] = (scaled * gain_ref[1:2, :]).astype(BF)
        return carry

    lax.fori_loop(0, 8, norm, 0)
    here = pl.ds(pl.multiple_of(z * 128, 128), 128)
    own_ref[...] = h1_ref[here, :]
    grad_own_ref[...] = grad_ref[here, :]
    for copy in copies[8:]:
        copy.wait()
    outs = [
        pltpu.make_async_copy(here_ref, there_ref, sems.at[16 + index])
        for index, (here_ref, there_ref) in enumerate(
            (
                (normed_ref, normed_out),
                (grad_ref, grad_out),
                (hidden_ref, hidden_out),
                (dgate_ref, dgate_out),
                (dup_ref, dup_out),
            )
        )
    ]
    outs[0].start()
    outs[1].start()
    normed, grads = normed_ref[...], grad_ref[...]
    for index in range(3):
        start = index * 256
        gate_ref[index] = jnp.dot(normed, w_ref[:, start : start + 256], preferred_element_type=F32)
        up_ref[index] = jnp.dot(normed, w_ref[:, start + 768 : start + 1024], preferred_element_type=F32)
        dh_ref[index] = jnp.dot(grads, w_ref[:, start + 1536 : start + 1792], preferred_element_type=F32)
        there = slice(start, start + 256)
        for block in range(8):
            rows = slice(block * 64, block * 64 + 64)
            gate, up, grad = gate_ref[index, rows, :], up_ref[index, rows, :], dh_ref[index, rows, :]
            sigmoid = jax.nn.sigmoid(gate)
            active = gate * sigmoid
            hidden_ref[rows, there] = (active * up).astype(BF)
            dgate_ref[rows, there] = (grad * up * sigmoid * (1.0 + gate * (1.0 - sigmoid))).astype(BF)
            dup_ref[rows, there] = (grad * active).astype(BF)
    for copy in outs[2:]:
        copy.start()
    hidden, dgate, dup = hidden_ref[...], dgate_ref[...], dup_ref[...]
    for first in range(0, DIM, 1152):
        rows = slice(first, first + 1152)
        dn_sum_ref[:, rows] = lax.dot_general(
            dgate, w_ref[rows, 0:768], NT, preferred_element_type=F32
        ) + lax.dot_general(dup, w_ref[rows, 768:1536], NT, preferred_element_type=F32)
        out_sum_ref[:, rows] = lax.dot_general(
            hidden, w_ref[rows, 1536:2304], NT, preferred_element_type=F32
        )

    def finish(index, total):
        here = pl.ds(pl.multiple_of(index * 64, 64), 64)
        grad = dn_sum_ref[here, :]
        dn_ref[here, :] = grad.astype(BF)
        terms = grad * scaled_ref[here, :].astype(F32)
        return total + jnp.sum(terms.reshape(8, 8, DIM), axis=0)

    gain_grad_ref[...] = lax.fori_loop(0, 8, finish, jnp.zeros((8, DIM), F32))

    out0_ref[...] = own_ref[...] + out_sum_ref[here, :]
    for step, out_ref in enumerate((out1_ref, out2_ref, out3_ref)):
        there = pl.ds(pl.multiple_of(((z + step + 1) % 4) * 128, 128), 128)
        out_ref[...] = out_sum_ref[there, :].astype(BF)

    @pl.when(z % 2 == 0)
    def _():
        part_ref[...] = w_ref[:, 2304:2880]

    @pl.when(z % 2 == 1)
    def _():
        part_ref[...] = w_ref[:, 2880:3456]

    for copy in outs:
        copy.wait()


def outer_products(lefts, rights, near_ref, far_ref, extra=None):
    for start in range(0, DIM, 128):
        lane = 0
        for left, right in zip(lefts, rights):
            block = lax.dot_general(
                left[:, start : start + 128], right[...], TN, preferred_element_type=F32
            )
            if extra is not None:
                block = extra(start, block)
            block = block.astype(near_ref.dtype)
            width = block.shape[1]
            lanes = slice(lane, lane + width)
            if start < 512:
                near_ref[start : start + 128, lanes] = block
            elif start == 512:
                near_ref[512:576, lanes] = block[:64]
                far_ref[0:64, lanes] = block[64:].astype(BF)
            else:
                far_ref[start - 576 : start - 448, lanes] = block.astype(BF)
            lane += width


def ffn_grad_kernel(normed_ref, grad_ref, hidden_ref, dgate_ref, dup_ref, near_ref, far_ref):
    outer_products(
        (normed_ref, normed_ref, grad_ref), (dgate_ref, dup_ref, hidden_ref), near_ref, far_ref
    )


def output_grad_kernel(own_ref, pair_ref, heads_ref, near_ref, far_ref, rows_ref):
    rows_ref[0:128, :] = own_ref[...]
    rows_ref[128:256, :] = pair_ref[...]
    outer_products((rows_ref,), (heads_ref,), near_ref, far_ref)


def merge_kernel(*refs):
    count = len(refs) // 2 - 2
    targets = refs[2 * count :]
    for index in range(4):
        lane = 0
        for near_ref, far_ref in zip(refs[:count], refs[count : 2 * count]):
            width = near_ref.shape[1]
            rows = slice(index * 144, index * 144 + 144)
            total = near_ref[rows, :].astype(F32) + far_ref[rows, :].astype(F32)
            targets[index][:, lane : lane + width] = total.astype(targets[index].dtype)
            lane += width


def spread_kernel(order_ref, *refs):
    targets = refs[-4:]
    first = 0
    for group in range(2):
        near_ref, *others = refs[4 * group : 4 * group + 4]
        count = near_ref.shape[1]
        for start in range(0, count, 512):
            lanes = slice(start, min(start + 512, count))
            total = near_ref[:, lanes]
            for other_ref in others:
                total = total + other_ref[:, lanes].astype(F32)
            parts = lax.dot_general(order_ref[...], total.astype(BF), TN, preferred_element_type=F32)
            there = slice(first + lanes.start, first + lanes.stop)
            for index in range(4):
                targets[index][:, there] = parts[index * 40 : index * 40 + 40].astype(BF)
        first += count
        if first % 128:
            for target in targets:
                target[:, first : first + 64] = jnp.zeros((40, 64), BF)
            first += 64


def split_kernel(order_ref, near_ref, a_ref, b_ref, c_ref, target):
    lasts = []
    for start in range(0, PIECES, 512):
        lanes = slice(start, min(start + 512, PIECES))
        total = near_ref[:, lanes].astype(F32) + a_ref[:, lanes].astype(F32)
        total = total + b_ref[:, lanes].astype(F32) + c_ref[:, lanes].astype(F32)
        parts = lax.dot_general(order_ref[...], total.astype(BF), TN, preferred_element_type=F32)
        rows = jnp.concatenate([parts[part * 16 : part * 16 + 8] for part in range(4)], axis=0)
        target[:, lanes] = rows.astype(BF)
        last = jnp.concatenate([parts[part * 16 + 8 : part * 16 + 9] for part in range(4)], axis=0)
        rest = 512 - last.shape[1]
        if rest:
            last = jnp.concatenate([last, jnp.zeros((4, rest), F32)], axis=1)
        lasts.append(last)
    tail = jnp.concatenate([last[part : part + 1] for part in range(4) for last in lasts], axis=0)
    target[:, PIECES:] = tail.astype(BF)


def core_sum_kernel(near_ref, far_ref, out_ref):
    out_ref[...] = (near_ref[...].astype(F32) + far_ref[...].astype(F32)).astype(BF)


def branch_kernel(terms_ref, own_ref, grad_ref, gain_ref, full_ref, low_ref):
    grad = terms_ref[0:128, :].astype(F32)
    for part in range(1, 4):
        grad = grad + terms_ref[part * 128 : part * 128 + 128, :].astype(F32)
    rows = own_ref[...]
    inverse = lax.rsqrt(jnp.mean(rows * rows, axis=-1, keepdims=True) + EPS)
    scaled = rows * inverse
    grad = grad * gain_ref[1:2, :]
    grad = inverse * (grad - scaled * jnp.mean(grad * scaled, axis=-1, keepdims=True))
    grad = grad + grad_ref[...].astype(F32)
    full_ref[...] = grad
    low_ref[...] = grad.astype(BF)


def out_kernel(own_ref, a_ref, b_ref, c_ref, out_ref):
    total = own_ref[...] + a_ref[...].astype(F32)
    out_ref[...] = (total + b_ref[...].astype(F32) + c_ref[...].astype(F32)).astype(BF)


def attn_grad_kernel(
    dq_ref, dkv_ref, cos_ref, sin_ref, normed_ref, half_ref, other_ref, x_ref, gain_ref, ffn_gain_ref,
    near_ref, far_ref, own_ref, pair_ref, grad_ref, weight_ref,
):
    weight_ref[0:576, :] = half_ref[...]
    weight_ref[576:1152, :] = other_ref[...]
    cos_table, sin_table = cos_ref[...], sin_ref[...]

    def turn(block):
        return block * cos_table - swap_halves(block) * sin_table

    def summed(start):
        total = dkv_ref[0:256, start : start + 128].astype(F32)
        for part in range(1, 8):
            total = total + dkv_ref[part * 256 : part * 256 + 256, start : start + 128].astype(F32)
        return total

    for start in range(0, 512, 128):
        grad_ref[:, start : start + 128] = turn(dq_ref[:, start : start + 128]).astype(BF)
    tail = dq_ref[:, 512:576]
    wide = jnp.concatenate([tail, jnp.zeros_like(tail)], axis=1)
    grad_ref[:, 512:640] = turn(wide).astype(BF)
    grad_ref[:, 640:768] = turn(summed(0)).astype(BF)
    block = summed(128)
    lane = lax.broadcasted_iota(jnp.int32, block.shape, 1)
    grad_ref[:, 768:896] = jnp.where(lane < HEAD, turn(block), block).astype(BF)
    grad_ref[:, 896:1024] = summed(256).astype(BF)
    grads = lax.dot_general(grad_ref[...], weight_ref[...], NT, preferred_element_type=F32)
    own_ref[...] = grads[:128]
    pair_ref[...] = grads[128:].astype(BF)
    rows = x_ref[...].astype(F32)
    inverse = lax.rsqrt(jnp.mean(rows * rows, axis=-1, keepdims=True) + EPS)
    attn_terms = jnp.sum(grads * (rows * inverse), axis=0, keepdims=True)
    ffn_terms = jnp.sum(ffn_gain_ref[...], axis=0, keepdims=True)
    parts = []
    for terms in (attn_terms, ffn_terms):
        high = terms.astype(BF)
        parts.append(high.astype(F32))
        parts.append(terms - high.astype(F32))
    row = lax.broadcasted_iota(jnp.int32, (16, DIM), 0)
    gains = jnp.zeros((16, DIM), F32)
    for index, part in enumerate(parts):
        gains = jnp.where(row == index, part, gains)
    gains = gains.astype(BF)
    place_row = lax.broadcasted_iota(jnp.int32, (16, 128), 0)
    place_lane = lax.broadcasted_iota(jnp.int32, (16, 128), 1)
    places = ((place_lane == 64 + place_row // 2) & (place_row < 4)).astype(BF)

    def extra(start, block):
        columns = lax.dot_general(
            gains[:, start : start + 128], places, TN, preferred_element_type=F32
        )
        return jnp.concatenate([block[:, :512], block[:, 512:640] + columns, block[:, 640:]], axis=1)

    outer_products((normed_ref,), (grad_ref,), near_ref, far_ref, extra)


def token_kernel(own_ref, pair_ref, x_ref, gain_ref, full_ref, out_ref):
    grad = own_ref[...] + pair_ref[...].astype(F32)
    rows = x_ref[0:128, :].astype(F32)
    inverse = lax.rsqrt(jnp.mean(rows * rows, axis=-1, keepdims=True) + EPS)
    scaled = rows * inverse
    grad = grad * gain_ref[0:1, :]
    grad = inverse * (grad - scaled * jnp.mean(grad * scaled, axis=-1, keepdims=True))
    out_ref[...] = (full_ref[...] + grad).astype(BF)


def finish_kernel(pieces_ref, gain_ref, q_ref, k_ref, v_ref, o_ref, gate_ref, up_ref, down_ref):
    wholes = []
    pieces = pieces_ref[...].astype(F32)
    for part in range(4):
        rows = pieces[part * 8 : part * 8 + 8]
        last = jnp.concatenate([rows[index : index + 1, PIECES:] for index in range(8)], axis=1)
        wholes.append(jnp.concatenate([rows[:, :PIECES], last[:, :PIECES]], axis=0))
    for side in range(2):
        total = wholes[side][:, :1600] + wholes[side + 2][:, :1600]
        q_ref[:, side * 576 : side * 576 + 576] = total[:, 0:576]
        k_ref[:, side * 192 : side * 192 + 192] = total[:, 640:832]
        v_ref[:, side * 192 : side * 192 + 192] = total[:, 832:1024]
        o_ref[:, side * 576 : side * 576 + 576] = total[:, 1024:1600]
        if side == 0:
            gain_ref[...] = total[:, 512:640]
        else:
            gain_ref[...] += total[:, 512:640]
    for part in range(4):
        lanes = slice(part * FF_PART, part * FF_PART + FF_PART)
        gate_ref[:, lanes] = wholes[part][:, 1664:2432]
        up_ref[:, lanes] = wholes[part][:, 2432:3200]
        down_ref[:, lanes] = wholes[part][:, 3200:3968]


VMEM = pl.BlockSpec(memory_space=pltpu.VMEM)
SMEM = pl.BlockSpec(memory_space=pltpu.SMEM)
HBM = pl.BlockSpec(memory_space=pltpu.HBM)


def takes(microseconds):
    return pl.CostEstimate(flops=int(microseconds * 6e8), bytes_accessed=1 << 20, transcendentals=0)


def shapes(*sizes):
    return tuple(jax.ShapeDtypeStruct(size[:-1], size[-1]) for size in sizes)


def kernel_call(kernel, ins, outs, scalars=0, scratch=(), micros=3, far=(), sems=0, far_outs=(), room=6, late=()):
    specs = [SMEM if index < scalars else HBM if index in far else VMEM for index in range(len(ins))]
    scratch_shapes = [pltpu.VMEM(size[:-1], size[-1]) for size in scratch]
    if sems:
        scratch_shapes.append(pltpu.SemaphoreType.DMA((sems,)))
    scratch_shapes += [pltpu.VMEM(size[:-1], size[-1]) for size in late]
    return pl.pallas_call(
        kernel,
        out_shape=shapes(*outs),
        in_specs=specs,
        out_specs=tuple(HBM if index in far_outs else VMEM for index in range(len(outs))),
        scratch_shapes=scratch_shapes,
        compiler_params=pltpu.CompilerParams(vmem_limit_bytes=room * 1024 * 1024),
        cost_estimate=takes(micros),
    )(*ins)


def pack(z, *weights):
    return kernel_call(
        pack_kernel,
        (z,) + weights,
        ((512, DIM, BF),) + ((16, FFN, BF),) * 4,
        scalars=1,
        scratch=[weight.shape + (BF,) for weight in weights],
        far=range(1, 9),
        sems=8,
        room=60,
        late=((32, QKV, BF),),
    )


def feed_forward(*ins):
    return kernel_call(
        ffn_kernel,
        ins,
        (
            (512, DIM, BF),
            (128, DIM, F32),
            (128, DIM, BF),
            (128, DIM, BF),
            (128, DIM, BF),
            (128, DIM, F32),
            (128, DIM, BF),
            (512, DIM, BF),
            (512, FF_PART, BF),
            (512, FF_PART, BF),
            (512, FF_PART, BF),
            (512, DIM, BF),
            (DIM, HALF_Q, BF),
            (8, DIM, F32),
        ),
        scalars=1,
        scratch=(
            (512, DIM, BF),
            (512, FF_PART, BF),
            (512, FF_PART, BF),
            (512, FF_PART, BF),
            (512, DIM, BF),
            (DIM, FFN, BF),
            (512, DIM, BF),
            (512, DIM, BF),
            (512, DIM, F32),
            (512, DIM, F32),
            (512, DIM, F32),
            (3, 512, 256, F32),
            (3, 512, 256, F32),
            (3, 512, 256, F32),
        ),
        far=range(7, 15),
        far_outs=range(7, 12),
        sems=21,
        micros=15,
        room=60,
    )


def project(*ins):
    return kernel_call(
        qkv_kernel,
        ins,
        (
            (256, DIM, BF),
            (256, DIM, BF),
            (256, HALF_Q, BF),
            (2048, KV, BF),
            (8, DIM, F32),
        ),
        scratch=((DIM, QKV, BF),),
        room=60,
    )


def attend(*ins):
    return kernel_call(
        attend_kernel,
        ins,
        ((256, HALF_Q, F32), (3, 768, 128, F32), (4096, KV, BF), (1024, 640, BF)),
        scalars=3,
        scratch=((3, 18, 192, WIDE_TILE, F32), (3, 768, 128, BF)) + ((3, 768, 128, F32),) * 3,
        micros=20,
        room=36,
    )


def attend_back(*ins):
    return kernel_call(
        attend_back_kernel,
        ins,
        ((256, HALF_Q, F32), (2048, KV, BF), (2048, KV, BF)),
        scalars=2,
        scratch=(
            (4096, KV, F32),
            (256, DIM, BF),
            (256, HALF_Q, BF),
            (3, 768, 128, BF),
            (3, 768, 128, BF),
            (3, 768, 128, F32),
            (3, 768, TILE, BF),
            (3, 768, TILE, BF),
            (3, 768, 128, F32),
        ),
        micros=40,
        room=20,
    )


def pick(matrix, value):
    return jnp.dot(matrix, value, preferred_element_type=F32).astype(BF)


def send_turn(block, first):
    return [send(block, turn_by(step, first)) for step in (1, 3, 2)]


def merge_cores(nears, fars):
    width = sum(near.shape[1] for near in nears)
    near, *rest = kernel_call(
        merge_kernel, tuple(nears) + tuple(fars), ((144, width, F32),) + ((144, width, BF),) * 3
    )
    return near, rest


def send_back(parts):
    return [send(part, turn_by(-step, False)) for part, step in zip(parts, (1, 3, 2))]


def scatter_rows(groups, inner_order):
    near, *rest = kernel_call(
        spread_kernel, (inner_order, *groups), ((40, PIECES, BF),) * 4
    )
    return [near] + [send(part, turn_by(-step, True)) for part, step in zip(rest, (1, 3, 2))]


def rope_tables(positions):
    lane = jnp.arange(128, dtype=jnp.int32)
    inverse = 1.0 / 10000.0 ** ((lane % 32).astype(F32) * (2.0 / HEAD))
    angles = positions.astype(F32)[:, None] * inverse[None, :]
    sign = jnp.where(lane % HEAD < HEAD // 2, -1.0, 1.0)
    return (jnp.cos(angles), jnp.sin(angles) * sign[None, :])


def after(value, *others):
    return lax.optimization_barrier((value,) + others)[0]


def one_hot(rows, columns):
    return (rows == columns).astype(BF)


def body(
    tokens,
    grad_out,
    pair_order,
    attn_gain,
    query_weight,
    key_weight,
    value_weight,
    output_weight,
    ffn_gain,
    gate_weight,
    up_weight,
    down_weight,
):
    dp, ctx = lax.axis_index("dp"), lax.axis_index("ctx")
    l, c = dp // 2, dp % 2
    h, x, z = ctx // 16, (ctx // 4) % 4, ctx % 4
    y, b = 2 * h + l, z % 2
    even = b == 0

    local = jnp.arange(DIM, dtype=jnp.int32)
    from_c = (local // 576) ^ (z // 2)
    turns = jnp.array([0, 1, 3, 2], jnp.int32)
    outer, inner = turns[(local // 144) % 4], turns[(local // 36) % 4]
    from_x = (x - jnp.where(from_c == 0, outer, inner)) % 4
    from_y = (y - jnp.where(from_c == 0, inner, outer)) % 4
    from_z = (local // 9) % 4
    owner = (2 * (from_y % 2) + from_c) * 32 + (4 * (from_y // 2) + from_x) * 4 + from_z
    natural = owner * 9 + local % 9
    order = one_hot(jnp.arange(DIM, dtype=jnp.int32)[:, None], natural[None, :])
    rows40 = jnp.arange(40, dtype=jnp.int32)
    z_order = one_hot(
        jnp.where(rows40 < 36, (rows40 // 9) * 16 + rows40 % 9, -1)[:, None],
        jnp.arange(64, dtype=jnp.int32)[None, :],
    )
    z_arrival = one_hot(
        jnp.where(rows40 < 36, ((z - rows40 // 9) % 4) * 16 + rows40 % 9, -1)[:, None],
        jnp.arange(64, dtype=jnp.int32)[None, :],
    )
    rows144 = jnp.arange(144, dtype=jnp.int32)
    inner_order = one_hot(
        ((rows144 // 36) * 40 + rows144 % 36)[:, None], jnp.arange(160, dtype=jnp.int32)[None, :]
    )
    chunk = jnp.arange(64, dtype=jnp.int32)
    chunk_ctx = (
        ((chunk // 4) % 8) * 4
        + 2 * ((chunk // 32) ^ c)
        + ((chunk // 2) % 2 ^ b)
    )
    ctx_match = chunk_ctx[:, None] == jnp.arange(32, dtype=jnp.int32)[None, :]
    chunk_pair = jnp.sum(jnp.where(ctx_match, pair_order[None, :], 0), axis=1)
    spot = jnp.where(chunk % 2 == 0, chunk_pair, 63 - chunk_pair)
    place = lax.dynamic_slice_in_dim(spot, (4 * h + x) * 4, 4)
    ahead = jnp.sum((place[None, :] > place[:, None]).astype(jnp.int32), axis=1)
    at_rank = ahead[None, :] == jnp.arange(4, dtype=jnp.int32)[:, None]
    rank = jnp.concatenate(
        [
            jnp.sum(jnp.where(at_rank, place[None, :], 0), axis=1),
            jnp.sum(jnp.where(at_rank, jnp.arange(4, dtype=jnp.int32)[None, :], 0), axis=1),
        ]
    )
    positions = (place[:, None] * 64 + jnp.arange(64, dtype=jnp.int32)[None, :]).reshape(256)
    cos_table, sin_table = rope_tables(positions)


    z_own = jnp.reshape(z, (1,))
    attn_send, *ffn_send = pack(
        z_own,
        jnp.stack([attn_gain, ffn_gain]),
        query_weight,
        key_weight,
        value_weight,
        output_weight,
        gate_weight,
        up_weight,
        down_weight,
    )
    rows_both = kernel_call(
        rows_kernel, (after(tokens[0], attn_send), grad_out[0], natural[None, :]), ((128, 2 * DIM, BF),), room=16
    )[0]
    rows_near = [send(rows_both, home(flip)) for flip in (0, 1)]
    ffn_all = [ffn_send[0]] + [send(ffn_send[step], to_z(step)) for step in (1, 2, 3)]
    attn_all = lax.all_to_all(attn_send, ALL, 0, 0, tiled=True, axis_index_groups=CHIP_GROUPS)
    chip = jnp.arange(64, dtype=jnp.int32)
    far_x, far_y = (x - chip // 16) % 4, (y - (chip // 4) % 4) % 4
    turn_x, turn_y = turns[far_x], turns[far_y]
    target = jnp.where(c == 0, turn_x * 4 + turn_y, turn_y * 4 + turn_x) * 36 + (chip % 4) * 9
    first_rows = (target[:, None] + jnp.arange(8, dtype=jnp.int32)[None, :]).reshape(512)
    rows576 = jnp.arange(576, dtype=jnp.int32)[:, None]
    attn_half = kernel_call(
        unpack_kernel,
        (
            after(attn_all, cos_table, sin_table, *rows_near),
            one_hot(rows576, first_rows[None, :]),
            one_hot(rows576, (target + 8)[None, :]),
        ),
        ((576, QKV, BF),),
        scratch=((512, 128, F32),),
    )[0]
    ffn_half = after(pick(z_arrival, jnp.concatenate(ffn_all, axis=0)), attn_all)
    rows_both = after(rows_both, attn_all)
    rows_far = [send(rows_both, home(flip)) for flip in (2, 3)]

    attn_other = send(attn_half, other_core)
    inputs, normed_a, queries, kv_send, gains = project(
        *rows_near,
        attn_half,
        attn_other,
        cos_table,
        sin_table,
    )
    kv = after(exchange(kv_send, HX_GROUPS), ffn_half, *rows_far)
    ffn_half = after(ffn_half, kv)
    ffn_half = [ffn_half] + send_turn(ffn_half, True)
    heads_out, logs, kv_sorted, heads_send = attend(
        spot, rank, jnp.reshape(b, (1,)), queries, kv, send(kv, other_core)
    )
    heads_low = heads_out.astype(BF)
    ffn_half = [after(piece, heads_send) for piece in ffn_half]
    ffn_half = pick(inner_order, jnp.concatenate(ffn_half, axis=0))
    ffn_near = [ffn_half] + send_turn(ffn_half, False)
    heads_all = exchange(heads_send, Z_GROUPS)
    ffn_far = [send(ffn_near[0], other_core)]
    ffn_far += [send(after(piece, heads_all), other_core) for piece in ffn_near[1:]]

    (
        normed_grad,
        out_own,
        *out_terms,
        hidden_own,
        grad_own,
        grad_local,
        hidden,
        dgate,
        dup,
        normed_f,
        output_part,
        ffn_gain_terms,
    ) = feed_forward(
        z_own, *rows_near, *rows_far, heads_all, gains, *ffn_near, *ffn_far
    )
    normed_grad = exchange(normed_grad, Z_GROUPS)
    ffn_near, ffn_far = kernel_call(
        ffn_grad_kernel,
        (normed_f, grad_local, hidden, dgate, dup),
        ((576, 2304, BF), (576, 2304, BF)),
        micros=6,
        room=60,
    )
    grad_hidden_one, grad_branch = kernel_call(
        branch_kernel,
        (normed_grad, hidden_own, grad_own, gains),
        ((128, DIM, F32), (128, DIM, BF)),
    )
    grad_pair = send(grad_branch, z_pair)
    ffn_far = send(after(ffn_far, normed_grad), other_core)
    ffn_near, ffn_rest = merge_cores([ffn_near], [ffn_far])
    ffn_rest = send_back(ffn_rest)

    output_near, output_far = kernel_call(
        output_grad_kernel,
        (grad_branch, grad_pair, heads_low),
        ((576, HALF_Q, BF), (576, HALF_Q, BF)),
        scratch=((256, DIM, BF),),
    )
    output_far = send(output_far, other_core)
    dq, dkv, dkv_far = attend_back(
        spot, rank, queries, kv_sorted, heads_out, logs, after(grad_branch, ffn_near), grad_pair, output_part
    )
    out_terms = [after(terms, dq) for terms in out_terms]
    out_terms = [send(terms, to_z(step)) for step, terms in enumerate(out_terms, 1)]
    dkv = kernel_call(core_sum_kernel, (dkv, send(after(dkv_far, *ffn_rest), other_core)), ((2048, KV, BF),))[0]
    dkv = exchange(dkv, HX_GROUPS)
    block_out = kernel_call(out_kernel, (out_own, *out_terms), ((128, DIM, BF),))[0]
    block_out = unpick_columns(send(block_out, home(0)), order)
    attn_near, attn_far, grad_own, grad_pair = kernel_call(
        attn_grad_kernel,
        (after(dq, output_far, *out_terms), dkv, cos_table, sin_table, normed_a, attn_half, attn_other, inputs, gains, ffn_gain_terms),
        ((576, QKV, BF), (576, QKV, BF), (128, DIM, F32), (128, DIM, BF)),
        scratch=((256, QKV, BF), (DIM, QKV, BF)),
        room=60,
    )
    attn_far = send(attn_far, other_core)
    grad_pair = send(grad_pair, z_pair)
    attn_near, attn_rest = merge_cores([attn_near, output_near], [attn_far, output_far])
    attn_rest = send_back(attn_rest)
    grad_inputs = kernel_call(
        token_kernel,
        (grad_own, grad_pair, inputs, gains, grad_hidden_one),
        ((128, DIM, BF),),
    )[0]
    grad_inputs = unpick_columns(send(grad_inputs, home(0)), order)
    parts = scatter_rows((attn_near, *attn_rest, ffn_near, *ffn_rest), inner_order)

    pieces = kernel_call(split_kernel, (z_order, *parts), ((32, PIECES + 512, BF),))[0]
    pieces = exchange(pieces, Z_GROUPS)
    gain_grads, *weight_grads = kernel_call(
        finish_kernel,
        (pieces,),
        ((9, 128, F32), (9, DIM, F32), (9, KV, F32), (9, KV, F32), (9, DIM, F32)) + ((9, 3072, F32),) * 3,
    )

    return (
        block_out[None],
        grad_inputs[None],
        gain_grads[:, 64],
        *weight_grads[:4],
        gain_grads[:, 65],
        *weight_grads[4:],
    )


def unpick_columns(rows, order):
    return jnp.einsum("tk,dk->td", rows, order, preferred_element_type=F32).astype(BF)


def solution(mesh):
    weights = P(ALL, None)
    rows = P("dp", "ctx", None)
    return jax.shard_map(
        body,
        mesh=mesh,
        in_specs=(rows, rows, P(), P(ALL), weights, weights, weights, weights, P(ALL), weights, weights, weights),
        out_specs=(rows, rows, P(ALL), weights, weights, weights, weights, P(ALL), weights, weights, weights),
        check_vma=False,
    )
```
